32 devices in a mesh: row: 8 (over z, y), col: 4 (over x, core).
Axes of the slice: x: 2, y: 2, z: 4, core: 2. Of those that a mesh axis runs over, the one named last changes fastest.
Arguments:
- points: float32 [8192, 16], P(('row', 'col')), may hold values from -6 to 6
- inv_lengths: float32 [16], replicated, may hold values from 0.35 to 0.7
- signal_level: float32 [1], replicated, may hold values from 0.5 to 2
- noise_level: float32 [1], replicated, may hold values from 0.05 to 0.5
- right_sides: float32 [8192, 32], P(('row', 'col')), may hold values from -6 to 6
- block_counts: int32 [32], P(('row', 'col')), may hold values from 1 to 256, 6144 in all
Outputs:
- solution: float32 [8192, 32], P(('row', 'col'))
- residual: float32 [8192, 32], P(('row', 'col'))
The draws below stay inside these ranges and needn't reach their ends.
Inputs may be any that keep to these rules, and one draw needn't show every extreme that they name: `block_counts`: each block of 256 slots holds its valid points first; the slots after them are padding.
All inputs are finite; a program needn't handle non-finite values.
Results may differ from the reference program's by a relative error of at most 0.012.
The reference program's roundings to bfloat16 on the way count: a program that leaves them out, or rounds other values in their place, can miss the bound.
Values may be sent and summed in bfloat16 or wider, within the bound.
No kernel may reach another device: no remote copies, remote signals or barrier semaphores. Data moves between devices by JAX's collectives and lax.ppermute only.
A program may use at most 64 MiB of HBM per device.

```python
import math
import jax
import jax.numpy as jnp
import numpy as np
from jax import lax

FEAT = 16
PROBES = 32
BLOCK = 256
ITERS = 2
NBLK = 32
NPTS = 8192
VALID = 6144


def draw_points(key, part):
    perm_key = jax.random.fold_in(key, 11)
    center_key = jax.random.fold_in(key, 12)
    offset_key = jax.random.fold_in(key, 13)
    groups = NPTS // 8
    shuffled = jax.random.permutation(perm_key, NPTS)
    member = shuffled // 8
    centers = 2.0 * jax.random.normal(center_key, (groups, FEAT), jnp.float32)
    offsets = 0.47 * jax.random.normal(offset_key, (NPTS, FEAT), jnp.float32)
    return jnp.clip(centers[member] + offsets, -6.0, 6.0)


def level_of(stream_key, dims, shards, least, top_value):
    loudness, own = 1.0, jax.random.fold_in(stream_key, 6)
    for dim, blocks in shards:
        heights = jnp.exp(jax.random.uniform(jax.random.fold_in(own, dim), (blocks,), jnp.float32, least / len(shards), top_value / len(shards)))
        loudness = loudness * jnp.repeat(heights, dims[dim] // blocks).reshape([-1 if axis == dim else 1 for axis in range(len(dims))])
    return loudness


def split_up(number_of, total, bound, slope):
    weights = [(1 << 20) // math.isqrt(standing ** slope) + 1 for standing in range(2, number_of + 1)]
    surplus, counts = total - bound - (number_of - 1), [1] * (number_of - 1)
    while surplus > 0:
        free = [i for i in range(number_of - 1) if counts[i] < bound]
        pool, left = sum([weights[i] for i in free]), surplus
        for i in free:
            more = min(bound - counts[i], max(1, left * weights[i] // pool), surplus)
            counts[i] = counts[i] + more
            surplus = surplus - more
    return np.array([bound] + counts)


def ragged(stream_key, number_of, total, limit, lean):
    if number_of == 2:
        one = jax.random.randint(stream_key, (), max(1, total - limit), min(limit, total - 1) + 1)
        return jnp.stack([one, total - one])
    lengths = jnp.asarray(split_up(number_of, total, limit, lean), jnp.int32)
    twos = (number_of - 1) // 2
    source_of, receiver = lengths[1:1 + 2 * twos:2], lengths[2:2 + 2 * twos:2]
    margin = jnp.minimum(source_of - 1, limit - receiver)
    passed = jax.random.randint(jax.random.fold_in(stream_key, 1), (twos,), 0, 1 << 20) % (margin + 1)
    lengths = lengths.at[1:1 + 2 * twos:2].set(source_of - passed).at[2:2 + 2 * twos:2].set(receiver + passed)
    return lengths[jax.random.permutation(jax.random.fold_in(stream_key, 2), number_of)]


def noise(key, shape, deviation, most, split=(), held_as=jnp.bfloat16):
    entries = jax.random.normal(key, shape, jnp.float32) * deviation
    if len(split) > 0:
        entries = level_of(key, shape, split, -0.22, 0.18) * entries
    return jnp.clip(entries, min=-most, max=most).astype(held_as)


def setup_inputs(seed: int = 0) -> dict:
    arg_keys = jax.random.split(jax.random.key(seed), 7)
    return {
        "points": draw_points(jax.random.fold_in(arg_keys[6], 71), 0),
        "inv_lengths": jnp.clip(jnp.exp(jax.random.uniform(arg_keys[1], (FEAT,), jnp.float32, math.log(0.35), math.log(0.7))), 0.35, 0.7),
        "signal_level": jnp.clip(jnp.exp(jax.random.uniform(arg_keys[2], (1,), jnp.float32, math.log(0.5), math.log(2.0))), 0.5, 2.0),
        "noise_level": jnp.clip(jnp.exp(jax.random.uniform(arg_keys[3], (1,), jnp.float32, math.log(0.05), math.log(0.5))), 0.05, 0.5),
        "right_sides": noise(arg_keys[4], (NPTS, PROBES), 1.0, 6.0, ((0, 32),), jnp.float32),
        "block_counts": ragged(arg_keys[5], NBLK, VALID, BLOCK, 2).astype(jnp.int32),
    }


def kernel_rows(scaled_rows, square_rows, scaled_cols, square_cols, signal):
    inner_product = lax.dot_general(scaled_rows, scaled_cols, (((1,), (1,)), ((), ())), precision=lax.Precision.HIGHEST, preferred_element_type=jnp.float32)
    distance = square_rows[:, None] + square_cols[None, :] - 2.0 * inner_product
    return (signal * jnp.exp(-0.5 * distance)).astype(jnp.bfloat16)


def reference(points, inv_lengths, signal_level, noise_level, right_sides, block_counts):
    signal = signal_level[0]
    noise_var = noise_level[0]
    scaled = points * inv_lengths[None, :]
    squares = jnp.sum(scaled * scaled, axis=1)
    slots = jnp.arange(BLOCK, dtype=jnp.int32)
    valid_rows = (slots[None, :] < block_counts[:, None]).astype(jnp.float32).reshape(NPTS, 1)
    scaled_blocks = scaled.reshape(NBLK, BLOCK, FEAT)
    square_blocks = squares.reshape(NBLK, BLOCK)

    def apply(direction):
        dir_wide = direction.astype(jnp.float32)

        def one_block(pieces):
            scaled_piece, square_piece = pieces
            kernel_block = kernel_rows(scaled_piece, square_piece, scaled, squares, signal)
            return jnp.dot(kernel_block.astype(jnp.float32), dir_wide, preferred_element_type=jnp.float32)

        products = lax.map(one_block, (scaled_blocks, square_blocks)).reshape(NPTS, PROBES)
        return valid_rows * products + noise_var * dir_wide

    residual = valid_rows * right_sides
    solution = jnp.zeros_like(residual)
    direction = residual.astype(jnp.bfloat16)
    norm_now = jnp.sum(residual * residual, axis=0)
    for iteration in range(ITERS):
        applied = apply(direction)
        dir_float = direction.astype(jnp.float32)
        curvature = jnp.sum(dir_float * applied, axis=0)
        step_size = norm_now / curvature
        solution = solution + step_size * dir_float
        residual = residual - step_size * applied
        if iteration + 1 < ITERS:
            norm_next = jnp.sum(residual * residual, axis=0)
            direction = (residual + (norm_next / norm_now) * dir_float).astype(jnp.bfloat16)
            norm_now = norm_next
    return solution, residual
```

```python
import functools
import math

import jax
import jax.numpy as jnp
from jax import lax
from jax.experimental import pallas as pl
from jax.experimental.pallas import tpu as pltpu
from jax.sharding import PartitionSpec as P

AXES = ("row", "col")
LOG2E = 1.0 / math.log(2.0)
FAR = 64.0
KEEP_BYTES = 20 * 2**20
COPIES = 4
F32, BF16 = jnp.float32, jnp.bfloat16
VMEM = pl.BlockSpec(memory_space=pltpu.VMEM)


def swap(array, bit, count):
    return lax.ppermute(array, AXES, [(i, i ^ bit) for i in range(count)])


def three_parts(wide):
    high = wide.astype(BF16)
    rest = wide - high.astype(F32)
    middle = rest.astype(BF16)
    return high, middle, (rest - middle.astype(F32)).astype(BF16)


def features(scaled, level, left):
    high, middle, low = three_parts(scaled)
    half = -0.5 * jnp.sum(scaled * scaled, axis=0, keepdims=True)
    if not left:
        half = half + level
    halves = [part.astype(F32) for part in three_parts(half)]
    ones = [jnp.ones_like(half)] * 3
    tail = (halves + ones if left else ones + halves) + [jnp.zeros((10, half.shape[1]), F32)]
    parts = [high, high, middle, high, low, middle] if left else [high, middle, high, low, high, middle]
    return jnp.concatenate(parts + [jnp.concatenate(tail, axis=0).astype(BF16)], axis=0)


def feature_rows(feat):
    return 6 * feat + 16


def prepare_kernel(points_ref, inv_ref, right_ref, count_ref, sent_ref):
    feat, slots = points_ref.shape
    valid = lax.broadcasted_iota(jnp.int32, (1, slots), 1) < count_ref[0]
    scaled = points_ref[...] * inv_ref[...] * math.sqrt(LOG2E)
    sent_ref[0, :feat, :] = jnp.where(valid, scaled, FAR)
    sent_ref[0, feat:, :] = jnp.where(valid, right_ref[...], 0.0)


def fill_right(near_ref, signal_ref, right_ref, feat):
    blocks, slots = right_ref.shape[1] // near_ref.shape[2], near_ref.shape[2]
    for b in range(blocks):
        level = jnp.log(jnp.full((1, slots), signal_ref[0], F32)) * LOG2E
        right_ref[:, b * slots : (b + 1) * slots] = features(near_ref[b, :feat, :], level, False)


def entries(left, right):
    powers = lax.dot_general(left, right, (((0,), (0,)), ((), ())), preferred_element_type=F32)
    return jnp.exp2(powers).astype(BF16)


def apply_kernel(feat, group, keep, near_ref, far_ref, signal_ref, so_far_ref, *refs):
    if keep:
        kept_ref, out_ref, right_ref, left_ref, dirs_ref = refs
    else:
        out_ref, right_ref, left_ref, dirs_ref = refs
    slots = far_ref.shape[2]
    fill_right(near_ref, signal_ref, right_ref, feat)
    out_ref[...] = so_far_ref[...]

    def step(g, carry):
        for b in range(group):
            place = slice(b * slots, (b + 1) * slots)
            left_ref[:, place] = features(far_ref[g * group + b, :feat, :], None, True)
            dirs_ref[:, place] = far_ref[g * group + b, feat:, :].astype(BF16)
        block = entries(left_ref[...], right_ref[...])
        if keep:
            kept_ref[g] = block
        out_ref[...] += jnp.dot(dirs_ref[...], block, preferred_element_type=F32)
        return carry

    lax.fori_loop(0, far_ref.shape[0] // group, step, 0)


def apply_first(near, far, signal, so_far, copies, feat, group, keep):
    slots, probes = far.shape[2], far.shape[1] - feat
    wide, steps = group * slots, far.shape[0] // group
    outs = [jax.ShapeDtypeStruct((probes, copies * slots), F32)]
    if keep:
        outs = [pltpu.VMEM((steps, wide, copies * slots), BF16)] + outs
    done = pl.pallas_call(
        functools.partial(apply_kernel, feat, group, keep),
        out_shape=outs,
        in_specs=[VMEM, VMEM, pl.BlockSpec(memory_space=pltpu.SMEM), VMEM],
        out_specs=[VMEM] * len(outs),
        scratch_shapes=[
            pltpu.VMEM((feature_rows(feat), copies * slots), BF16),
            pltpu.VMEM((feature_rows(feat), wide), BF16),
            pltpu.VMEM((probes, wide), BF16),
        ],
        compiler_params=pltpu.CompilerParams(vmem_limit_bytes=(16 if keep else 40) * 2**20),
        cost_estimate=pl.CostEstimate(
            flops=2 * copies * slots * far.shape[0] * slots * 256, bytes_accessed=far.size * 4, transcendentals=0
        ),
    )(near, far, signal, so_far)
    return (done[0], done[1]) if keep else (None, done[0])


def image_kernel(feat, copies, near_ref, noise_ref, product_ref, image_ref):
    slots = near_ref.shape[2]
    for b in range(copies):
        direction = near_ref[b, feat:, :].astype(BF16).astype(F32)
        image_ref[b] = product_ref[:, b * slots : (b + 1) * slots] + noise_ref[0] * direction


def second_kernel(feat, group, keep, copies, signal_ref, noise_ref, *refs):
    points, images, refs = refs[:4], refs[4:8], refs[8:]
    if keep:
        kept, refs = refs[:4], refs[4:]
    (partial_ref, solution_ref, residual_ref, own_dir_ref, own_image_ref, norm_ref, product_ref, dirs_ref) = refs[:8]
    if not keep:
        right_ref, left_ref = refs[8:]
    slots, probes = images[0].shape[2], images[0].shape[1]
    pairs = list(zip(points, images))

    def over_blocks(visit, start):
        carry = start
        for x_ref, w_ref in pairs:
            carry = lax.fori_loop(0, x_ref.shape[0], functools.partial(visit, x_ref, w_ref), carry, unroll=True if x_ref.shape[0] <= 8 else 8)
        return carry

    def column(total):
        return jnp.sum(total, axis=1, keepdims=True)

    zero = jnp.zeros((probes, slots), F32)

    def sums(x_ref, w_ref, b, carry):
        norm, curve = carry
        right = x_ref[b, feat:, :]
        return norm + right * right, curve + right.astype(BF16).astype(F32) * w_ref[b]

    norm, curve = over_blocks(sums, (zero, zero))
    norm_now = column(norm)
    step_size = norm_now / column(curve)

    def next_sum(x_ref, w_ref, b, norm):
        residual = x_ref[b, feat:, :] - step_size * w_ref[b]
        return norm + residual * residual

    norm_next = column(over_blocks(next_sum, zero))
    ratio = norm_next / norm_now

    def direct(x_ref, w_ref, b):
        right = x_ref[b, feat:, :]
        first = right.astype(BF16).astype(F32)
        residual = right - step_size * w_ref[b]
        return residual, first, (residual + ratio * first).astype(BF16)

    product_ref[...] = jnp.zeros_like(product_ref)
    if not keep:
        fill_right(points[0], signal_ref, right_ref, feat)
    for piece, (x_ref, w_ref) in enumerate(pairs):

        def step(g, carry, piece=piece, x_ref=x_ref, w_ref=w_ref):
            for b in range(group):
                place = slice(b * slots, (b + 1) * slots)
                dirs_ref[:, place] = direct(x_ref, w_ref, g * group + b)[2]
                if not keep:
                    left_ref[:, place] = features(x_ref[g * group + b, :feat, :], None, True)
            block = kept[piece][g] if keep else entries(left_ref[...], right_ref[...])
            product_ref[...] += jnp.dot(dirs_ref[...], block, preferred_element_type=F32)
            return carry

        lax.fori_loop(0, x_ref.shape[0] // group, step, 0)

    total = zero
    for b in range(copies):
        residual, first, direction = direct(points[0], images[0], b)
        direction = direction.astype(F32)
        image = product_ref[:, b * slots : (b + 1) * slots] + noise_ref[0] * direction
        total = total + direction * image
        if b == 0:
            solution_ref[...] = step_size * first
            residual_ref[...] = residual
            own_dir_ref[...] = direction
            own_image_ref[...] = image
    partial_ref[...] = jnp.broadcast_to(column(total), partial_ref.shape)
    norm_ref[...] = jnp.broadcast_to(norm_next, norm_ref.shape)


def second(signal, noise, points, images, kept, copies, feat, group):
    keep = kept is not None
    slots, probes = images[0].shape[2], images[0].shape[1]
    own = jax.ShapeDtypeStruct((probes, slots), F32)
    small = jax.ShapeDtypeStruct((probes, 128), F32)
    wide = group * slots
    scratch = [pltpu.VMEM((probes, copies * slots), F32), pltpu.VMEM((probes, wide), BF16)]
    if not keep:
        scratch += [pltpu.VMEM((feature_rows(feat), copies * slots), BF16), pltpu.VMEM((feature_rows(feat), wide), BF16)]
    smem = pl.BlockSpec(memory_space=pltpu.SMEM)
    return pl.pallas_call(
        functools.partial(second_kernel, feat, group, keep, copies),
        out_shape=[small, own, own, own, own, small],
        in_specs=[smem, smem] + [VMEM] * (12 if keep else 8),
        out_specs=[VMEM] * 6,
        scratch_shapes=scratch,
        compiler_params=pltpu.CompilerParams(vmem_limit_bytes=(16 if keep else 48) * 2**20),
    )(signal, noise, *points, *images, *(kept or ()))


def finish_kernel(curve_ref, norm_ref, solution_ref, residual_ref, direction_ref, image_ref, out_ref, left_ref):
    step_size = norm_ref[:, :1] / curve_ref[:, :1]
    out_ref[...] = solution_ref[...] + step_size * direction_ref[...]
    left_ref[...] = residual_ref[...] - step_size * image_ref[...]


def spread(own, bits, count):
    held = own
    for bit in bits[:-2]:
        held = jnp.concatenate([held, swap(held, bit, count)], axis=0)
    across = swap(held, bits[-2], count)
    return held, swap(held, bits[-1], count), across, swap(across, bits[-1], count)


def body(count, points, inv_lengths, signal_level, noise_level, right_sides, block_counts):
    slots, feat = points.shape
    probes = right_sides.shape[1]
    copies = COPIES
    while copies > 1 and (copies * 4 > count or copies * count * slots * slots * 2 > KEEP_BYTES):
        copies //= 2
    keep = copies * count * slots * slots * 2 <= KEEP_BYTES
    group = math.gcd(count // 4, 8)
    bits = [1 << k for k in reversed(range(count.bit_length() - 1))]
    later = bits[copies.bit_length() - 1 :]
    smem = pl.BlockSpec(memory_space=pltpu.SMEM)
    own = pl.pallas_call(
        prepare_kernel,
        out_shape=jax.ShapeDtypeStruct((1, feat + probes, slots), F32),
        in_specs=[VMEM, VMEM, VMEM, smem],
        out_specs=VMEM,
    )(points.T, inv_lengths[:, None], right_sides.T, block_counts)
    pieces = spread(own, bits, count)
    near = pieces[0][:copies]
    kept = []
    product = jnp.zeros((probes, copies * slots), F32)
    for piece in pieces:
        block, product = apply_first(near, piece, signal_level, product, copies, feat, group, keep)
        kept.append(block)
    image = pl.pallas_call(
        functools.partial(image_kernel, feat, copies),
        out_shape=jax.ShapeDtypeStruct((copies, probes, slots), F32),
        in_specs=[VMEM, smem, VMEM],
        out_specs=VMEM,
    )(near, noise_level, product)
    images = spread(image, later, count)
    partial, solution, residual, direction, own_image, norm = second(
        signal_level, noise_level, pieces, images, kept if keep else None, copies, feat, group
    )
    for bit in reversed(later):
        partial = partial + swap(partial, bit, count)
    done = jax.ShapeDtypeStruct((probes, slots), F32)
    solution, residual = pl.pallas_call(
        finish_kernel,
        out_shape=[done, done],
        in_specs=[VMEM] * 6,
        out_specs=[VMEM] * 2,
    )(partial, norm, solution, residual, direction, own_image)
    return solution.T, residual.T


def solution(mesh):
    count = math.prod(mesh.shape[axis] for axis in AXES)
    rows = P(AXES, None)
    return jax.shard_map(
        functools.partial(body, count),
        mesh=mesh,
        in_specs=(rows, P(), P(), P(), rows, P(AXES)),
        out_specs=(rows, rows),
        check_vma=False,
    )
```

```python
import functools
import math

import jax
import jax.numpy as jnp
from jax import lax
from jax.experimental import pallas as pl
from jax.experimental.pallas import tpu as pltpu
from jax.sharding import PartitionSpec as P

AXES = ("row", "col")
LOG2E = 1.0 / math.log(2.0)
FAR = 64.0
KEEP_BYTES = 20 * 2**20
COPIES = 4
F32, BF16 = jnp.float32, jnp.bfloat16
VMEM = pl.BlockSpec(memory_space=pltpu.VMEM)
SMEM = pl.BlockSpec(memory_space=pltpu.SMEM)


def stay(array):
    return pltpu.with_memory_space_constraint(array, pltpu.VMEM)


def swap(array, bit, count):
    return lax.ppermute(array, AXES, [(i, i ^ bit) for i in range(count)])


def three_parts(wide):
    high = wide.astype(BF16)
    rest = wide - high.astype(F32)
    middle = rest.astype(BF16)
    return high, middle, (rest - middle.astype(F32)).astype(BF16)


def features(scaled, level, left):
    high, middle, low = three_parts(scaled)
    half = -0.5 * jnp.sum(scaled * scaled, axis=0, keepdims=True)
    if not left:
        half = half + level
    halves = [part.astype(F32) for part in three_parts(half)]
    ones = [jnp.ones_like(half)] * 3
    tail = (halves + ones if left else ones + halves) + [jnp.zeros((10, half.shape[1]), F32)]
    parts = [high, high, middle, high, low, middle] if left else [high, middle, high, low, high, middle]
    return jnp.concatenate(parts + [jnp.concatenate(tail, axis=0).astype(BF16)], axis=0)


def feature_rows(feat):
    return 6 * feat + 16


def prepare_kernel(points_ref, inv_ref, right_ref, count_ref, sent_ref):
    feat, slots = points_ref.shape
    valid = lax.broadcasted_iota(jnp.int32, (1, slots), 1) < count_ref[0]
    row = lax.broadcasted_iota(jnp.int32, (feat, slots), 0)
    inverse = jnp.zeros((feat, slots), F32)
    for f in range(feat):
        inverse = jnp.where(row == f, inv_ref[f], inverse)
    scaled = points_ref[...] * inverse * math.sqrt(LOG2E)
    sent_ref[0, :feat, :] = jnp.where(valid, scaled, FAR)
    sent_ref[0, feat:, :] = jnp.where(valid, right_ref[...], 0.0)


def fill_right(near_ref, signal_ref, right_ref, feat):
    blocks, slots = right_ref.shape[1] // near_ref.shape[2], near_ref.shape[2]
    for b in range(blocks):
        level = jnp.log(jnp.full((1, slots), signal_ref[0], F32)) * LOG2E
        right_ref[:, b * slots : (b + 1) * slots] = features(near_ref[b, :feat, :], level, False)


def entries(left, right):
    powers = lax.dot_general(left, right, (((0,), (0,)), ((), ())), preferred_element_type=F32)
    return jnp.exp2(powers).astype(BF16)


def apply_kernel(feat, group, keep, last, near_ref, far_ref, signal_ref, noise_ref, so_far_ref, *refs):
    if keep:
        kept_ref, out_ref, right_ref, left_ref, dirs_ref, sum_ref = refs
    else:
        out_ref, right_ref, left_ref, dirs_ref, sum_ref = refs
    slots = far_ref.shape[2]
    fill_right(near_ref, signal_ref, right_ref, feat)
    if so_far_ref is None:
        sum_ref[...] = jnp.zeros_like(sum_ref)
    else:
        sum_ref[...] = so_far_ref[...]

    def step(g, carry):
        for b in range(group):
            place = slice(b * slots, (b + 1) * slots)
            left_ref[:, place] = features(far_ref[g * group + b, :feat, :], None, True)
            dirs_ref[:, place] = far_ref[g * group + b, feat:, :].astype(BF16)
        block = entries(left_ref[...], right_ref[...])
        if keep:
            kept_ref[g] = block
        sum_ref[...] += jnp.dot(dirs_ref[...], block, preferred_element_type=F32)
        return carry

    lax.fori_loop(0, far_ref.shape[0] // group, step, 0)
    if not last:
        out_ref[...] = sum_ref[...]
        return
    for b in range(near_ref.shape[0]):
        direction = near_ref[b, feat:, :].astype(BF16).astype(F32)
        out_ref[b] = sum_ref[:, b * slots : (b + 1) * slots] + noise_ref[0] * direction


def apply_first(near, far, signal, noise, so_far, feat, group, keep, last):
    copies, slots, probes = near.shape[0], far.shape[2], far.shape[1] - feat
    wide, steps = group * slots, far.shape[0] // group
    outs = [pltpu.VMEM((copies, probes, slots) if last else (probes, copies * slots), F32)]
    if keep:
        outs = [pltpu.VMEM((steps, wide, copies * slots), BF16)] + outs
    kernel = functools.partial(apply_kernel, feat, group, keep, last)
    if so_far is None:
        kernel = functools.partial(lambda inner, *refs: inner(*refs[:4], None, *refs[4:]), kernel)
    done = pl.pallas_call(
        kernel,
        out_shape=outs,
        in_specs=[VMEM, VMEM, SMEM, SMEM] + ([] if so_far is None else [VMEM]),
        out_specs=[VMEM] * len(outs),
        scratch_shapes=[
            pltpu.VMEM((feature_rows(feat), copies * slots), BF16),
            pltpu.VMEM((feature_rows(feat), wide), BF16),
            pltpu.VMEM((probes, wide), BF16),
            pltpu.VMEM((probes, copies * slots), F32),
        ],
        compiler_params=pltpu.CompilerParams(vmem_limit_bytes=(16 if keep else 40) * 2**20),
        cost_estimate=pl.CostEstimate(
            flops=2 * copies * slots * far.shape[0] * slots * 256, bytes_accessed=far.size * 4, transcendentals=0
        ),
    )(*([stay(near), stay(far)] if keep else [near, far]), signal, noise, *([] if so_far is None else [stay(so_far)]))
    return (done[0], done[1]) if keep else (None, done[0])


def second_kernel(feat, group, keep, copies, signal_ref, noise_ref, *refs):
    points, images, refs = refs[:4], refs[4:8], refs[8:]
    if keep:
        kept, refs = refs[:4], refs[4:]
    (partial_ref, solution_ref, residual_ref, own_dir_ref, own_image_ref, norm_ref, product_ref, dirs_ref) = refs[:8]
    if not keep:
        right_ref, left_ref = refs[8:]
    slots, probes = images[0].shape[2], images[0].shape[1]
    pairs = list(zip(points, images))

    def over_blocks(visit, start):
        carry = start
        for x_ref, w_ref in pairs:
            carry = lax.fori_loop(0, x_ref.shape[0], functools.partial(visit, x_ref, w_ref), carry, unroll=True if x_ref.shape[0] <= 8 else 8)
        return carry

    def column(total):
        return jnp.sum(total, axis=1, keepdims=True)

    zero = jnp.zeros((probes, slots), F32)

    def sums(x_ref, w_ref, b, carry):
        norm, curve = carry
        right = x_ref[b, feat:, :]
        return norm + right * right, curve + right.astype(BF16).astype(F32) * w_ref[b]

    norm, curve = over_blocks(sums, (zero, zero))
    norm_now = column(norm)
    step_size = norm_now / column(curve)

    def next_sum(x_ref, w_ref, b, norm):
        residual = x_ref[b, feat:, :] - step_size * w_ref[b]
        return norm + residual * residual

    norm_next = column(over_blocks(next_sum, zero))
    ratio = norm_next / norm_now

    def direct(x_ref, w_ref, b):
        right = x_ref[b, feat:, :]
        first = right.astype(BF16).astype(F32)
        residual = right - step_size * w_ref[b]
        return residual, first, (residual + ratio * first).astype(BF16)

    product_ref[...] = jnp.zeros_like(product_ref)
    if not keep:
        fill_right(points[0], signal_ref, right_ref, feat)
    for piece, (x_ref, w_ref) in enumerate(pairs):

        def step(g, carry, piece=piece, x_ref=x_ref, w_ref=w_ref):
            for b in range(group):
                place = slice(b * slots, (b + 1) * slots)
                dirs_ref[:, place] = direct(x_ref, w_ref, g * group + b)[2]
                if not keep:
                    left_ref[:, place] = features(x_ref[g * group + b, :feat, :], None, True)
            block = kept[piece][g] if keep else entries(left_ref[...], right_ref[...])
            product_ref[...] += jnp.dot(dirs_ref[...], block, preferred_element_type=F32)
            return carry

        lax.fori_loop(0, x_ref.shape[0] // group, step, 0)

    total = zero
    for b in range(copies):
        residual, first, direction = direct(points[0], images[0], b)
        direction = direction.astype(F32)
        image = product_ref[:, b * slots : (b + 1) * slots] + noise_ref[0] * direction
        total = total + direction * image
        if b == 0:
            solution_ref[...] = step_size * first
            residual_ref[...] = residual
            own_dir_ref[...] = direction
            own_image_ref[...] = image
    partial_ref[...] = jnp.broadcast_to(column(total), partial_ref.shape)
    norm_ref[...] = jnp.broadcast_to(norm_next, norm_ref.shape)


def second(signal, noise, points, images, kept, copies, feat, group):
    keep = kept is not None
    slots, probes = images[0].shape[2], images[0].shape[1]
    own, small, wide = pltpu.VMEM((probes, slots), F32), pltpu.VMEM((probes, 128), F32), group * slots
    scratch = [pltpu.VMEM((probes, copies * slots), F32), pltpu.VMEM((probes, wide), BF16)]
    if keep:
        points, images, kept = ([stay(piece) for piece in pieces] for pieces in (points, images, kept))
    else:
        scratch += [pltpu.VMEM((feature_rows(feat), copies * slots), BF16), pltpu.VMEM((feature_rows(feat), wide), BF16)]
    return pl.pallas_call(
        functools.partial(second_kernel, feat, group, keep, copies),
        out_shape=[small, own, own, own, own, small],
        in_specs=[SMEM, SMEM] + [VMEM] * (12 if keep else 8),
        out_specs=[VMEM] * 6,
        scratch_shapes=scratch,
        compiler_params=pltpu.CompilerParams(vmem_limit_bytes=(16 if keep else 48) * 2**20),
    )(signal, noise, *points, *images, *(kept or ()))


def finish_kernel(curve_ref, norm_ref, solution_ref, residual_ref, direction_ref, image_ref, out_ref, left_ref):
    step_size = norm_ref[:, :1] / curve_ref[:, :1]
    out_ref[...] = solution_ref[...] + step_size * direction_ref[...]
    left_ref[...] = residual_ref[...] - step_size * image_ref[...]


def gather(held, bits, count):
    for bit in bits:
        held = jnp.concatenate([held, swap(held, bit, count)], axis=0)
    return held


def body(count, points, inv_lengths, signal_level, noise_level, right_sides, block_counts):
    slots, feat = points.shape
    probes = right_sides.shape[1]
    copies = COPIES
    while copies > 1 and (copies * 4 > count or copies * count * slots * slots * 2 > KEEP_BYTES):
        copies //= 2
    keep = copies * count * slots * slots * 2 <= KEEP_BYTES
    group = math.gcd(count // 4, 8)
    bits = [1 << k for k in reversed(range(count.bit_length() - 1))]
    later = bits[copies.bit_length() - 1 :]
    own = pl.pallas_call(
        prepare_kernel,
        out_shape=pltpu.VMEM((1, feat + probes, slots), F32),
        in_specs=[VMEM, SMEM, VMEM, SMEM],
        out_specs=VMEM,
    )(points.T, inv_lengths, right_sides.T, block_counts)
    first = functools.partial(apply_first, feat=feat, group=group, keep=keep)

    held = gather(own, bits[:-2], count)
    near = held[:copies]
    across, beside = swap(held, bits[-2], count), swap(held, bits[-1], count)
    kept_held, product = first(near, held, signal_level, noise_level, None, last=False)
    kept_beside, product = first(near, beside, signal_level, noise_level, product, last=False)
    across, product = lax.optimization_barrier((across, product))
    beyond = swap(across, bits[-1], count)
    kept_across, product = first(near, across, signal_level, noise_level, product, last=False)
    kept_beyond, image = first(near, beyond, signal_level, noise_level, product, last=True)
    pieces = [held, beside, across, beyond]
    kept = [kept_held, kept_beside, kept_across, kept_beyond]

    held = gather(image, later[:-2], count)
    across, beside = swap(held, bits[-2], count), swap(held, bits[-1], count)
    images = [held, beside, across, swap(across, bits[-1], count)]
    partial, solution, residual, direction, own_image, norm = second(
        signal_level, noise_level, pieces, images, kept if keep else None, copies, feat, group
    )
    for bit in reversed(later):
        partial = partial + swap(partial, bit, count)
    done = jax.ShapeDtypeStruct((probes, slots), F32)
    solution, residual = pl.pallas_call(
        finish_kernel,
        out_shape=[done, done],
        in_specs=[VMEM] * 6,
        out_specs=[VMEM] * 2,
    )(*[stay(array) for array in (partial, norm, solution, residual, direction, own_image)])
    return solution.T, residual.T


def solution(mesh):
    count = math.prod(mesh.shape[axis] for axis in AXES)
    rows = P(AXES, None)
    return jax.shard_map(
        functools.partial(body, count),
        mesh=mesh,
        in_specs=(rows, P(), P(), P(), rows, P(AXES)),
        out_specs=(rows, rows),
        check_vma=False,
    )
```

```python
import functools
import math

import jax
import jax.numpy as jnp
from jax import lax
from jax.experimental import pallas as pl
from jax.experimental.pallas import tpu as pltpu
from jax.sharding import PartitionSpec as P

AXES = ("row", "col")
LOG2E = 1.0 / math.log(2.0)
FAR = 64.0
KEEP_BYTES = 20 * 2**20
COPIES = 4
PIECES = 8
F32, BF16 = jnp.float32, jnp.bfloat16
VMEM = pl.BlockSpec(memory_space=pltpu.VMEM)
SMEM = pl.BlockSpec(memory_space=pltpu.SMEM)


def stay(array):
    return pltpu.with_memory_space_constraint(array, pltpu.VMEM)


def swap(array, bit, count):
    return lax.ppermute(array, AXES, [(i, i ^ bit) for i in range(count)])


def three_parts(wide):
    high = wide.astype(BF16)
    rest = wide - high.astype(F32)
    middle = rest.astype(BF16)
    return high, middle, (rest - middle.astype(F32)).astype(BF16)


def features(scaled, level, left):
    high, middle, low = three_parts(scaled)
    half = -0.5 * jnp.sum(scaled * scaled, axis=0, keepdims=True)
    if not left:
        half = half + level
    halves = [part.astype(F32) for part in three_parts(half)]
    ones = [jnp.ones_like(half)] * 3
    tail = (halves + ones if left else ones + halves) + [jnp.zeros((10, half.shape[1]), F32)]
    parts = [high, high, middle, high, low, middle] if left else [high, middle, high, low, high, middle]
    return jnp.concatenate(parts + [jnp.concatenate(tail, axis=0).astype(BF16)], axis=0)


def feature_rows(feat):
    return 6 * feat + 16


def prepare_kernel(points_ref, inv_ref, right_ref, count_ref, sent_ref):
    feat, slots = points_ref.shape
    valid = lax.broadcasted_iota(jnp.int32, (1, slots), 1) < count_ref[0]
    row = lax.broadcasted_iota(jnp.int32, (feat, slots), 0)
    inverse = jnp.zeros((feat, slots), F32)
    for f in range(feat):
        inverse = jnp.where(row == f, inv_ref[f], inverse)
    scaled = points_ref[...] * inverse * math.sqrt(LOG2E)
    sent_ref[0, :feat, :] = jnp.where(valid, scaled, FAR)
    sent_ref[0, feat:, :] = jnp.where(valid, right_ref[...], 0.0)


def fill_right(near_ref, signal_ref, right_ref, feat):
    blocks, slots = right_ref.shape[1] // near_ref.shape[2], near_ref.shape[2]
    for b in range(blocks):
        level = jnp.log(jnp.full((1, slots), signal_ref[0], F32)) * LOG2E
        right_ref[:, b * slots : (b + 1) * slots] = features(near_ref[b, :feat, :], level, False)


def entries(left, right):
    powers = lax.dot_general(left, right, (((0,), (0,)), ((), ())), preferred_element_type=F32)
    return jnp.exp2(powers).astype(BF16)


def apply_kernel(feat, group, keep, begin, last, count, near_ref, signal_ref, noise_ref, *refs):
    far, refs = refs[:count], refs[count:]
    if begin:
        right_ref, refs = refs[-4], refs[:-4] + refs[-3:]
    else:
        right_ref, so_far_ref, refs = refs[0], refs[1], refs[2:]
    kept, refs = (refs[:count], refs[count:]) if keep else ((), refs)
    out_ref, left_ref, dirs_ref, sum_ref = refs
    slots = near_ref.shape[2]
    if begin:
        fill_right(near_ref, signal_ref, right_ref, feat)
        sum_ref[...] = jnp.zeros_like(sum_ref)
    else:
        sum_ref[...] = so_far_ref[...]
    for piece, far_ref in enumerate(far):

        def step(g, carry, piece=piece, far_ref=far_ref):
            for b in range(group):
                place = slice(b * slots, (b + 1) * slots)
                left_ref[:, place] = features(far_ref[g * group + b, :feat, :], None, True)
                dirs_ref[:, place] = far_ref[g * group + b, feat:, :].astype(BF16)
            block = entries(left_ref[...], right_ref[...])
            if keep:
                kept[piece][g] = block
            sum_ref[...] += jnp.dot(dirs_ref[...], block, preferred_element_type=F32)
            return carry

        lax.fori_loop(0, far_ref.shape[0] // group, step, 0)
    if not last:
        out_ref[...] = sum_ref[...]
        return
    for b in range(near_ref.shape[0]):
        direction = near_ref[b, feat:, :].astype(BF16).astype(F32)
        out_ref[b] = sum_ref[:, b * slots : (b + 1) * slots] + noise_ref[0] * direction


def apply_first(near, far, signal, noise, so_far, feat, group, keep, last=False):
    copies, slots, probes = near.shape[0], near.shape[2], near.shape[1] - feat
    wide, steps, begin = group * slots, far[0].shape[0] // group, so_far is None
    outs = [pltpu.VMEM((copies, probes, slots) if last else (probes, copies * slots), F32)]
    if keep:
        outs = [pltpu.VMEM((steps, wide, copies * slots), BF16)] * len(far) + outs
    if begin:
        outs = outs + [pltpu.VMEM((feature_rows(feat), copies * slots), BF16)]
    arrays = [near, *far, *([] if begin else so_far)]
    if keep:
        arrays = [stay(array) for array in arrays]
    done = pl.pallas_call(
        functools.partial(apply_kernel, feat, group, keep, begin, last, len(far)),
        out_shape=outs,
        in_specs=[VMEM, SMEM, SMEM] + [VMEM] * (len(arrays) - 1),
        out_specs=[VMEM] * len(outs),
        scratch_shapes=[
            pltpu.VMEM((feature_rows(feat), wide), BF16),
            pltpu.VMEM((probes, wide), BF16),
            pltpu.VMEM((probes, copies * slots), F32),
        ],
        compiler_params=pltpu.CompilerParams(vmem_limit_bytes=(16 if keep else 40) * 2**20),
        cost_estimate=pl.CostEstimate(
            flops=2 * copies * slots * len(far) * far[0].shape[0] * slots * 256,
            bytes_accessed=far[0].size * 4,
            transcendentals=0,
        ),
    )(arrays[0], signal, noise, *arrays[1:])
    kept, rest = (done[: len(far)], done[len(far) :]) if keep else ([None] * len(far), done)
    if begin:
        return kept, (rest[1], rest[0])
    return kept, rest[0] if last else (so_far[0], rest[0])


def second_kernel(feat, group, keep, copies, signal_ref, noise_ref, *refs):
    points, images, refs = refs[:PIECES], refs[PIECES : 2 * PIECES], refs[2 * PIECES :]
    if keep:
        kept, refs = refs[:PIECES], refs[PIECES:]
    (partial_ref, solution_ref, residual_ref, own_dir_ref, own_image_ref, norm_ref, product_ref, dirs_ref) = refs[:8]
    if not keep:
        right_ref, left_ref = refs[8:]
    slots, probes = images[0].shape[2], images[0].shape[1]
    pairs = list(zip(points, images))

    def over_blocks(visit, start):
        carry = start
        for x_ref, w_ref in pairs:
            carry = lax.fori_loop(0, x_ref.shape[0], functools.partial(visit, x_ref, w_ref), carry, unroll=True if x_ref.shape[0] <= 8 else 8)
        return carry

    def column(total):
        return jnp.sum(total, axis=1, keepdims=True)

    zero = jnp.zeros((probes, slots), F32)

    def sums(x_ref, w_ref, b, carry):
        norm, curve = carry
        right = x_ref[b, feat:, :]
        return norm + right * right, curve + right.astype(BF16).astype(F32) * w_ref[b]

    norm, curve = over_blocks(sums, (zero, zero))
    norm_now = column(norm)
    step_size = norm_now / column(curve)

    def next_sum(x_ref, w_ref, b, norm):
        residual = x_ref[b, feat:, :] - step_size * w_ref[b]
        return norm + residual * residual

    norm_next = column(over_blocks(next_sum, zero))
    ratio = norm_next / norm_now

    def direct(x_ref, w_ref, b):
        right = x_ref[b, feat:, :]
        first = right.astype(BF16).astype(F32)
        residual = right - step_size * w_ref[b]
        return residual, first, (residual + ratio * first).astype(BF16)

    product_ref[...] = jnp.zeros_like(product_ref)
    if not keep:
        fill_right(points[0], signal_ref, right_ref, feat)
    for piece, (x_ref, w_ref) in enumerate(pairs):

        def step(g, carry, piece=piece, x_ref=x_ref, w_ref=w_ref):
            for b in range(group):
                place = slice(b * slots, (b + 1) * slots)
                dirs_ref[:, place] = direct(x_ref, w_ref, g * group + b)[2]
                if not keep:
                    left_ref[:, place] = features(x_ref[g * group + b, :feat, :], None, True)
            block = kept[piece][g] if keep else entries(left_ref[...], right_ref[...])
            product_ref[...] += jnp.dot(dirs_ref[...], block, preferred_element_type=F32)
            return carry

        lax.fori_loop(0, x_ref.shape[0] // group, step, 0)

    total = zero
    for b in range(copies):
        residual, first, direction = direct(points[0], images[0], b)
        direction = direction.astype(F32)
        image = product_ref[:, b * slots : (b + 1) * slots] + noise_ref[0] * direction
        total = total + direction * image
        if b == 0:
            solution_ref[...] = step_size * first
            residual_ref[...] = residual
            own_dir_ref[...] = direction
            own_image_ref[...] = image
    partial_ref[...] = jnp.broadcast_to(column(total), partial_ref.shape)
    norm_ref[...] = jnp.broadcast_to(norm_next, norm_ref.shape)


def second(signal, noise, points, images, kept, copies, feat, group):
    keep = kept is not None
    slots, probes = images[0].shape[2], images[0].shape[1]
    own, small, wide = pltpu.VMEM((probes, slots), F32), pltpu.VMEM((probes, 128), F32), group * slots
    scratch = [pltpu.VMEM((probes, copies * slots), F32), pltpu.VMEM((probes, wide), BF16)]
    if keep:
        points, images, kept = ([stay(piece) for piece in pieces] for pieces in (points, images, kept))
    else:
        scratch += [pltpu.VMEM((feature_rows(feat), copies * slots), BF16), pltpu.VMEM((feature_rows(feat), wide), BF16)]
    return pl.pallas_call(
        functools.partial(second_kernel, feat, group, keep, copies),
        out_shape=[small, own, own, own, own, small],
        in_specs=[SMEM, SMEM] + [VMEM] * (3 * PIECES if keep else 2 * PIECES),
        out_specs=[VMEM] * 6,
        scratch_shapes=scratch,
        compiler_params=pltpu.CompilerParams(vmem_limit_bytes=(16 if keep else 48) * 2**20),
    )(signal, noise, *points, *images, *(kept or ()))


def finish_kernel(curve_ref, norm_ref, solution_ref, residual_ref, direction_ref, image_ref, out_ref, left_ref):
    step_size = norm_ref[:, :1] / curve_ref[:, :1]
    out_ref[...] = solution_ref[...] + step_size * direction_ref[...]
    left_ref[...] = residual_ref[...] - step_size * image_ref[...]


def gather(held, bits, count):
    for bit in bits:
        held = jnp.concatenate([held, swap(held, bit, count)], axis=0)
    return held


def body(count, points, inv_lengths, signal_level, noise_level, right_sides, block_counts):
    slots, feat = points.shape
    probes = right_sides.shape[1]
    copies = COPIES
    while copies > 1 and (copies * PIECES > count or copies * count * slots * slots * 2 > KEEP_BYTES):
        copies //= 2
    keep = copies * count * slots * slots * 2 <= KEEP_BYTES
    group = math.gcd(count // PIECES, 8)
    bits = [1 << k for k in reversed(range(count.bit_length() - 1))]
    later = bits[copies.bit_length() - 1 :]
    one, two, core = bits[-3:]
    own = pl.pallas_call(
        prepare_kernel,
        out_shape=pltpu.VMEM((1, feat + probes, slots), F32),
        in_specs=[VMEM, SMEM, VMEM, SMEM],
        out_specs=VMEM,
    )(points.T, inv_lengths, right_sides.T, block_counts)
    first = functools.partial(apply_first, feat=feat, group=group, keep=keep)

    held = gather(own, bits[:-3], count)
    near = held[:copies]
    beside, up, over, corner = (swap(held, bit, count) for bit in (core, one, two, one | two))
    kept_0, product = first(near, [held, beside], signal_level, noise_level, None)
    up, product = lax.optimization_barrier((up, product))
    up_beside = swap(up, core, count)
    kept_1, product = first(near, [up], signal_level, noise_level, product)
    over, product = lax.optimization_barrier((over, product))
    over_beside = swap(over, core, count)
    kept_2, product = first(near, [up_beside, over], signal_level, noise_level, product)
    corner, product = lax.optimization_barrier((corner, product))
    corner_beside = swap(corner, core, count)
    kept_3, product = first(near, [over_beside, corner], signal_level, noise_level, product)
    kept_4, image = first(near, [corner_beside], signal_level, noise_level, product, last=True)
    pieces = [held, beside, up, up_beside, over, over_beside, corner, corner_beside]
    kept = [*kept_0, *kept_1, *kept_2, *kept_3, *kept_4]

    held = gather(image, later[:-3], count)
    direct = [held] + [swap(held, bit, count) for bit in (one, two, one | two)]
    images = [array for piece in direct for array in (piece, swap(piece, core, count))]
    partial, solution, residual, direction, own_image, norm = second(
        signal_level, noise_level, pieces, images, kept if keep else None, copies, feat, group
    )
    for bit in reversed(later):
        partial = partial + swap(partial, bit, count)
    done = jax.ShapeDtypeStruct((probes, slots), F32)
    solution, residual = pl.pallas_call(
        finish_kernel,
        out_shape=[done, done],
        in_specs=[VMEM] * 6,
        out_specs=[VMEM] * 2,
    )(*[stay(array) for array in (partial, norm, solution, residual, direction, own_image)])
    return solution.T, residual.T


def solution(mesh):
    count = math.prod(mesh.shape[axis] for axis in AXES)
    rows = P(AXES, None)
    return jax.shard_map(
        functools.partial(body, count),
        mesh=mesh,
        in_specs=(rows, P(), P(), P(), rows, P(AXES)),
        out_specs=(rows, rows),
        check_vma=False,
    )
```

```python
import functools
import math

import jax
import jax.numpy as jnp
from jax import lax
from jax.experimental import pallas as pl
from jax.experimental.pallas import tpu as pltpu
from jax.sharding import PartitionSpec as P

AXES = ("row", "col")
LOG2E = 1.0 / math.log(2.0)
FAR = 64.0
KEEP_BYTES = 20 * 2**20
COPIES = 4
PIECES = 8
F32, BF16 = jnp.float32, jnp.bfloat16
VMEM = pl.BlockSpec(memory_space=pltpu.VMEM)


def stay(array):
    return pltpu.with_memory_space_constraint(array, pltpu.VMEM)


def swap(array, bit, count):
    return lax.ppermute(array, AXES, [(i, i ^ bit) for i in range(count)])


def three_parts(wide):
    high = wide.astype(BF16)
    rest = wide - high.astype(F32)
    middle = rest.astype(BF16)
    return high, middle, (rest - middle.astype(F32)).astype(BF16)


def features(scaled, level, left):
    high, middle, low = three_parts(scaled)
    half = -0.5 * jnp.sum(scaled * scaled, axis=0, keepdims=True)
    if not left:
        half = half + level
    halves = [part.astype(F32) for part in three_parts(half)]
    ones = [jnp.ones_like(half)] * 3
    tail = (halves + ones if left else ones + halves) + [jnp.zeros((10, half.shape[1]), F32)]
    parts = [high, high, middle, high, low, middle] if left else [high, middle, high, low, high, middle]
    return jnp.concatenate(parts + [jnp.concatenate(tail, axis=0).astype(BF16)], axis=0)


def feature_rows(feat):
    return 6 * feat + 16


def prepare_kernel(points_ref, inv_ref, right_ref, count_ref, sent_ref):
    feat, slots = points_ref.shape
    valid = lax.broadcasted_iota(jnp.int32, (1, slots), 1) < count_ref[0]
    row = lax.broadcasted_iota(jnp.int32, (feat, slots), 0)
    inverse = jnp.zeros((feat, slots), F32)
    for f in range(feat):
        inverse = jnp.where(row == f, inv_ref[f], inverse)
    scaled = points_ref[...] * inverse * math.sqrt(LOG2E)
    sent_ref[0, :feat, :] = jnp.where(valid, scaled, FAR)
    sent_ref[0, feat:, :] = jnp.where(valid, right_ref[...], 0.0)


def prepare(points, inv_lengths, right_sides, block_counts):
    smem = pl.BlockSpec(memory_space=pltpu.SMEM)
    return pl.pallas_call(
        prepare_kernel,
        out_shape=pltpu.VMEM((1, points.shape[1] + right_sides.shape[1], points.shape[0]), F32),
        in_specs=[VMEM, smem, VMEM, smem],
        out_specs=VMEM,
    )(points.T, inv_lengths, right_sides.T, block_counts)


def fill_right(near_ref, levels_ref, right_ref, feat):
    blocks, slots = right_ref.shape[1] // near_ref.shape[2], near_ref.shape[2]
    for b in range(blocks):
        right_ref[:, b * slots : (b + 1) * slots] = features(near_ref[b, :feat, :], levels_ref[0:1, :], False)


def entries(left, right):
    powers = lax.dot_general(left, right, (((0,), (0,)), ((), ())), preferred_element_type=F32)
    return jnp.exp2(powers).astype(BF16)


def apply_kernel(feat, group, keep, begin, last, count, near_ref, levels_ref, *refs):
    far, refs = refs[:count], refs[count:]
    if begin:
        right_ref, refs = refs[-4], refs[:-4] + refs[-3:]
    else:
        right_ref, so_far_ref, refs = refs[0], refs[1], refs[2:]
    kept, refs = (refs[:count], refs[count:]) if keep else ((), refs)
    out_ref, left_ref, dirs_ref, sum_ref = refs
    slots = near_ref.shape[2]
    if begin:
        fill_right(near_ref, levels_ref, right_ref, feat)
        sum_ref[...] = jnp.zeros_like(sum_ref)
    else:
        sum_ref[...] = so_far_ref[...]
    for piece, far_ref in enumerate(far):

        def step(g, carry, piece=piece, far_ref=far_ref):
            for b in range(group):
                place = slice(b * slots, (b + 1) * slots)
                left_ref[:, place] = features(far_ref[g * group + b, :feat, :], None, True)
                dirs_ref[:, place] = far_ref[g * group + b, feat:, :].astype(BF16)
            block = entries(left_ref[...], right_ref[...])
            if keep:
                kept[piece][g] = block
            sum_ref[...] += jnp.dot(dirs_ref[...], block, preferred_element_type=F32)
            return carry

        lax.fori_loop(0, far_ref.shape[0] // group, step, 0)
    if not last:
        out_ref[...] = sum_ref[...]
        return
    for b in range(near_ref.shape[0]):
        direction = near_ref[b, feat:, :].astype(BF16).astype(F32)
        out_ref[b] = sum_ref[:, b * slots : (b + 1) * slots] + levels_ref[1:2, :] * direction


def apply_first(near, far, levels, so_far, feat, group, keep, last=False):
    copies, slots, probes = near.shape[0], near.shape[2], near.shape[1] - feat
    wide, steps, begin = group * slots, far[0].shape[0] // group, so_far is None
    outs = [pltpu.VMEM((copies, probes, slots) if last else (probes, copies * slots), F32)]
    if keep:
        outs = [pltpu.VMEM((steps, wide, copies * slots), BF16)] * len(far) + outs
    if begin:
        outs = outs + [pltpu.VMEM((feature_rows(feat), copies * slots), BF16)]
    arrays = [near, levels, *far, *([] if begin else so_far)]
    if keep:
        arrays = [stay(array) for array in arrays]
    done = pl.pallas_call(
        functools.partial(apply_kernel, feat, group, keep, begin, last, len(far)),
        out_shape=outs,
        in_specs=[VMEM] * len(arrays),
        out_specs=[VMEM] * len(outs),
        scratch_shapes=[
            pltpu.VMEM((feature_rows(feat), wide), BF16),
            pltpu.VMEM((probes, wide), BF16),
            pltpu.VMEM((probes, copies * slots), F32),
        ],
        compiler_params=pltpu.CompilerParams(vmem_limit_bytes=(16 if keep else 40) * 2**20),
        cost_estimate=pl.CostEstimate(
            flops=2 * copies * slots * len(far) * far[0].shape[0] * slots * 256,
            bytes_accessed=far[0].size * 4,
            transcendentals=0,
        ),
    )(*arrays)
    kept, rest = (done[: len(far)], done[len(far) :]) if keep else ([None] * len(far), done)
    if begin:
        return kept, (rest[1], rest[0])
    return kept, rest[0] if last else (so_far[0], rest[0])


def second_kernel(feat, group, keep, copies, levels_ref, *refs):
    points, images, refs = refs[:PIECES], refs[PIECES : 2 * PIECES], refs[2 * PIECES :]
    if keep:
        kept, refs = refs[:PIECES], refs[PIECES:]
    (partial_ref, solution_ref, residual_ref, own_dir_ref, own_image_ref, norm_ref, product_ref, dirs_ref) = refs[:8]
    if not keep:
        right_ref, left_ref = refs[8:]
    slots, probes = images[0].shape[2], images[0].shape[1]
    pairs = list(zip(points, images))

    def over_blocks(visit, start):
        carry = start
        for x_ref, w_ref in pairs:
            carry = lax.fori_loop(0, x_ref.shape[0], functools.partial(visit, x_ref, w_ref), carry, unroll=True if x_ref.shape[0] <= 8 else 8)
        return carry

    def column(total):
        return jnp.sum(total, axis=1, keepdims=True)

    zero = jnp.zeros((probes, slots), F32)

    def sums(x_ref, w_ref, b, carry):
        norm, curve = carry
        right = x_ref[b, feat:, :]
        return norm + right * right, curve + right.astype(BF16).astype(F32) * w_ref[b]

    norm, curve = over_blocks(sums, (zero, zero))
    norm_now = column(norm)
    step_size = norm_now / column(curve)

    def next_sum(x_ref, w_ref, b, norm):
        residual = x_ref[b, feat:, :] - step_size * w_ref[b]
        return norm + residual * residual

    norm_next = column(over_blocks(next_sum, zero))
    ratio = norm_next / norm_now

    def direct(x_ref, w_ref, b):
        right = x_ref[b, feat:, :]
        first = right.astype(BF16).astype(F32)
        residual = right - step_size * w_ref[b]
        return residual, first, (residual + ratio * first).astype(BF16)

    product_ref[...] = jnp.zeros_like(product_ref)
    if not keep:
        fill_right(points[0], levels_ref, right_ref, feat)
    for piece, (x_ref, w_ref) in enumerate(pairs):

        def step(g, carry, piece=piece, x_ref=x_ref, w_ref=w_ref):
            for b in range(group):
                place = slice(b * slots, (b + 1) * slots)
                dirs_ref[:, place] = direct(x_ref, w_ref, g * group + b)[2]
                if not keep:
                    left_ref[:, place] = features(x_ref[g * group + b, :feat, :], None, True)
            block = kept[piece][g] if keep else entries(left_ref[...], right_ref[...])
            product_ref[...] += jnp.dot(dirs_ref[...], block, preferred_element_type=F32)
            return carry

        lax.fori_loop(0, x_ref.shape[0] // group, step, 0)

    total = zero
    for b in range(copies):
        residual, first, direction = direct(points[0], images[0], b)
        direction = direction.astype(F32)
        image = product_ref[:, b * slots : (b + 1) * slots] + levels_ref[1:2, :] * direction
        total = total + direction * image
        if b == 0:
            solution_ref[...] = step_size * first
            residual_ref[...] = residual
            own_dir_ref[...] = direction
            own_image_ref[...] = image
    partial_ref[...] = jnp.broadcast_to(column(total), partial_ref.shape)
    norm_ref[...] = jnp.broadcast_to(norm_next, norm_ref.shape)


def second(levels, points, images, kept, copies, feat, group):
    keep = kept is not None
    slots, probes = images[0].shape[2], images[0].shape[1]
    own, small, wide = pltpu.VMEM((probes, slots), F32), pltpu.VMEM((probes, 128), F32), group * slots
    scratch = [pltpu.VMEM((probes, copies * slots), F32), pltpu.VMEM((probes, wide), BF16)]
    if keep:
        levels = stay(levels)
        points, images, kept = ([stay(piece) for piece in pieces] for pieces in (points, images, kept))
    else:
        scratch += [pltpu.VMEM((feature_rows(feat), copies * slots), BF16), pltpu.VMEM((feature_rows(feat), wide), BF16)]
    return pl.pallas_call(
        functools.partial(second_kernel, feat, group, keep, copies),
        out_shape=[small, own, own, own, own, small],
        in_specs=[VMEM] * (3 * PIECES + 1 if keep else 2 * PIECES + 1),
        out_specs=[VMEM] * 6,
        scratch_shapes=scratch,
        compiler_params=pltpu.CompilerParams(vmem_limit_bytes=(16 if keep else 48) * 2**20),
    )(levels, *points, *images, *(kept or ()))


def finish_kernel(curve_ref, norm_ref, solution_ref, residual_ref, direction_ref, image_ref, out_ref, left_ref):
    step_size = norm_ref[:, :1] / curve_ref[:, :1]
    out_ref[...] = solution_ref[...] + step_size * direction_ref[...]
    left_ref[...] = residual_ref[...] - step_size * image_ref[...]


def gather(held, bits, count):
    for at in range(0, len(bits), 2):
        pair = bits[at : at + 2]
        flips = pair if len(pair) == 1 else [pair[0], pair[1], sum(pair)]
        held = jnp.concatenate([held] + [swap(held, flip, count) for flip in flips], axis=0)
    return held


def total(held, bits, count):
    for at in range(0, len(bits), 2):
        pair = bits[at : at + 2]
        flips = pair if len(pair) == 1 else [pair[0], pair[1], sum(pair)]
        held = sum([swap(held, flip, count) for flip in flips], held)
    return held


def body(count, points, inv_lengths, signal_level, noise_level, right_sides, block_counts):
    slots, feat = points.shape
    probes = right_sides.shape[1]
    copies = COPIES
    while copies > 1 and (copies * PIECES > count or copies * count * slots * slots * 2 > KEEP_BYTES):
        copies //= 2
    keep = copies * count * slots * slots * 2 <= KEEP_BYTES
    group = math.gcd(count // PIECES, 8)
    bits = [1 << k for k in reversed(range(count.bit_length() - 1))]
    later = bits[copies.bit_length() - 1 :]
    one, two, core = bits[-3:]
    own = prepare(points, inv_lengths, right_sides, block_counts)
    own, signal_level, noise_level = lax.optimization_barrier((own, signal_level, noise_level))
    levels = jnp.stack([jnp.log(signal_level[0]) * LOG2E, noise_level[0]])
    levels = jnp.broadcast_to(levels[:, None], (2, slots))
    first = functools.partial(apply_first, feat=feat, group=group, keep=keep)

    held = gather(own, bits[:-3], count)
    held, levels = lax.optimization_barrier((held, levels))
    near = held[:copies]
    beside, up, over = (swap(held, bit, count) for bit in (core, one, two))
    kept_0, product = first(near, [held, beside], levels, None)
    up, product = lax.optimization_barrier((up, product))
    corner, up_beside = swap(up, two, count), swap(up, core, count)
    kept_1, product = first(near, [up], levels, product)
    over, product = lax.optimization_barrier((over, product))
    over_beside = swap(over, core, count)
    kept_2, product = first(near, [up_beside, over], levels, product)
    corner, product = lax.optimization_barrier((corner, product))
    corner_beside = swap(corner, core, count)
    kept_3, product = first(near, [over_beside, corner], levels, product)
    kept_4, image = first(near, [corner_beside], levels, product, last=True)
    pieces = [held, beside, up, up_beside, over, over_beside, corner, corner_beside]
    kept = [*kept_0, *kept_1, *kept_2, *kept_3, *kept_4]

    held = gather(image, later[:-3], count)
    up, over, corner = (swap(held, bit, count) for bit in (one, two, one | two))
    beside, up_beside, over_beside, corner_beside = (swap(array, core, count) for array in (held, up, over, corner))
    images = [held, beside, up, up_beside, over, over_beside, corner, corner_beside]
    partial, solution, residual, direction, own_image, norm = second(
        levels, pieces, images, kept if keep else None, copies, feat, group
    )
    partial = total(partial + swap(partial, core, count), later[:-1][::-1], count)
    done = jax.ShapeDtypeStruct((probes, slots), F32)
    solution, residual = pl.pallas_call(
        finish_kernel,
        out_shape=[done, done],
        in_specs=[VMEM] * 6,
        out_specs=[VMEM] * 2,
    )(*[stay(array) for array in (partial, norm, solution, residual, direction, own_image)])
    return solution.T, residual.T


def solution(mesh):
    count = math.prod(mesh.shape[axis] for axis in AXES)
    rows = P(AXES, None)
    return jax.shard_map(
        functools.partial(body, count),
        mesh=mesh,
        in_specs=(rows, P(), P(), P(), rows, P(AXES)),
        out_specs=(rows, rows),
        check_vma=False,
    )
```

```python
import functools
import math

import jax
import jax.numpy as jnp
from jax import lax
from jax.experimental import pallas as pl
from jax.experimental.pallas import tpu as pltpu
from jax.sharding import PartitionSpec as P

AXES = ("row", "col")
LOG2E = 1.0 / math.log(2.0)
FAR = 64.0
KEEP_BYTES = 20 * 2**20
COPIES = 4
PIECES = 8
F32, BF16 = jnp.float32, jnp.bfloat16
VMEM = pl.BlockSpec(memory_space=pltpu.VMEM)


def stay(array):
    return pltpu.with_memory_space_constraint(array, pltpu.VMEM)


def swap(array, bit, count):
    return lax.ppermute(array, AXES, [(i, i ^ bit) for i in range(count)])


def two_parts(wide):
    high = wide.astype(BF16)
    return high, (wide - high.astype(F32)).astype(BF16)


def three_parts(wide):
    high, _ = two_parts(wide)
    return high, *two_parts(wide - high.astype(F32))


def features(parts, level, left):
    feat = parts.shape[0] // 2
    high, low = parts[:feat], parts[feat:]
    scaled = high.astype(F32) + low.astype(F32)
    half = -0.5 * jnp.sum(scaled * scaled, axis=0, keepdims=True)
    if not left:
        half = half + level
    halves = [part.astype(F32) for part in three_parts(half)]
    ones = [jnp.ones_like(half)] * 3
    tail = (halves + ones if left else ones + halves) + [jnp.zeros((10, half.shape[1]), F32)]
    rows = [high, high, low, low] if left else [high, low, high, low]
    return jnp.concatenate(rows + [jnp.concatenate(tail, axis=0).astype(BF16)], axis=0)


def feature_rows(feat):
    return 4 * feat + 16


def prepare_kernel(points_ref, inv_ref, right_ref, count_ref, sent_ref):
    feat, slots = points_ref.shape
    probes = right_ref.shape[0]
    valid = lax.broadcasted_iota(jnp.int32, (1, slots), 1) < count_ref[0]
    row = lax.broadcasted_iota(jnp.int32, (feat, slots), 0)
    inverse = jnp.zeros((feat, slots), F32)
    for f in range(feat):
        inverse = jnp.where(row == f, inv_ref[f], inverse)
    scaled = points_ref[...] * inverse * math.sqrt(LOG2E)
    high, low = two_parts(jnp.where(valid, scaled, FAR))
    direction, rest = two_parts(jnp.where(valid, right_ref[...], 0.0))
    sent_ref[0, :feat, :] = high
    sent_ref[0, feat : 2 * feat, :] = low
    sent_ref[0, 2 * feat : 2 * feat + probes, :] = direction
    sent_ref[0, 2 * feat + probes :, :] = rest


def prepare(points, inv_lengths, right_sides, block_counts):
    smem = pl.BlockSpec(memory_space=pltpu.SMEM)
    return pl.pallas_call(
        prepare_kernel,
        out_shape=pltpu.VMEM((1, 2 * points.shape[1] + 2 * right_sides.shape[1], points.shape[0]), BF16),
        in_specs=[VMEM, smem, VMEM, smem],
        out_specs=VMEM,
    )(points.T, inv_lengths, right_sides.T, block_counts)


def fill_right(near_ref, levels_ref, right_ref, feat):
    blocks, slots = right_ref.shape[1] // near_ref.shape[2], near_ref.shape[2]
    for b in range(blocks):
        right_ref[:, b * slots : (b + 1) * slots] = features(near_ref[b, : 2 * feat, :], levels_ref[0:1, :], False)


def entries(left, right):
    powers = lax.dot_general(left, right, (((0,), (0,)), ((), ())), preferred_element_type=F32)
    return jnp.exp2(powers).astype(BF16)


def apply_kernel(feat, group, keep, begin, last, count, near_ref, levels_ref, *refs):
    far, refs = refs[:count], refs[count:]
    if begin:
        right_ref, refs = refs[-4], refs[:-4] + refs[-3:]
    else:
        right_ref, so_far_ref, refs = refs[0], refs[1], refs[2:]
    kept, refs = (refs[:count], refs[count:]) if keep else ((), refs)
    own_ref = None
    if last:
        own_ref, refs = refs[1], refs[:1] + refs[2:]
    out_ref, left_ref, dirs_ref, sum_ref = refs
    slots, probes = near_ref.shape[2], dirs_ref.shape[0]
    if begin:
        fill_right(near_ref, levels_ref, right_ref, feat)
        sum_ref[...] = jnp.zeros_like(sum_ref)
    else:
        sum_ref[...] = so_far_ref[...]
    for piece, far_ref in enumerate(far):

        def step(g, carry, piece=piece, far_ref=far_ref):
            for b in range(group):
                place = slice(b * slots, (b + 1) * slots)
                left_ref[:, place] = features(far_ref[g * group + b, : 2 * feat, :], None, True)
                dirs_ref[:, place] = far_ref[g * group + b, 2 * feat :, :]
            block = entries(left_ref[...], right_ref[...])
            if keep:
                kept[piece][g] = block
            sum_ref[...] += jnp.dot(dirs_ref[...], block, preferred_element_type=F32)
            return carry

        lax.fori_loop(0, far_ref.shape[0] // group, step, 0)
    if not last:
        out_ref[...] = sum_ref[...]
        return
    images, rests = [], []
    norm = curve = jnp.zeros((probes, slots), F32)
    for b in range(near_ref.shape[0]):
        direction = near_ref[b, 2 * feat : 2 * feat + probes, :].astype(F32)
        rest = near_ref[b, 2 * feat + probes :, :].astype(F32)
        image = sum_ref[:, b * slots : (b + 1) * slots] + levels_ref[1:2, :] * direction
        norm = norm + (direction + rest) * (direction + rest)
        curve = curve + direction * image
        images.append(image)
        rests.append(rest)
    own_ref[...] = images[0]
    norm, curve = (jnp.sum(each, axis=1, keepdims=True) for each in (norm, curve))
    slope = jnp.where(norm > 0.0, curve / norm, 0.0)
    for b, (image, rest) in enumerate(zip(images, rests)):
        out_ref[0, b * probes : (b + 1) * probes, :] = image - slope * rest
    lane = lax.broadcasted_iota(jnp.int32, (probes, 128), 1)
    both = jnp.where(lane == 0, norm, jnp.where(lane == 1, curve, 0.0))
    flat = jnp.concatenate([both, jnp.zeros((128 - probes, 128), F32)], axis=0).T
    out_ref[0, len(images) * probes :, :] = jnp.concatenate([flat[:8], jnp.zeros((8, slots - 128), F32)], axis=1)


def apply_first(near, far, levels, so_far, feat, group, keep, last=False):
    copies, slots, probes = near.shape[0], near.shape[2], far[0].shape[1] - 2 * feat
    wide, steps, begin = group * slots, far[0].shape[0] // group, so_far is None
    outs = [pltpu.VMEM((1, copies * probes + 8, slots) if last else (probes, copies * slots), F32)]
    if last:
        outs = outs + [pltpu.VMEM((probes, slots), F32)]
    if keep:
        outs = [pltpu.VMEM((steps, wide, copies * slots), BF16)] * len(far) + outs
    if begin:
        outs = outs + [pltpu.VMEM((feature_rows(feat), copies * slots), BF16)]
    arrays = [near, levels, *far, *([] if begin else so_far)]
    if keep:
        arrays = [stay(array) for array in arrays]
    done = pl.pallas_call(
        functools.partial(apply_kernel, feat, group, keep, begin, last, len(far)),
        out_shape=outs,
        in_specs=[VMEM] * len(arrays),
        out_specs=[VMEM] * len(outs),
        scratch_shapes=[
            pltpu.VMEM((feature_rows(feat), wide), BF16),
            pltpu.VMEM((probes, wide), BF16),
            pltpu.VMEM((probes, copies * slots), F32),
        ],
        compiler_params=pltpu.CompilerParams(vmem_limit_bytes=(16 if keep else 40) * 2**20),
        cost_estimate=pl.CostEstimate(
            flops=2 * copies * slots * len(far) * far[0].shape[0] * slots * 256,
            bytes_accessed=far[0].size * 4,
            transcendentals=0,
        ),
    )(*arrays)
    kept, rest = (done[: len(far)], done[len(far) :]) if keep else ([None] * len(far), done)
    if begin:
        return kept, (rest[1], rest[0])
    return kept, rest if last else (so_far[0], rest[0])


def second_kernel(feat, group, keep, copies, levels_ref, own_ref, own_image_in_ref, *refs):
    points, images, refs = refs[:PIECES], refs[PIECES : 2 * PIECES], refs[2 * PIECES :]
    if keep:
        kept, refs = refs[:PIECES], refs[PIECES:]
    (partial_ref, solution_ref, residual_ref, own_dir_ref, own_image_ref, norm_ref, product_ref, dirs_ref) = refs[:8]
    if not keep:
        right_ref, left_ref = refs[8:]
    slots, probes = images[0].shape[2], own_image_in_ref.shape[0]
    pairs = list(zip(points, images))

    def over_blocks(visit, start):
        carry = start
        for x_ref, w_ref in pairs:
            blocks = x_ref.shape[0]
            carry = lax.fori_loop(0, blocks, functools.partial(visit, x_ref, w_ref), carry, unroll=min(blocks, 8))
        return carry

    def column(wide):
        return jnp.sum(wide, axis=1, keepdims=True)

    def residual_of(x_ref, w_ref, b):
        first = x_ref[b, 2 * feat :, :].astype(F32)
        image = w_ref[b // copies, pl.ds(pl.multiple_of(b % copies * probes, probes), probes), :]
        return first - step_size * image, first

    sums = jnp.zeros((8, 128), F32)
    for w_ref in images:
        for g in range(w_ref.shape[0]):
            sums = sums + w_ref[g, copies * probes :, :128]
    sums = jnp.concatenate([sums, jnp.zeros((120, 128), F32)], axis=0).T[:probes]
    norm_now = sums[:, 0:1]
    step_size = norm_now / sums[:, 1:2]

    def next_sum(x_ref, w_ref, b, norm):
        residual, _ = residual_of(x_ref, w_ref, b)
        return norm + residual * residual

    norm_next = column(over_blocks(next_sum, jnp.zeros((probes, slots), F32)))
    ratio = norm_next / norm_now

    def direct(x_ref, w_ref, b):
        residual, first = residual_of(x_ref, w_ref, b)
        return (residual + ratio * first).astype(BF16)

    product_ref[...] = jnp.zeros_like(product_ref)
    if not keep:
        fill_right(points[0], levels_ref, right_ref, feat)
    for piece, (x_ref, w_ref) in enumerate(pairs):

        def step(g, carry, piece=piece, x_ref=x_ref, w_ref=w_ref):
            for b in range(group):
                place = slice(b * slots, (b + 1) * slots)
                dirs_ref[:, place] = direct(x_ref, w_ref, g * group + b)
                if not keep:
                    left_ref[:, place] = features(x_ref[g * group + b, : 2 * feat, :], None, True)
            block = kept[piece][g] if keep else entries(left_ref[...], right_ref[...])
            product_ref[...] += jnp.dot(dirs_ref[...], block, preferred_element_type=F32)
            return carry

        lax.fori_loop(0, x_ref.shape[0] // group, step, 0)

    curve = jnp.zeros((probes, slots), F32)
    for b in range(copies):
        direction = direct(points[0], images[0], b).astype(F32)
        curve = curve + direction * (product_ref[:, b * slots : (b + 1) * slots] + levels_ref[1:2, :] * direction)
    first = own_ref[0, 2 * feat : 2 * feat + probes, :].astype(F32)
    right = first + own_ref[0, 2 * feat + probes :, :].astype(F32)
    residual = right - step_size * own_image_in_ref[...]
    direction = (residual + ratio * first).astype(BF16).astype(F32)
    solution_ref[...] = step_size * first
    residual_ref[...] = residual
    own_dir_ref[...] = direction
    own_image_ref[...] = product_ref[:, :slots] + levels_ref[1:2, :] * direction
    partial_ref[...] = jnp.broadcast_to(column(curve), partial_ref.shape)
    norm_ref[...] = jnp.broadcast_to(norm_next, norm_ref.shape)


def second(levels, own, own_image, points, images, kept, copies, feat, group):
    keep = kept is not None
    slots, probes = own_image.shape[1], own_image.shape[0]
    one, small, wide = pltpu.VMEM((probes, slots), F32), pltpu.VMEM((probes, 128), F32), group * slots
    scratch = [pltpu.VMEM((probes, copies * slots), F32), pltpu.VMEM((probes, wide), BF16)]
    arrays = [levels, own, own_image, *points, *images, *(kept or ())]
    if keep:
        arrays = [stay(array) for array in arrays]
    else:
        scratch += [pltpu.VMEM((feature_rows(feat), copies * slots), BF16), pltpu.VMEM((feature_rows(feat), wide), BF16)]
    return pl.pallas_call(
        functools.partial(second_kernel, feat, group, keep, copies),
        out_shape=[small, one, one, one, one, small],
        in_specs=[VMEM] * len(arrays),
        out_specs=[VMEM] * 6,
        scratch_shapes=scratch,
        compiler_params=pltpu.CompilerParams(vmem_limit_bytes=(16 if keep else 48) * 2**20),
    )(*arrays)


def finish_kernel(curve_ref, norm_ref, solution_ref, residual_ref, direction_ref, image_ref, out_ref, left_ref):
    step_size = norm_ref[:, :1] / curve_ref[:, :1]
    out_ref[...] = solution_ref[...] + step_size * direction_ref[...]
    left_ref[...] = residual_ref[...] - step_size * image_ref[...]


def gather(held, bits, count):
    for at in range(0, len(bits), 2):
        pair = bits[at : at + 2]
        flips = pair if len(pair) == 1 else [pair[0], pair[1], sum(pair)]
        held = jnp.concatenate([held] + [swap(held, flip, count) for flip in flips], axis=0)
    return held


def total(held, bits, count):
    for at in range(0, len(bits), 2):
        pair = bits[at : at + 2]
        flips = pair if len(pair) == 1 else [pair[0], pair[1], sum(pair)]
        held = sum([swap(held, flip, count) for flip in flips], held)
    return held


def body(count, points, inv_lengths, signal_level, noise_level, right_sides, block_counts):
    slots, feat = points.shape
    probes = right_sides.shape[1]
    copies = COPIES
    while copies > 1 and (copies * PIECES > count or copies * count * slots * slots * 2 > KEEP_BYTES):
        copies //= 2
    keep = copies * count * slots * slots * 2 <= KEEP_BYTES
    group = math.gcd(count // PIECES, 8)
    bits = [1 << k for k in reversed(range(count.bit_length() - 1))]
    later = bits[copies.bit_length() - 1 :]
    one, two, core = bits[-3:]
    own = prepare(points, inv_lengths, right_sides, block_counts)
    own, signal_level, noise_level = lax.optimization_barrier((own, signal_level, noise_level))
    levels = jnp.stack([jnp.log(signal_level[0]) * LOG2E, noise_level[0]])
    levels = jnp.broadcast_to(levels[:, None], (2, slots))
    first = functools.partial(apply_first, feat=feat, group=group, keep=keep)

    held = gather(own, bits[:-3], count)
    held, levels = lax.optimization_barrier((held, levels))
    near = held[:copies]
    held = held[:, : 2 * feat + probes]
    beside, up, over = (swap(held, bit, count) for bit in (core, one, two))
    kept_0, product = first(near, [held, beside], levels, None)
    up, product = lax.optimization_barrier((up, product))
    corner, up_beside = swap(up, two, count), swap(up, core, count)
    kept_1, product = first(near, [up], levels, product)
    over, product = lax.optimization_barrier((over, product))
    over_beside = swap(over, core, count)
    kept_2, product = first(near, [up_beside, over], levels, product)
    corner, product = lax.optimization_barrier((corner, product))
    corner_beside = swap(corner, core, count)
    kept_3, product = first(near, [over_beside, corner], levels, product)
    kept_4, (image, own_image) = first(near, [corner_beside], levels, product, last=True)
    pieces = [held, beside, up, up_beside, over, over_beside, corner, corner_beside]
    kept = [*kept_0, *kept_1, *kept_2, *kept_3, *kept_4]

    held = gather(image, later[:-3], count)
    up, over, corner = (swap(held, bit, count) for bit in (one, two, one | two))
    beside, up_beside, over_beside, corner_beside = (swap(array, core, count) for array in (held, up, over, corner))
    images = [held, beside, up, up_beside, over, over_beside, corner, corner_beside]
    partial, solution, residual, direction, second_image, norm = second(
        levels, own, own_image, pieces, images, kept if keep else None, copies, feat, group
    )
    partial = total(partial + swap(partial, core, count), later[:-1][::-1], count)
    done = jax.ShapeDtypeStruct((probes, slots), F32)
    solution, residual = pl.pallas_call(
        finish_kernel,
        out_shape=[done, done],
        in_specs=[VMEM] * 6,
        out_specs=[VMEM] * 2,
    )(*[stay(array) for array in (partial, norm, solution, residual, direction, second_image)])
    return solution.T, residual.T


def solution(mesh):
    count = math.prod(mesh.shape[axis] for axis in AXES)
    rows = P(AXES, None)
    return jax.shard_map(
        functools.partial(body, count),
        mesh=mesh,
        in_specs=(rows, P(), P(), P(), rows, P(AXES)),
        out_specs=(rows, rows),
        check_vma=False,
    )
```

```python
import functools
import math

import jax
import jax.numpy as jnp
from jax import lax
from jax.experimental import pallas as pl
from jax.experimental.pallas import tpu as pltpu
from jax.sharding import PartitionSpec as P

AXES = ("row", "col")
LOG2E = 1.0 / math.log(2.0)
FAR = 64.0
KEEP_BYTES = 20 * 2**20
COPIES = 4
PIECES = 8
TAIL = 16
F32, BF16 = jnp.float32, jnp.bfloat16
VMEM = pl.BlockSpec(memory_space=pltpu.VMEM)


def stay(array):
    return pltpu.with_memory_space_constraint(array, pltpu.VMEM)


def swap(array, bit, count):
    return lax.ppermute(array, AXES, [(i, i ^ bit) for i in range(count)])


def two_parts(wide):
    high = wide.astype(BF16)
    return high, (wide - high.astype(F32)).astype(BF16)


def three_parts(wide):
    high, _ = two_parts(wide)
    return high, *two_parts(wide - high.astype(F32))


def features(parts, level, left):
    feat = parts.shape[0] // 2
    high, low = parts[:feat], parts[feat:]
    scaled = high.astype(F32) + low.astype(F32)
    half = -0.5 * jnp.sum(scaled * scaled, axis=0, keepdims=True)
    if not left:
        half = half + level
    halves = [part.astype(F32) for part in three_parts(half)]
    ones = [jnp.ones_like(half)] * 3
    tail = (halves + ones if left else ones + halves) + [jnp.zeros((10, half.shape[1]), F32)]
    rows = [high, high, low, low] if left else [high, low, high, low]
    return jnp.concatenate(rows + [jnp.concatenate(tail, axis=0).astype(BF16)], axis=0)


def feature_rows(feat):
    return 4 * feat + 16


def prepare_kernel(points_ref, inv_ref, right_ref, count_ref, sent_ref):
    feat, slots = points_ref.shape
    probes = right_ref.shape[0]
    valid = lax.broadcasted_iota(jnp.int32, (1, slots), 1) < count_ref[0]
    row = lax.broadcasted_iota(jnp.int32, (feat, slots), 0)
    inverse = jnp.zeros((feat, slots), F32)
    for f in range(feat):
        inverse = jnp.where(row == f, inv_ref[f], inverse)
    scaled = points_ref[...] * inverse * math.sqrt(LOG2E)
    high, low = two_parts(jnp.where(valid, scaled, FAR))
    direction, rest = two_parts(jnp.where(valid, right_ref[...], 0.0))
    sent_ref[0, :feat, :] = high
    sent_ref[0, feat : 2 * feat, :] = low
    sent_ref[0, 2 * feat : 2 * feat + probes, :] = direction
    sent_ref[0, 2 * feat + probes :, :] = rest


def prepare(points, inv_lengths, right_sides, block_counts):
    smem = pl.BlockSpec(memory_space=pltpu.SMEM)
    return pl.pallas_call(
        prepare_kernel,
        out_shape=pltpu.VMEM((1, 2 * points.shape[1] + 2 * right_sides.shape[1], points.shape[0]), BF16),
        in_specs=[VMEM, smem, VMEM, smem],
        out_specs=VMEM,
    )(points.T, inv_lengths, right_sides.T, block_counts)


def fill_right(near_ref, levels_ref, right_ref, feat):
    blocks, slots = right_ref.shape[1] // near_ref.shape[2], near_ref.shape[2]
    for b in range(blocks):
        right_ref[:, b * slots : (b + 1) * slots] = features(near_ref[b, : 2 * feat, :], levels_ref[0:1, :], False)


def entries(left, right):
    powers = lax.dot_general(left, right, (((0,), (0,)), ((), ())), preferred_element_type=F32)
    return jnp.exp2(powers).astype(BF16)


def apply_kernel(feat, group, keep, begin, last, count, near_ref, levels_ref, *refs):
    far, refs = refs[:count], refs[count:]
    if begin:
        right_ref, refs = refs[-4], refs[:-4] + refs[-3:]
    else:
        right_ref, so_far_ref, refs = refs[0], refs[1], refs[2:]
    kept, refs = (refs[:count], refs[count:]) if keep else ((), refs)
    own_ref = None
    if last:
        own_ref, refs = refs[1], refs[:1] + refs[2:]
    out_ref, left_ref, dirs_ref, sum_ref = refs
    slots, probes = near_ref.shape[2], dirs_ref.shape[0]
    if begin:
        fill_right(near_ref, levels_ref, right_ref, feat)
        sum_ref[...] = jnp.zeros_like(sum_ref)
    else:
        sum_ref[...] = so_far_ref[...]
    for piece, far_ref in enumerate(far):

        def step(g, carry, piece=piece, far_ref=far_ref):
            for b in range(group):
                place = slice(b * slots, (b + 1) * slots)
                left_ref[:, place] = features(far_ref[g * group + b, : 2 * feat, :], None, True)
                dirs_ref[:, place] = far_ref[g * group + b, 2 * feat :, :]
            block = entries(left_ref[...], right_ref[...])
            if keep:
                kept[piece][g] = block
            sum_ref[...] += jnp.dot(dirs_ref[...], block, preferred_element_type=F32)
            return carry

        lax.fori_loop(0, far_ref.shape[0] // group, step, 0)
    if not last:
        out_ref[...] = sum_ref[...]
        return
    images, rights = [], []
    norm = curve = jnp.zeros((probes, slots), F32)
    for b in range(near_ref.shape[0]):
        direction = near_ref[b, 2 * feat : 2 * feat + probes, :].astype(F32)
        right = direction + near_ref[b, 2 * feat + probes :, :].astype(F32)
        image = sum_ref[:, b * slots : (b + 1) * slots] + levels_ref[1:2, :] * direction
        norm = norm + right * right
        curve = curve + direction * image
        images.append(image)
        rights.append(right)
    own_ref[...] = images[0]
    norm, curve = (jnp.sum(each, axis=1, keepdims=True) for each in (norm, curve))
    usual = 1.0 / (jnp.exp2(levels_ref[0:1, :1]) + levels_ref[1:2, :1])
    likely = (norm > 0.0) & (curve > 1e-6 * norm)
    guess = jnp.where(likely, norm / jnp.where(likely, curve, 1.0), usual)
    guess = jnp.clip(guess, 1e-6, 1e3).astype(BF16)
    for b, (image, right) in enumerate(zip(images, rights)):
        out_ref[0, b * probes : (b + 1) * probes, :] = (right - guess.astype(F32) * image).astype(BF16)
    parts = [part.astype(F32) for part in (*three_parts(norm), *three_parts(curve), guess)]
    lane = lax.broadcasted_iota(jnp.int32, (probes, 128), 1)
    flat = jnp.zeros((probes, 128), F32)
    for at, part in enumerate(parts):
        flat = jnp.where(lane == at, part, flat)
    flat = jnp.concatenate([flat, jnp.zeros((128 - probes, 128), F32)], axis=0).T[:TAIL]
    flat = jnp.concatenate([flat, jnp.zeros((TAIL, slots - 128), F32)], axis=1)
    out_ref[0, len(images) * probes :, :] = flat.astype(BF16)


def apply_first(near, far, levels, so_far, feat, group, keep, last=False):
    copies, slots, probes = near.shape[0], near.shape[2], far[0].shape[1] - 2 * feat
    wide, steps, begin = group * slots, far[0].shape[0] // group, so_far is None
    outs = [pltpu.VMEM((probes, copies * slots), F32)]
    if last:
        outs = [pltpu.VMEM((1, copies * probes + TAIL, slots), BF16)]
        outs = outs + [pltpu.VMEM((probes, slots), F32)]
    if keep:
        outs = [pltpu.VMEM((steps, wide, copies * slots), BF16)] * len(far) + outs
    if begin:
        outs = outs + [pltpu.VMEM((feature_rows(feat), copies * slots), BF16)]
    arrays = [near, levels, *far, *([] if begin else so_far)]
    if keep:
        arrays = [stay(array) for array in arrays]
    done = pl.pallas_call(
        functools.partial(apply_kernel, feat, group, keep, begin, last, len(far)),
        out_shape=outs,
        in_specs=[VMEM] * len(arrays),
        out_specs=[VMEM] * len(outs),
        scratch_shapes=[
            pltpu.VMEM((feature_rows(feat), wide), BF16),
            pltpu.VMEM((probes, wide), BF16),
            pltpu.VMEM((probes, copies * slots), F32),
        ],
        compiler_params=pltpu.CompilerParams(vmem_limit_bytes=(16 if keep else 40) * 2**20),
        cost_estimate=pl.CostEstimate(
            flops=2 * copies * slots * len(far) * far[0].shape[0] * slots * 256,
            bytes_accessed=far[0].size * 4,
            transcendentals=0,
        ),
    )(*arrays)
    kept, rest = (done[: len(far)], done[len(far) :]) if keep else ([None] * len(far), done)
    if begin:
        return kept, (rest[1], rest[0])
    return kept, rest if last else (so_far[0], rest[0])


def second_kernel(feat, group, keep, copies, levels_ref, own_ref, own_image_in_ref, *refs):
    points, images, refs = refs[:PIECES], refs[PIECES : 2 * PIECES], refs[2 * PIECES :]
    if keep:
        kept, refs = refs[:PIECES], refs[PIECES:]
    (partial_ref, solution_ref, residual_ref, own_dir_ref, own_image_ref, norm_ref, product_ref, dirs_ref, scale_ref) = refs[:9]
    if not keep:
        right_ref, left_ref = refs[9:]
    slots, probes = images[0].shape[2], own_image_in_ref.shape[0]
    pairs = list(zip(points, images))
    groups = images[0].shape[0]

    def over_blocks(visit, start):
        carry = start
        for piece, (x_ref, _) in enumerate(pairs):
            blocks = x_ref.shape[0]
            carry = lax.fori_loop(0, blocks, functools.partial(visit, piece), carry, unroll=min(blocks, 8))
        return carry

    def column(wide):
        return jnp.sum(wide, axis=1, keepdims=True)

    per = 128 // TAIL
    tails = [(piece, g) for piece in range(PIECES) for g in range(groups)]
    norm_now = curve = jnp.zeros((probes, 1), F32)
    for start in range(0, len(tails), per):
        flat = [images[piece][g, copies * probes :, :128].astype(F32) for piece, g in tails[start : start + per]]
        flat = jnp.concatenate(flat + [jnp.zeros((TAIL, 128), F32)] * (per - len(flat)), axis=0).T[:probes]
        for at in range(min(per, len(tails) - start)):
            norm_now = norm_now + column(flat[:, TAIL * at : TAIL * at + 3])
            curve = curve + column(flat[:, TAIL * at + 3 : TAIL * at + 6])
            scale_ref[start + at] = jnp.broadcast_to(flat[:, TAIL * at + 6 : TAIL * at + 7], (probes, 128))
    step_size = norm_now / curve
    for start in range(len(tails)):
        scale_ref[start] = step_size / scale_ref[start]

    def residual_of(piece, b):
        first = points[piece][b, 2 * feat :, :].astype(F32)
        sent = images[piece][b // copies, pl.ds(pl.multiple_of(b % copies * probes, probes), probes), :].astype(F32)
        return first + scale_ref[piece * groups + b // copies][:, :1] * (sent - first), first

    def next_sum(piece, b, norm):
        residual, _ = residual_of(piece, b)
        return norm + residual * residual

    norm_next = column(over_blocks(next_sum, jnp.zeros((probes, slots), F32)))
    ratio = norm_next / norm_now

    def direct(piece, b):
        residual, first = residual_of(piece, b)
        return (residual + ratio * first).astype(BF16)

    first = own_ref[0, 2 * feat : 2 * feat + probes, :].astype(F32)
    right = first + own_ref[0, 2 * feat + probes :, :].astype(F32)
    residual = right - step_size * own_image_in_ref[...]
    own_direction = (residual + ratio * first).astype(BF16)
    solution_ref[...] = step_size * first
    residual_ref[...] = residual
    own_dir_ref[...] = own_direction.astype(F32)
    product_ref[...] = jnp.zeros_like(product_ref)
    if not keep:
        fill_right(points[0], levels_ref, right_ref, feat)
    for piece, (x_ref, _) in enumerate(pairs):

        def step(g, carry, piece=piece, x_ref=x_ref):
            for b in range(group):
                place = slice(b * slots, (b + 1) * slots)
                dirs_ref[:, place] = direct(piece, g * group + b)
            if piece == 0:

                @pl.when(g == 0)
                def own_block():
                    dirs_ref[:, :slots] = own_direction

            for b in range(group):
                place = slice(b * slots, (b + 1) * slots)
                if not keep:
                    left_ref[:, place] = features(x_ref[g * group + b, : 2 * feat, :], None, True)
            block = kept[piece][g] if keep else entries(left_ref[...], right_ref[...])
            product_ref[...] += jnp.dot(dirs_ref[...], block, preferred_element_type=F32)
            return carry

        lax.fori_loop(0, x_ref.shape[0] // group, step, 0)

    curve = jnp.zeros((probes, slots), F32)
    for b in range(copies):
        direction = (direct(0, b) if b else own_direction).astype(F32)
        image = product_ref[:, b * slots : (b + 1) * slots] + levels_ref[1:2, :] * direction
        curve = curve + direction * image
        if b == 0:
            own_image_ref[...] = image
    lane = lax.broadcasted_iota(jnp.int32, (probes, 128), 1)
    flat = jnp.where(lane == 0, column(curve), 0.0)
    partial_ref[...] = jnp.concatenate([flat, jnp.zeros((128 - probes, 128), F32)], axis=0).T[:8]
    norm_ref[...] = jnp.broadcast_to(norm_next, norm_ref.shape)


def second(levels, own, own_image, points, images, kept, copies, feat, group):
    keep = kept is not None
    slots, probes = own_image.shape[1], own_image.shape[0]
    one, small, wide = pltpu.VMEM((probes, slots), F32), pltpu.VMEM((probes, 128), F32), group * slots
    scratch = [
        pltpu.VMEM((probes, copies * slots), F32),
        pltpu.VMEM((probes, wide), BF16),
        pltpu.VMEM((PIECES * images[0].shape[0], probes, 128), F32),
    ]
    arrays = [levels, own, own_image, *points, *images, *(kept or ())]
    if keep:
        arrays = [stay(array) for array in arrays]
    else:
        scratch += [pltpu.VMEM((feature_rows(feat), copies * slots), BF16), pltpu.VMEM((feature_rows(feat), wide), BF16)]
    return pl.pallas_call(
        functools.partial(second_kernel, feat, group, keep, copies),
        out_shape=[pltpu.VMEM((8, 128), F32), one, one, one, one, small],
        in_specs=[VMEM] * len(arrays),
        out_specs=[VMEM] * 6,
        scratch_shapes=scratch,
        compiler_params=pltpu.CompilerParams(vmem_limit_bytes=(16 if keep else 48) * 2**20),
    )(*arrays)


def finish_kernel(curve_ref, norm_ref, solution_ref, residual_ref, direction_ref, image_ref, out_ref, left_ref):
    probes = norm_ref.shape[0]
    curve = jnp.concatenate([curve_ref[...], jnp.zeros((120, 128), F32)], axis=0).T[:probes, :1]
    step_size = norm_ref[:, :1] / curve
    out_ref[...] = solution_ref[...] + step_size * direction_ref[...]
    left_ref[...] = residual_ref[...] - step_size * image_ref[...]


def gather(held, bits, count):
    for at in range(0, len(bits), 2):
        pair = bits[at : at + 2]
        flips = pair if len(pair) == 1 else [pair[0], pair[1], sum(pair)]
        held = jnp.concatenate([held] + [swap(held, flip, count) for flip in flips], axis=0)
    return held


def total(held, bits, count):
    for at in range(0, len(bits), 2):
        pair = bits[at : at + 2]
        flips = pair if len(pair) == 1 else [pair[0], pair[1], sum(pair)]
        held = sum([swap(held, flip, count) for flip in flips], held)
    return held


def body(count, points, inv_lengths, signal_level, noise_level, right_sides, block_counts):
    slots, feat = points.shape
    probes = right_sides.shape[1]
    copies = COPIES
    while copies > 1 and (copies * PIECES > count or copies * count * slots * slots * 2 > KEEP_BYTES):
        copies //= 2
    keep = copies * count * slots * slots * 2 <= KEEP_BYTES
    group = math.gcd(count // PIECES, 8)
    bits = [1 << k for k in reversed(range(count.bit_length() - 1))]
    later = bits[copies.bit_length() - 1 :]
    one, two, core = bits[-3:]
    own = prepare(points, inv_lengths, right_sides, block_counts)
    own, signal_level, noise_level = lax.optimization_barrier((own, signal_level, noise_level))
    levels = jnp.stack([jnp.log(signal_level[0]) * LOG2E, noise_level[0]])
    levels = jnp.broadcast_to(levels[:, None], (2, slots))
    first = functools.partial(apply_first, feat=feat, group=group, keep=keep)

    held = gather(own, bits[:-3], count)
    held, levels = lax.optimization_barrier((held, levels))
    near = held[:copies]
    held = held[:, : 2 * feat + probes]
    beside, up, over = (swap(held, bit, count) for bit in (core, one, two))
    kept_0, product = first(near, [held, beside], levels, None)
    up, product = lax.optimization_barrier((up, product))
    corner, up_beside = swap(up, two, count), swap(up, core, count)
    kept_1, product = first(near, [up], levels, product)
    over, product = lax.optimization_barrier((over, product))
    over_beside = swap(over, core, count)
    kept_2, product = first(near, [up_beside, over], levels, product)
    corner, product = lax.optimization_barrier((corner, product))
    corner_beside = swap(corner, core, count)
    kept_3, product = first(near, [over_beside, corner], levels, product)
    kept_4, (image, own_image) = first(near, [corner_beside], levels, product, last=True)
    pieces = [held, beside, up, up_beside, over, over_beside, corner, corner_beside]
    kept = [*kept_0, *kept_1, *kept_2, *kept_3, *kept_4]

    held = gather(image, later[:-3], count)
    up, over, corner = (swap(held, bit, count) for bit in (one, two, one | two))
    beside, up_beside, over_beside, corner_beside = (swap(array, core, count) for array in (held, up, over, corner))
    images = [held, beside, up, up_beside, over, over_beside, corner, corner_beside]
    partial, solution, residual, direction, second_image, norm = second(
        levels, own, own_image, pieces, images, kept if keep else None, copies, feat, group
    )
    partial = total(partial + swap(partial, core, count), later[:-1][::-1], count)
    done = jax.ShapeDtypeStruct((probes, slots), F32)
    solution, residual = pl.pallas_call(
        finish_kernel,
        out_shape=[done, done],
        in_specs=[VMEM] * 6,
        out_specs=[VMEM] * 2,
    )(*[stay(array) for array in (partial, norm, solution, residual, direction, second_image)])
    return solution.T, residual.T


def solution(mesh):
    count = math.prod(mesh.shape[axis] for axis in AXES)
    rows = P(AXES, None)
    return jax.shard_map(
        functools.partial(body, count),
        mesh=mesh,
        in_specs=(rows, P(), P(), P(), rows, P(AXES)),
        out_specs=(rows, rows),
        check_vma=False,
    )
```

```python
import functools
import math

import jax
import jax.numpy as jnp
from jax import lax
from jax.experimental import pallas as pl
from jax.experimental.pallas import tpu as pltpu
from jax.sharding import PartitionSpec as P

AXES = ("row", "col")
LOG2E = 1.0 / math.log(2.0)
FAR = 64.0
KEEP_BYTES = 20 * 2**20
COPIES = 4
PIECES = 8
TAIL = 16
F32, BF16 = jnp.float32, jnp.bfloat16
VMEM = pl.BlockSpec(memory_space=pltpu.VMEM)


def stay(array):
    return pltpu.with_memory_space_constraint(array, pltpu.VMEM)


def swap(array, bit, count):
    return lax.ppermute(array, AXES, [(i, i ^ bit) for i in range(count)])


def two_parts(wide):
    high = wide.astype(BF16)
    return high, (wide - high.astype(F32)).astype(BF16)


def three_parts(wide):
    high, _ = two_parts(wide)
    return high, *two_parts(wide - high.astype(F32))


def features(parts, level, left):
    feat = parts.shape[0] // 2
    high, low = parts[:feat], parts[feat:]
    scaled = high.astype(F32) + low.astype(F32)
    half = -0.5 * jnp.sum(scaled * scaled, axis=0, keepdims=True)
    if not left:
        half = half + level
    halves = [part.astype(F32) for part in three_parts(half)]
    ones = [jnp.ones_like(half)] * 3
    tail = (halves + ones if left else ones + halves) + [jnp.zeros((10, half.shape[1]), F32)]
    rows = [high, high, low, low] if left else [high, low, high, low]
    return jnp.concatenate(rows + [jnp.concatenate(tail, axis=0).astype(BF16)], axis=0)


def feature_rows(feat):
    return 4 * feat + 16


def prepare_kernel(points_ref, inv_ref, right_ref, count_ref, sent_ref):
    feat, slots = points_ref.shape
    probes = right_ref.shape[0]
    valid = lax.broadcasted_iota(jnp.int32, (1, slots), 1) < count_ref[0]
    row = lax.broadcasted_iota(jnp.int32, (feat, slots), 0)
    inverse = jnp.zeros((feat, slots), F32)
    for f in range(feat):
        inverse = jnp.where(row == f, inv_ref[f], inverse)
    scaled = points_ref[...] * inverse * math.sqrt(LOG2E)
    high, low = two_parts(jnp.where(valid, scaled, FAR))
    direction, rest = two_parts(jnp.where(valid, right_ref[...], 0.0))
    sent_ref[0, :feat, :] = high
    sent_ref[0, feat : 2 * feat, :] = low
    sent_ref[0, 2 * feat : 2 * feat + probes, :] = direction
    sent_ref[0, 2 * feat + probes :, :] = rest


def prepare(points, inv_lengths, right_sides, block_counts):
    smem = pl.BlockSpec(memory_space=pltpu.SMEM)
    return pl.pallas_call(
        prepare_kernel,
        out_shape=pltpu.VMEM((1, 2 * points.shape[1] + 2 * right_sides.shape[1], points.shape[0]), BF16),
        in_specs=[VMEM, smem, VMEM, smem],
        out_specs=VMEM,
    )(points.T, inv_lengths, right_sides.T, block_counts)


def fill_right(near_ref, levels_ref, right_ref, feat):
    blocks, slots = right_ref.shape[1] // near_ref.shape[2], near_ref.shape[2]
    for b in range(blocks):
        right_ref[:, b * slots : (b + 1) * slots] = features(near_ref[b, : 2 * feat, :], levels_ref[0:1, :], False)


def turned(rows, height):
    if rows.shape[0] < height:
        rows = jnp.concatenate([rows, jnp.zeros((height - rows.shape[0], rows.shape[1]), F32)], axis=0)
    return rows.T


def entries(left, right):
    powers = lax.dot_general(left, right, (((0,), (0,)), ((), ())), preferred_element_type=F32)
    return jnp.exp2(powers).astype(BF16)


def apply_kernel(feat, group, keep, begin, last, count, near_ref, levels_ref, *refs):
    far, refs = refs[:count], refs[count:]
    if begin:
        right_ref, refs = refs[-2], refs[:-2] + refs[-1:]
    else:
        right_ref, so_far_ref, refs = refs[0], refs[1], refs[2:]
    kept, refs = (refs[:count], refs[count:]) if keep else ((), refs)
    own_ref = None
    if last:
        own_ref, refs = refs[1], refs[:1] + refs[2:]
    out_ref, sum_ref = refs
    slots, probes = near_ref.shape[2], sum_ref.shape[0]
    if begin:
        fill_right(near_ref, levels_ref, right_ref, feat)
        product = jnp.zeros(sum_ref.shape, F32)
    else:
        product = so_far_ref[...]

    def step(piece, g):
        blocks = [far[piece][g * group + b] for b in range(group)]
        left = jnp.concatenate([features(block[: 2 * feat], None, True) for block in blocks], axis=1)
        directions = jnp.concatenate([block[2 * feat :] for block in blocks], axis=1)
        block = entries(left, right_ref[...])
        if keep:
            kept[piece][g] = block
        return jnp.dot(directions, block, preferred_element_type=F32)

    steps = far[0].shape[0] // group
    if steps == 1:
        for piece in range(count):
            product = product + step(piece, 0)
    else:
        sum_ref[...] = product

        def add(piece, g, carry):
            sum_ref[...] += step(piece, g)
            return carry

        for piece in range(count):
            lax.fori_loop(0, steps, functools.partial(add, piece), 0)
        product = sum_ref[...]
    if not last:
        out_ref[...] = product
        return
    images, rights = [], []
    norm = curve = jnp.zeros((probes, slots), F32)
    for b in range(near_ref.shape[0]):
        direction = near_ref[b, 2 * feat : 2 * feat + probes, :].astype(F32)
        right = direction + near_ref[b, 2 * feat + probes :, :].astype(F32)
        image = product[:, b * slots : (b + 1) * slots] + levels_ref[1:2, :] * direction
        norm = norm + right * right
        curve = curve + direction * image
        images.append(image)
        rights.append(right)
    own_ref[...] = images[0]
    norm, curve = (jnp.sum(each, axis=1, keepdims=True) for each in (norm, curve))
    usual = 1.0 / (jnp.exp2(levels_ref[0:1, :1]) + levels_ref[1:2, :1])
    likely = (norm > 0.0) & (curve > 1e-6 * norm)
    guess = jnp.where(likely, norm / jnp.where(likely, curve, 1.0), usual)
    guess = jnp.clip(guess, 1e-6, 1e3).astype(BF16)
    steps = [right - guess.astype(F32) * image for image, right in zip(images, rights)]
    for b, after in enumerate(steps):
        out_ref[0, b * probes : (b + 1) * probes, :] = after.astype(BF16)
    products = [[x * y for x, y in zip(*pair)] for pair in ((steps, steps), (steps, images), (images, images))]
    sums = [norm, curve] + [jnp.sum(sum(each), axis=1, keepdims=True) for each in products]
    lane = lax.broadcasted_iota(jnp.int32, (probes, 128), 1)
    flat = jnp.zeros((probes, 128), F32)
    for at, each in enumerate([*sums, guess.astype(F32)]):
        flat = jnp.where(lane == at, each, flat)
    high, middle, low = (part.astype(F32) for part in three_parts(turned(flat, 128)[:8]))
    rows = jnp.concatenate([jnp.concatenate([high, middle], axis=1), jnp.concatenate([low, jnp.zeros_like(low)], axis=1)])
    if slots > 256:
        rows = jnp.concatenate([rows, jnp.zeros((TAIL, slots - 256), F32)], axis=1)
    out_ref[0, len(images) * probes :, :] = rows.astype(BF16)


def apply_first(near, far, levels, so_far, feat, group, keep, last=False):
    copies, slots, probes = near.shape[0], near.shape[2], far[0].shape[1] - 2 * feat
    wide, steps, begin = group * slots, far[0].shape[0] // group, so_far is None
    outs = [pltpu.VMEM((probes, copies * slots), F32)]
    if last:
        outs = [pltpu.VMEM((1, copies * probes + TAIL, slots), BF16)]
        outs = outs + [pltpu.VMEM((probes, slots), F32)]
    if keep:
        outs = [pltpu.VMEM((steps, wide, copies * slots), BF16)] * len(far) + outs
    if begin:
        outs = outs + [pltpu.VMEM((feature_rows(feat), copies * slots), BF16)]
    arrays = [near, levels, *far, *([] if begin else so_far)]
    if keep:
        arrays = [stay(array) for array in arrays]
    done = pl.pallas_call(
        functools.partial(apply_kernel, feat, group, keep, begin, last, len(far)),
        out_shape=outs,
        in_specs=[VMEM] * len(arrays),
        out_specs=[VMEM] * len(outs),
        scratch_shapes=[pltpu.VMEM((probes, copies * slots), F32)],
        compiler_params=pltpu.CompilerParams(vmem_limit_bytes=(16 if keep else 40) * 2**20),
        cost_estimate=pl.CostEstimate(
            flops=2 * copies * slots * len(far) * far[0].shape[0] * slots * 256,
            bytes_accessed=far[0].size * 4,
            transcendentals=0,
        ),
    )(*arrays)
    kept, rest = (done[: len(far)], done[len(far) :]) if keep else ([None] * len(far), done)
    if begin:
        return kept, (rest[1], rest[0])
    return kept, rest if last else (so_far[0], rest[0])


def second_kernel(feat, group, keep, copies, levels_ref, own_ref, own_image_in_ref, *refs):
    points, images, refs = refs[:PIECES], refs[PIECES : 2 * PIECES], refs[2 * PIECES :]
    if keep:
        kept, refs = refs[:PIECES], refs[PIECES:]
    (partial_ref, solution_ref, residual_ref, own_dir_ref, own_image_ref, norm_ref, product_ref, scale_ref) = refs[:8]
    if not keep:
        right_ref = refs[8]
    slots, probes = images[0].shape[2], own_image_in_ref.shape[0]
    pairs = list(zip(points, images))
    groups = images[0].shape[0]

    def column(wide):
        return jnp.sum(wide, axis=1, keepdims=True)

    tails = []
    for w_ref in images:
        for g in range(groups):
            parts = w_ref[g, copies * probes :, :].astype(F32)
            tails.append(parts[:8, :128] + parts[:8, 128:256] + parts[8:, :128])
    norm_now, curve = (sum(tail[at : at + 1] for tail in tails) for at in range(2))
    step_size = norm_now / curve
    norm_next = jnp.zeros_like(norm_now)
    guesses = [tail[5:6] for tail in tails]
    for tail, guess in zip(tails, guesses):
        apart = guess - step_size
        norm_next = norm_next + (tail[2:3] + apart * (2.0 * tail[3:4] + apart * tail[4:5]))
    few = jnp.concatenate([step_size, norm_next / norm_now, norm_next, jnp.zeros((5, 128), F32)], axis=0)
    for start in range(0, len(guesses), 120):
        some = guesses[start : start + 120]
        columns = turned(jnp.concatenate([few] + [step_size / guess for guess in some], axis=0), 128)[:probes]
        for at in range(len(some)):
            scale_ref[start + at] = jnp.broadcast_to(columns[:, at + 8 : at + 9], (probes, 128))
    step_size, ratio, norm_next = (columns[:, at : at + 1] for at in range(3))

    def residual_of(piece, b):
        first = points[piece][b, 2 * feat :, :].astype(F32)
        sent = images[piece][b // copies, pl.ds(pl.multiple_of(b % copies * probes, probes), probes), :].astype(F32)
        return first + scale_ref[piece * groups + b // copies][:, :1] * (sent - first), first

    def direct(piece, b):
        residual, first = residual_of(piece, b)
        return (residual + ratio * first).astype(BF16)

    first = own_ref[0, 2 * feat : 2 * feat + probes, :].astype(F32)
    right = first + own_ref[0, 2 * feat + probes :, :].astype(F32)
    residual = right - step_size * own_image_in_ref[...]
    own_direction = (residual + ratio * first).astype(BF16)
    solution_ref[...] = step_size * first
    residual_ref[...] = residual
    own_dir_ref[...] = own_direction.astype(F32)
    if not keep:
        fill_right(points[0], levels_ref, right_ref, feat)

    def step(piece, g):
        directions = [direct(piece, g * group + b) for b in range(group)]
        if piece == 0:
            directions[0] = jnp.where(g == 0, own_direction, directions[0])
        if keep:
            block = kept[piece][g]
        else:
            blocks = [points[piece][g * group + b, : 2 * feat, :] for b in range(group)]
            left = jnp.concatenate([features(block, None, True) for block in blocks], axis=1)
            block = entries(left, right_ref[...])
        return jnp.dot(jnp.concatenate(directions, axis=1), block, preferred_element_type=F32)

    steps = points[0].shape[0] // group
    if steps == 1:
        product = sum(step(piece, 0) for piece in range(PIECES))
    else:
        product_ref[...] = jnp.zeros_like(product_ref)

        def add(piece, g, carry):
            product_ref[...] += step(piece, g)
            return carry

        for piece in range(PIECES):
            lax.fori_loop(0, steps, functools.partial(add, piece), 0)
        product = product_ref[...]

    curve = jnp.zeros((probes, slots), F32)
    for b in range(copies):
        direction = (direct(0, b) if b else own_direction).astype(F32)
        image = product[:, b * slots : (b + 1) * slots] + levels_ref[1:2, :] * direction
        curve = curve + direction * image
        if b == 0:
            own_image_ref[...] = image
    lane = lax.broadcasted_iota(jnp.int32, (probes, 128), 1)
    flat = jnp.where(lane == 0, column(curve), 0.0)
    partial_ref[...] = turned(flat, 128)[:8]
    norm_ref[...] = jnp.broadcast_to(norm_next, norm_ref.shape)


def second(levels, own, own_image, points, images, kept, copies, feat, group):
    keep = kept is not None
    slots, probes = own_image.shape[1], own_image.shape[0]
    one, small = pltpu.VMEM((probes, slots), F32), pltpu.VMEM((probes, 128), F32)
    scratch = [
        pltpu.VMEM((probes, copies * slots), F32),
        pltpu.VMEM((PIECES * images[0].shape[0], probes, 128), F32),
    ]
    arrays = [levels, own, own_image, *points, *images, *(kept or ())]
    if keep:
        arrays = [stay(array) for array in arrays]
    else:
        scratch.append(pltpu.VMEM((feature_rows(feat), copies * slots), BF16))
    return pl.pallas_call(
        functools.partial(second_kernel, feat, group, keep, copies),
        out_shape=[pltpu.VMEM((8, 128), F32), one, one, one, one, small],
        in_specs=[VMEM] * len(arrays),
        out_specs=[VMEM] * 6,
        scratch_shapes=scratch,
        compiler_params=pltpu.CompilerParams(vmem_limit_bytes=(16 if keep else 48) * 2**20),
    )(*arrays)


def finish_kernel(curve_ref, norm_ref, solution_ref, residual_ref, direction_ref, image_ref, out_ref, left_ref):
    probes = norm_ref.shape[0]
    curve = turned(curve_ref[...], 128)[:probes, :1]
    step_size = norm_ref[:, :1] / curve
    out_ref[...] = solution_ref[...] + step_size * direction_ref[...]
    left_ref[...] = residual_ref[...] - step_size * image_ref[...]


def gather(held, bits, count):
    for at in range(0, len(bits), 2):
        pair = bits[at : at + 2]
        flips = pair if len(pair) == 1 else [pair[0], pair[1], sum(pair)]
        held = jnp.concatenate([held] + [swap(held, flip, count) for flip in flips], axis=0)
    return held


def total(held, bits, count):
    for at in range(0, len(bits), 2):
        pair = bits[at : at + 2]
        flips = pair if len(pair) == 1 else [pair[0], pair[1], sum(pair)]
        held = sum([swap(held, flip, count) for flip in flips], held)
    return held


def body(count, points, inv_lengths, signal_level, noise_level, right_sides, block_counts):
    slots, feat = points.shape
    probes = right_sides.shape[1]
    copies = COPIES
    while copies > 1 and (copies * PIECES > count or copies * count * slots * slots * 2 > KEEP_BYTES):
        copies //= 2
    keep = copies * count * slots * slots * 2 <= KEEP_BYTES
    group = math.gcd(count // PIECES, 8)
    bits = [1 << k for k in reversed(range(count.bit_length() - 1))]
    later = bits[copies.bit_length() - 1 :]
    one, two, core = bits[-3:]
    own = prepare(points, inv_lengths, right_sides, block_counts)
    own, signal_level, noise_level = lax.optimization_barrier((own, signal_level, noise_level))
    levels = jnp.stack([jnp.log(signal_level[0]) * LOG2E, noise_level[0]])
    levels = jnp.broadcast_to(levels[:, None], (2, slots))
    first = functools.partial(apply_first, feat=feat, group=group, keep=keep)

    held = gather(own, bits[:-3], count)
    held, levels = lax.optimization_barrier((held, levels))
    near = held[:copies]
    held = held[:, : 2 * feat + probes]
    beside, up, over = (swap(held, bit, count) for bit in (core, one, two))
    kept_0, product = first(near, [held, beside], levels, None)
    up, product = lax.optimization_barrier((up, product))
    corner = swap(up, two, count)
    up_beside = swap(up, core, count)
    kept_1, product = first(near, [up], levels, product)
    over_beside = swap(over, core, count)
    kept_2, product = first(near, [up_beside, over], levels, product)
    kept_3, product = first(near, [over_beside], levels, product)
    corner, product = lax.optimization_barrier((corner, product))
    corner_beside = swap(corner, core, count)
    kept_4, product = first(near, [corner], levels, product)
    kept_5, (image, own_image) = first(near, [corner_beside], levels, product, last=True)
    pieces = [held, beside, up, up_beside, over, over_beside, corner, corner_beside]
    kept = [*kept_0, *kept_1, *kept_2, *kept_3, *kept_4, *kept_5]

    held = gather(image, later[:-3], count)
    up, over, corner = (swap(held, bit, count) for bit in (one, two, one | two))
    beside, up_beside, over_beside, corner_beside = (swap(array, core, count) for array in (held, up, over, corner))
    images = [held, beside, up, up_beside, over, over_beside, corner, corner_beside]
    partial, solution, residual, direction, second_image, norm = second(
        levels, own, own_image, pieces, images, kept if keep else None, copies, feat, group
    )
    partial = total(partial + swap(partial, core, count), later[:-1][::-1], count)
    done = jax.ShapeDtypeStruct((probes, slots), F32)
    solution, residual = pl.pallas_call(
        finish_kernel,
        out_shape=[done, done],
        in_specs=[VMEM] * 6,
        out_specs=[VMEM] * 2,
    )(*[stay(array) for array in (partial, norm, solution, residual, direction, second_image)])
    return solution.T, residual.T


def solution(mesh):
    count = math.prod(mesh.shape[axis] for axis in AXES)
    rows = P(AXES, None)
    return jax.shard_map(
        functools.partial(body, count),
        mesh=mesh,
        in_specs=(rows, P(), P(), P(), rows, P(AXES)),
        out_specs=(rows, rows),
        check_vma=False,
    )
```

```python
import functools
import math

import jax
import jax.numpy as jnp
from jax import lax
from jax.experimental import pallas as pl
from jax.experimental.pallas import tpu as pltpu
from jax.sharding import PartitionSpec as P

AXES = ("row", "col")
LOG2E = 1.0 / math.log(2.0)
FAR = 64.0
KEEP_BYTES = 20 * 2**20
COPIES = 4
PIECES = 8
TAIL = 16
LATE = 2
F32, BF16 = jnp.float32, jnp.bfloat16
VMEM = pl.BlockSpec(memory_space=pltpu.VMEM)


def stay(array):
    return pltpu.with_memory_space_constraint(array, pltpu.VMEM)


def swap(array, bit, count):
    return lax.ppermute(array, AXES, [(i, i ^ bit) for i in range(count)])


def two_parts(wide):
    high = wide.astype(BF16)
    return high, (wide - high.astype(F32)).astype(BF16)


def swap_apart(array, bits, count):
    one, two, core = bits
    return lax.ppermute(array, AXES, [(i, i ^ (one | two if i & core else one)) for i in range(count)])


def three_parts(wide):
    high, _ = two_parts(wide)
    return high, *two_parts(wide - high.astype(F32))


def features(parts, level, left):
    feat = parts.shape[0] // 2
    high, low = parts[:feat], parts[feat:]
    scaled = high.astype(F32) + low.astype(F32)
    half = -0.5 * jnp.sum(scaled * scaled, axis=0, keepdims=True)
    if not left:
        half = half + level
    halves = [part.astype(F32) for part in three_parts(half)]
    ones = [jnp.ones_like(half)] * 3
    tail = (halves + ones if left else ones + halves) + [jnp.zeros((10, half.shape[1]), F32)]
    rows = [high, high, low, low] if left else [high, low, high, low]
    return jnp.concatenate(rows + [jnp.concatenate(tail, axis=0).astype(BF16)], axis=0)


def feature_rows(feat):
    return 4 * feat + 16


def prepare_kernel(points_ref, inv_ref, right_ref, count_ref, sent_ref):
    feat, slots = points_ref.shape
    probes = right_ref.shape[0]
    valid = lax.broadcasted_iota(jnp.int32, (1, slots), 1) < count_ref[0]
    row = lax.broadcasted_iota(jnp.int32, (feat, slots), 0)
    inverse = jnp.zeros((feat, slots), F32)
    for f in range(feat):
        inverse = jnp.where(row == f, inv_ref[f], inverse)
    scaled = points_ref[...] * inverse * math.sqrt(LOG2E)
    high, low = two_parts(jnp.where(valid, scaled, FAR))
    direction, rest = two_parts(jnp.where(valid, right_ref[...], 0.0))
    sent_ref[0, :feat, :] = high
    sent_ref[0, feat : 2 * feat, :] = low
    sent_ref[0, 2 * feat : 2 * feat + probes, :] = direction
    sent_ref[0, 2 * feat + probes :, :] = rest


def prepare(points, inv_lengths, right_sides, block_counts):
    smem = pl.BlockSpec(memory_space=pltpu.SMEM)
    return pl.pallas_call(
        prepare_kernel,
        out_shape=pltpu.VMEM((1, 2 * points.shape[1] + 2 * right_sides.shape[1], points.shape[0]), BF16),
        in_specs=[VMEM, smem, VMEM, smem],
        out_specs=VMEM,
    )(points.T, inv_lengths, right_sides.T, block_counts)


def fill_right(near_ref, levels_ref, right_ref, feat):
    blocks, slots = right_ref.shape[1] // near_ref.shape[2], near_ref.shape[2]
    for b in range(blocks):
        right_ref[:, b * slots : (b + 1) * slots] = features(near_ref[b, : 2 * feat, :], levels_ref[0:1, :], False)


def turned(rows, height):
    if rows.shape[0] < height:
        rows = jnp.concatenate([rows, jnp.zeros((height - rows.shape[0], rows.shape[1]), F32)], axis=0)
    return rows.T


def entries(left, right):
    powers = lax.dot_general(left, right, (((0,), (0,)), ((), ())), preferred_element_type=F32)
    return jnp.exp2(powers).astype(BF16)


def apply_kernel(feat, group, keep, begin, last, count, earlier, near_ref, levels_ref, *refs):
    far, refs = refs[:count], refs[count:]
    if begin:
        right_ref, refs = refs[-2], refs[:-2] + refs[-1:]
        fill_right(near_ref, levels_ref, right_ref, feat)
    else:
        right_ref, refs = refs[0], refs[1:]
    sum_ref, refs = refs[-1], refs[:-1]
    before, refs = refs[:earlier], refs[earlier:]
    kept, refs = (refs[:count], refs[count:]) if keep else ((), refs)
    products, refs = refs[: count if keep else 1 - last], refs[count if keep else 1 - last :]
    slots, probes = near_ref.shape[2], sum_ref.shape[0]

    def step(piece, g):
        blocks = [far[piece][g * group + b] for b in range(group)]
        left = jnp.concatenate([features(block[: 2 * feat], None, True) for block in blocks], axis=1)
        directions = jnp.concatenate([block[2 * feat :] for block in blocks], axis=1)
        block = entries(left, right_ref[...])
        if keep:
            kept[piece][g] = block
        return jnp.dot(directions, block, preferred_element_type=F32)

    steps = far[0].shape[0] // group
    if keep:
        done = [step(piece, 0) for piece in range(count)]
        for product_ref, product in zip(products, done):
            product_ref[...] = product
        if not last:
            return
        product = sum([before_ref[...] for before_ref in before], sum(done))
    else:
        sum_ref[...] = sum([before_ref[...] for before_ref in before], jnp.zeros(sum_ref.shape, F32))

        def add(piece, g, carry):
            sum_ref[...] += step(piece, g)
            return carry

        for piece in range(count):
            lax.fori_loop(0, steps, functools.partial(add, piece), 0)
        product = sum_ref[...]
        if not last:
            products[0][...] = product
            return
    out_ref, own_ref = refs
    images, rights = [], []
    norm = curve = jnp.zeros((probes, slots), F32)
    for b in range(near_ref.shape[0]):
        direction = near_ref[b, 2 * feat : 2 * feat + probes, :].astype(F32)
        right = direction + near_ref[b, 2 * feat + probes :, :].astype(F32)
        image = product[:, b * slots : (b + 1) * slots] + levels_ref[1:2, :] * direction
        norm = norm + right * right
        curve = curve + direction * image
        images.append(image)
        rights.append(right)
    own_ref[...] = images[0]
    norm, curve = (jnp.sum(each, axis=1, keepdims=True) for each in (norm, curve))
    usual = 1.0 / (jnp.exp2(levels_ref[0:1, :1]) + levels_ref[1:2, :1])
    likely = (norm > 0.0) & (curve > 1e-6 * norm)
    guess = jnp.where(likely, norm / jnp.where(likely, curve, 1.0), usual)
    guess = jnp.clip(guess, 1e-6, 1e3).astype(BF16)
    steps = [right - guess.astype(F32) * image for image, right in zip(images, rights)]
    for b, after in enumerate(steps):
        out_ref[0, b * probes : (b + 1) * probes, :] = after.astype(BF16)
    products = [[x * y for x, y in zip(*pair)] for pair in ((steps, steps), (steps, images), (images, images))]
    sums = [norm, curve] + [jnp.sum(sum(each), axis=1, keepdims=True) for each in products]
    lane = lax.broadcasted_iota(jnp.int32, (probes, 128), 1)
    flat = jnp.zeros((probes, 128), F32)
    for at, each in enumerate([*sums, guess.astype(F32)]):
        flat = jnp.where(lane == at, each, flat)
    high, middle, low = (part.astype(F32) for part in three_parts(turned(flat, 128)[:8]))
    rows = jnp.concatenate([jnp.concatenate([high, middle], axis=1), jnp.concatenate([low, jnp.zeros_like(low)], axis=1)])
    if slots > 256:
        rows = jnp.concatenate([rows, jnp.zeros((TAIL, slots - 256), F32)], axis=1)
    out_ref[0, len(images) * probes :, :] = rows.astype(BF16)


def apply_first(near, far, levels, right, products, feat, group, keep, last=False):
    copies, slots, probes = near.shape[0], near.shape[2], far[0].shape[1] - 2 * feat
    wide, steps, begin = group * slots, far[0].shape[0] // group, right is None
    product = pltpu.VMEM((probes, copies * slots), F32)
    outs = [product] * (len(far) if keep else 1 - last)
    if keep:
        outs = [pltpu.VMEM((steps, wide, copies * slots), BF16)] * len(far) + outs
    if last:
        outs = outs + [pltpu.VMEM((1, copies * probes + TAIL, slots), BF16), pltpu.VMEM((probes, slots), F32)]
    if begin:
        outs = outs + [pltpu.VMEM((feature_rows(feat), copies * slots), BF16)]
    before = products if last or not keep else products[-1:]
    arrays = [near, levels, *far, *([] if begin else [right]), *before]
    if keep:
        arrays = [stay(array) for array in arrays]
    done = pl.pallas_call(
        functools.partial(apply_kernel, feat, group, keep, begin, last, len(far), len(before)),
        out_shape=outs,
        in_specs=[VMEM] * len(arrays),
        out_specs=[VMEM] * len(outs),
        scratch_shapes=[pltpu.VMEM((probes, copies * slots), F32)],
        compiler_params=pltpu.CompilerParams(vmem_limit_bytes=(16 if keep else 40) * 2**20),
    )(*arrays)
    done = list(done)
    kept, done = (done[: len(far)], done[len(far) :]) if keep else ([None] * len(far), done)
    parts = len(far) if keep else 1 - last
    products = products + done[:parts] if keep else done[:parts]
    return kept, products, done[parts:] if last else done[parts] if begin else right


def step_sums(images, copies, probes):
    tails = []
    for w_ref in images:
        for g in range(w_ref.shape[0]):
            parts = w_ref[g, copies * probes :, :].astype(F32)
            tails.append(parts[:8, :128] + parts[:8, 128:256] + parts[8:, :128])
    norm_now, curve = (sum(tail[at : at + 1] for tail in tails) for at in range(2))
    step_size = norm_now / curve
    norm_next = jnp.zeros_like(norm_now)
    guesses = [tail[5:6] for tail in tails]
    for tail, guess in zip(tails, guesses):
        apart = guess - step_size
        norm_next = norm_next + (tail[2:3] + apart * (2.0 * tail[3:4] + apart * tail[4:5]))
    few = jnp.concatenate([step_size, norm_next / norm_now, norm_next, jnp.zeros((5, 128), F32)], axis=0)
    scales = []
    for start in range(0, len(guesses), 120):
        some = guesses[start : start + 120]
        columns = turned(jnp.concatenate([few] + [step_size / guess for guess in some], axis=0), 128)[:probes]
        scales += [columns[:, at + 8 : at + 9] for at in range(len(some))]
    return *(columns[:, at : at + 1] for at in range(3)), scales


def second_kernel(feat, group, keep, copies, levels_ref, own_ref, own_image_in_ref, *refs):
    points, images, refs = refs[:PIECES], refs[PIECES : 2 * PIECES], refs[2 * PIECES :]
    if keep:
        kept, refs = refs[:PIECES], refs[PIECES:]
    (partial_ref, solution_ref, residual_ref, own_dir_ref, own_image_ref, norm_ref, product_ref, scale_ref) = refs[:8]
    if not keep:
        right_ref = refs[8]
    slots, probes = images[0].shape[2], own_image_in_ref.shape[0]
    pairs = list(zip(points, images))
    groups = images[0].shape[0]

    def column(wide):
        return jnp.sum(wide, axis=1, keepdims=True)

    step_size, ratio, norm_next, scales = step_sums(images, copies, probes)
    for at, scale in enumerate(scales):
        scale_ref[at] = jnp.broadcast_to(scale, (probes, 128))

    def residual_of(piece, b):
        first = points[piece][b, 2 * feat :, :].astype(F32)
        sent = images[piece][b // copies, pl.ds(pl.multiple_of(b % copies * probes, probes), probes), :].astype(F32)
        return first + scale_ref[piece * groups + b // copies][:, :1] * (sent - first), first

    def direct(piece, b):
        residual, first = residual_of(piece, b)
        return (residual + ratio * first).astype(BF16)

    first = own_ref[0, 2 * feat : 2 * feat + probes, :].astype(F32)
    right = first + own_ref[0, 2 * feat + probes :, :].astype(F32)
    residual = right - step_size * own_image_in_ref[...]
    own_direction = (residual + ratio * first).astype(BF16)
    solution_ref[...] = step_size * first
    residual_ref[...] = residual
    own_dir_ref[...] = own_direction.astype(F32)
    if not keep:
        fill_right(points[0], levels_ref, right_ref, feat)

    def step(piece, g):
        directions = [direct(piece, g * group + b) for b in range(group)]
        if piece == 0:
            directions[0] = jnp.where(g == 0, own_direction, directions[0])
        if keep:
            block = kept[piece][g]
        else:
            blocks = [points[piece][g * group + b, : 2 * feat, :] for b in range(group)]
            left = jnp.concatenate([features(block, None, True) for block in blocks], axis=1)
            block = entries(left, right_ref[...])
        return jnp.dot(jnp.concatenate(directions, axis=1), block, preferred_element_type=F32)

    steps = points[0].shape[0] // group
    if steps == 1:
        product = sum(step(piece, 0) for piece in range(PIECES))
    else:
        product_ref[...] = jnp.zeros_like(product_ref)

        def add(piece, g, carry):
            product_ref[...] += step(piece, g)
            return carry

        for piece in range(PIECES):
            lax.fori_loop(0, steps, functools.partial(add, piece), 0)
        product = product_ref[...]

    curve = jnp.zeros((probes, slots), F32)
    for b in range(copies):
        direction = (direct(0, b) if b else own_direction).astype(F32)
        image = product[:, b * slots : (b + 1) * slots] + levels_ref[1:2, :] * direction
        curve = curve + direction * image
        if b == 0:
            own_image_ref[...] = image
    lane = lax.broadcasted_iota(jnp.int32, (probes, 128), 1)
    flat = jnp.where(lane == 0, column(curve), 0.0)
    partial_ref[...] = turned(flat, 128)[:8]
    norm_ref[...] = jnp.broadcast_to(norm_next, norm_ref.shape)


def sent_product(sent_ref, kept_ref, copies):
    probes = (sent_ref.shape[1] - TAIL) // copies
    sent = jnp.concatenate([sent_ref[0, b * probes : (b + 1) * probes, :] for b in range(copies)], axis=1)
    return jnp.dot(sent, kept_ref[0], preferred_element_type=F32)


def again_kernel(copies, count, *refs):
    for sent_ref, kept_ref, out_ref in zip(refs[:count], refs[count : 2 * count], refs[2 * count :]):
        out_ref[...] = sent_product(sent_ref, kept_ref, copies)


def apply_again(sent, kept, copies):
    outs = [pltpu.VMEM(((sent[0].shape[1] - TAIL) // copies, kept[0].shape[2]), F32)] * len(sent)
    done = pl.pallas_call(
        functools.partial(again_kernel, copies, len(sent)),
        out_shape=outs,
        in_specs=[VMEM] * (2 * len(sent)),
        out_specs=[VMEM] * len(sent),
        compiler_params=pltpu.CompilerParams(vmem_limit_bytes=16 * 2**20),
    )(*[stay(array) for array in (*sent, *kept)])
    return list(done)


def combine_kernel(feat, copies, levels_ref, own_ref, own_image_in_ref, near_ref, kept_near_ref, *refs):
    images, firsts, refs = refs[:PIECES], refs[PIECES : 2 * PIECES], refs[2 * PIECES :]
    late = LATE
    agains, kept, outs = refs[: PIECES - late], refs[PIECES - late : PIECES], refs[PIECES:]
    partial_ref, solution_ref, residual_ref, own_dir_ref, own_image_ref, norm_ref = outs
    slots, probes = images[0].shape[2], own_image_in_ref.shape[0]
    agains = [again_ref[...] for again_ref in agains]
    for image_ref, kept_ref in zip(images[PIECES - late :], kept):
        agains.append(sent_product(image_ref, kept_ref, copies))
    step_size, ratio, norm_next, scales = step_sums(images, copies, probes)
    product = jnp.zeros((probes, copies * slots), F32)
    for first_ref, again, scale in zip(firsts, agains, scales):
        product = product + ((1.0 - scale + ratio) * first_ref[...] + scale * again)

    first = own_ref[0, 2 * feat : 2 * feat + probes, :].astype(F32)
    right = first + own_ref[0, 2 * feat + probes :, :].astype(F32)
    residual = right - step_size * own_image_in_ref[...]
    directions = [(residual + ratio * first).astype(BF16).astype(F32)]
    solution_ref[...] = step_size * first
    residual_ref[...] = residual
    own_dir_ref[...] = directions[0]
    for b in range(copies):
        first = near_ref[b, 2 * feat :, :].astype(F32)
        sent = images[0][0, b * probes : (b + 1) * probes, :].astype(F32)
        directions.append((1.0 - scales[0] + ratio) * first + scales[0] * sent)
    exact, formed = directions[:2]
    product = product + jnp.dot((exact - formed).astype(BF16), kept_near_ref[0, :slots, :], preferred_element_type=F32)
    curve = jnp.zeros((probes, slots), F32)
    for b, direction in enumerate([exact] + directions[2:]):
        image = product[:, b * slots : (b + 1) * slots] + levels_ref[1:2, :] * direction
        curve = curve + direction * image
        if b == 0:
            own_image_ref[...] = image
    lane = lax.broadcasted_iota(jnp.int32, (probes, 128), 1)
    flat = jnp.where(lane == 0, jnp.sum(curve, axis=1, keepdims=True), 0.0)
    partial_ref[...] = turned(flat, 128)[:8]
    norm_ref[...] = jnp.broadcast_to(norm_next, norm_ref.shape)


def combine(levels, own, own_image, near, images, products, agains, kept, copies, feat):
    probes, slots = own_image.shape
    one, small = pltpu.VMEM((probes, slots), F32), pltpu.VMEM((probes, 128), F32)
    arrays = [levels, own, own_image, near, kept[0], *images, *products, *agains, *kept[len(agains) :]]
    return pl.pallas_call(
        functools.partial(combine_kernel, feat, copies),
        out_shape=[pltpu.VMEM((8, 128), F32), one, one, one, one, small],
        in_specs=[VMEM] * len(arrays),
        out_specs=[VMEM] * 6,
        compiler_params=pltpu.CompilerParams(vmem_limit_bytes=16 * 2**20),
    )(*[stay(array) for array in arrays])


def second(levels, own, own_image, points, images, kept, copies, feat, group):
    keep = kept is not None
    slots, probes = own_image.shape[1], own_image.shape[0]
    one, small = pltpu.VMEM((probes, slots), F32), pltpu.VMEM((probes, 128), F32)
    scratch = [
        pltpu.VMEM((probes, copies * slots), F32),
        pltpu.VMEM((PIECES * images[0].shape[0], probes, 128), F32),
    ]
    arrays = [levels, own, own_image, *points, *images, *(kept or ())]
    if keep:
        arrays = [stay(array) for array in arrays]
    else:
        scratch.append(pltpu.VMEM((feature_rows(feat), copies * slots), BF16))
    return pl.pallas_call(
        functools.partial(second_kernel, feat, group, keep, copies),
        out_shape=[pltpu.VMEM((8, 128), F32), one, one, one, one, small],
        in_specs=[VMEM] * len(arrays),
        out_specs=[VMEM] * 6,
        scratch_shapes=scratch,
        compiler_params=pltpu.CompilerParams(vmem_limit_bytes=(16 if keep else 48) * 2**20),
    )(*arrays)


def finish_kernel(curve_ref, norm_ref, solution_ref, residual_ref, direction_ref, image_ref, out_ref, left_ref):
    probes = norm_ref.shape[0]
    curve = turned(curve_ref[...], 128)[:probes, :1]
    step_size = norm_ref[:, :1] / curve
    out_ref[...] = solution_ref[...] + step_size * direction_ref[...]
    left_ref[...] = residual_ref[...] - step_size * image_ref[...]


def gather(held, bits, count):
    for at in range(0, len(bits), 2):
        pair = bits[at : at + 2]
        flips = pair if len(pair) == 1 else [pair[0], pair[1], sum(pair)]
        held = jnp.concatenate([held] + [swap(held, flip, count) for flip in reversed(flips)], axis=0)
    return held


def total(held, bits, count):
    for at in range(0, len(bits), 2):
        pair = bits[at : at + 2]
        flips = pair if len(pair) == 1 else [pair[0], pair[1], sum(pair)]
        held = sum([swap(held, flip, count) for flip in reversed(flips)], held)
    return held


def body(count, points, inv_lengths, signal_level, noise_level, right_sides, block_counts):
    slots, feat = points.shape
    probes = right_sides.shape[1]
    copies = COPIES
    while copies > 1 and (copies * PIECES > count or copies * count * slots * slots * 2 > KEEP_BYTES):
        copies //= 4
    group = math.gcd(count // PIECES, 8)
    keep = copies == group == count // PIECES and copies * count * slots * slots * 2 <= KEEP_BYTES
    bits = [1 << k for k in reversed(range(count.bit_length() - 1))]
    later = bits[copies.bit_length() - 1 :]
    one, two, core = bits[-3:]
    own = prepare(points, inv_lengths, right_sides, block_counts)
    own, signal_level, noise_level = lax.optimization_barrier((own, signal_level, noise_level))
    levels = jnp.stack([jnp.log(signal_level[0]) * LOG2E, noise_level[0]])
    levels = jnp.broadcast_to(levels[:, None], (2, slots))
    first = functools.partial(apply_first, feat=feat, group=group, keep=keep)

    held = gather(own, bits[:-3], count)
    held, levels = lax.optimization_barrier((held, levels))
    near = held[:copies]
    held = held[:, : 2 * feat + probes]
    beside, up, over = (swap(held, bit, count) for bit in (core, one, two))
    kept_0, products, near_features = first(near, [held, beside], levels, None, [])
    up, products[-1] = lax.optimization_barrier((up, products[-1]))
    corner, up_beside = swap(up, two, count), swap(up, core, count)
    kept_1, products, _ = first(near, [up], levels, near_features, products)
    over, products[-1] = lax.optimization_barrier((over, products[-1]))
    over_beside = swap(over, core, count)
    kept_2, products, _ = first(near, [up_beside, over], levels, near_features, products)
    corner, products[-1] = lax.optimization_barrier((corner, products[-1]))
    corner_beside = swap(corner, core, count)
    kept_3, products, _ = first(near, [over_beside, corner], levels, near_features, products)
    kept_4, products, (message, own_image) = first(near, [corner_beside], levels, near_features, products, last=True)
    pieces = [held, beside, up, up_beside, over, over_beside, corner, corner_beside]
    kept = [*kept_0, *kept_1, *kept_2, *kept_3, *kept_4]

    held = gather(message, later[:-3], count)
    beside, up, over, corner = (swap(held, bit, count) for bit in (core, one, two, one | two))
    if keep:
        corner_beside = swap(corner, core, count)
        again_0 = apply_again([held, beside], kept[:2], copies)
        over, up, again_0[0] = lax.optimization_barrier((over, up, again_0[0]))
    else:
        corner_beside = swap(corner, core, count)
    up_beside, over_beside = (swap(array, core, count) for array in (up, over))
    if keep:
        again_1 = apply_again([corner, corner_beside], kept[6:], copies)
        again_2 = apply_again([up, over], [kept[2], kept[4]], copies)
        images = [held, beside, corner, corner_beside, up, over, up_beside, over_beside]
        order = [0, 1, 6, 7, 2, 4, 3, 5]
        kept, products = ([each[at] for at in order] for each in (kept, products))
        agains = [*again_0, *again_1, *again_2]
        done = combine(levels, own, own_image, pieces[0], images, products, agains, kept, copies, feat)
    else:
        images = [held, beside, up, up_beside, over, over_beside, corner, corner_beside]
        done = second(levels, own, own_image, pieces, images, None, copies, feat, group)
    partial, solution, residual, direction, second_image, norm = done
    partial = partial + swap(partial, core, count)
    apart = swap_apart(partial, bits[-3:], count)
    partial = partial + swap(partial, two, count) + (apart + swap(apart, core, count))
    partial = total(partial, later[:-3], count)
    done = jax.ShapeDtypeStruct((probes, slots), F32)
    solution, residual = pl.pallas_call(
        finish_kernel,
        out_shape=[done, done],
        in_specs=[VMEM] * 6,
        out_specs=[VMEM] * 2,
    )(*[stay(array) for array in (partial, norm, solution, residual, direction, second_image)])
    return solution.T, residual.T


def solution(mesh):
    count = math.prod(mesh.shape[axis] for axis in AXES)
    rows = P(AXES, None)
    return jax.shard_map(
        functools.partial(body, count),
        mesh=mesh,
        in_specs=(rows, P(), P(), P(), rows, P(AXES)),
        out_specs=(rows, rows),
        check_vma=False,
    )
```

```python
import functools
import math

import jax
import jax.numpy as jnp
from jax import lax
from jax.experimental import pallas as pl
from jax.experimental.pallas import tpu as pltpu
from jax.sharding import PartitionSpec as P

AXES = ("row", "col")
LOG2E = 1.0 / math.log(2.0)
FAR = 64.0
KEEP_BYTES = 20 * 2**20
COPIES = 4
PIECES = 8
TAIL = 16
LATE = 2
F32, BF16 = jnp.float32, jnp.bfloat16
VMEM = pl.BlockSpec(memory_space=pltpu.VMEM)


def stay(array):
    return pltpu.with_memory_space_constraint(array, pltpu.VMEM)


def swap(array, bit, count):
    return lax.ppermute(array, AXES, [(i, i ^ bit) for i in range(count)])


def two_parts(wide):
    high = wide.astype(BF16)
    return high, (wide - high.astype(F32)).astype(BF16)


def swap_apart(array, first, second, core, count):
    return lax.ppermute(array, AXES, [(i, i ^ (second if i & core else first)) for i in range(count)])


def three_parts(wide):
    high, _ = two_parts(wide)
    return high, *two_parts(wide - high.astype(F32))


def features(parts, level, left):
    feat = parts.shape[0] // 2
    high, low = parts[:feat], parts[feat:]
    scaled = high.astype(F32) + low.astype(F32)
    half = -0.5 * jnp.sum(scaled * scaled, axis=0, keepdims=True)
    if not left:
        half = half + level
    halves = [part.astype(F32) for part in three_parts(half)]
    ones = [jnp.ones_like(half)] * 3
    tail = (halves + ones if left else ones + halves) + [jnp.zeros((10, half.shape[1]), F32)]
    rows = [high, high, low, low] if left else [high, low, high, low]
    return jnp.concatenate(rows + [jnp.concatenate(tail, axis=0).astype(BF16)], axis=0)


def feature_rows(feat):
    return 4 * feat + 16


def prepare_kernel(points_ref, inv_ref, right_ref, count_ref, sent_ref):
    feat, slots = points_ref.shape
    probes = right_ref.shape[0]
    valid = lax.broadcasted_iota(jnp.int32, (1, slots), 1) < count_ref[0]
    row = lax.broadcasted_iota(jnp.int32, (feat, slots), 0)
    inverse = jnp.zeros((feat, slots), F32)
    for f in range(feat):
        inverse = jnp.where(row == f, inv_ref[f], inverse)
    scaled = points_ref[...] * inverse * math.sqrt(LOG2E)
    high, low = two_parts(jnp.where(valid, scaled, FAR))
    direction, rest = two_parts(jnp.where(valid, right_ref[...], 0.0))
    sent_ref[0, :feat, :] = high
    sent_ref[0, feat : 2 * feat, :] = low
    sent_ref[0, 2 * feat : 2 * feat + probes, :] = direction
    sent_ref[0, 2 * feat + probes :, :] = rest


def prepare(points, inv_lengths, right_sides, block_counts):
    smem = pl.BlockSpec(memory_space=pltpu.SMEM)
    return pl.pallas_call(
        prepare_kernel,
        out_shape=pltpu.VMEM((1, 2 * points.shape[1] + 2 * right_sides.shape[1], points.shape[0]), BF16),
        in_specs=[VMEM, smem, VMEM, smem],
        out_specs=VMEM,
    )(points.T, inv_lengths, right_sides.T, block_counts)


def fill_right(near_ref, levels_ref, right_ref, feat):
    blocks, slots = right_ref.shape[1] // near_ref.shape[2], near_ref.shape[2]
    for b in range(blocks):
        right_ref[:, b * slots : (b + 1) * slots] = features(near_ref[b, : 2 * feat, :], levels_ref[0:1, :], False)


def turned(rows, height):
    if rows.shape[0] < height:
        rows = jnp.concatenate([rows, jnp.zeros((height - rows.shape[0], rows.shape[1]), F32)], axis=0)
    return rows.T


def entries(left, right):
    powers = lax.dot_general(left, right, (((0,), (0,)), ((), ())), preferred_element_type=F32)
    return jnp.exp2(powers).astype(BF16)


def apply_kernel(feat, group, keep, begin, last, count, earlier, near_ref, levels_ref, *refs):
    far, refs = refs[:count], refs[count:]
    if begin:
        right_ref, refs = refs[-2], refs[:-2] + refs[-1:]
        fill_right(near_ref, levels_ref, right_ref, feat)
    else:
        right_ref, refs = refs[0], refs[1:]
    sum_ref, refs = refs[-1], refs[:-1]
    before, refs = refs[:earlier], refs[earlier:]
    kept, refs = (refs[:count], refs[count:]) if keep else ((), refs)
    products, refs = refs[: count if keep else 1 - last], refs[count if keep else 1 - last :]
    slots, probes = near_ref.shape[2], sum_ref.shape[0]

    def step(piece, g):
        blocks = [far[piece][g * group + b] for b in range(group)]
        left = jnp.concatenate([features(block[: 2 * feat], None, True) for block in blocks], axis=1)
        directions = jnp.concatenate([block[2 * feat :] for block in blocks], axis=1)
        block = entries(left, right_ref[...])
        if keep:
            kept[piece][g] = block
        return jnp.dot(directions, block, preferred_element_type=F32)

    steps = far[0].shape[0] // group
    if keep:
        done = [step(piece, 0) for piece in range(count)]
        for product_ref, product in zip(products, done):
            product_ref[...] = product
        if not last:
            return
        product = sum([before_ref[...] for before_ref in before], sum(done))
    else:
        sum_ref[...] = sum([before_ref[...] for before_ref in before], jnp.zeros(sum_ref.shape, F32))

        def add(piece, g, carry):
            sum_ref[...] += step(piece, g)
            return carry

        for piece in range(count):
            lax.fori_loop(0, steps, functools.partial(add, piece), 0)
        product = sum_ref[...]
        if not last:
            products[0][...] = product
            return
    out_ref, own_ref = refs
    images, rights = [], []
    norm = curve = jnp.zeros((probes, slots), F32)
    for b in range(near_ref.shape[0]):
        direction = near_ref[b, 2 * feat : 2 * feat + probes, :].astype(F32)
        right = direction + near_ref[b, 2 * feat + probes :, :].astype(F32)
        image = product[:, b * slots : (b + 1) * slots] + levels_ref[1:2, :] * direction
        norm = norm + right * right
        curve = curve + direction * image
        images.append(image)
        rights.append(right)
    own_ref[...] = images[0]
    norm, curve = (jnp.sum(each, axis=1, keepdims=True) for each in (norm, curve))
    usual = 1.0 / (jnp.exp2(levels_ref[0:1, :1]) + levels_ref[1:2, :1])
    likely = (norm > 0.0) & (curve > 1e-6 * norm)
    guess = jnp.where(likely, norm / jnp.where(likely, curve, 1.0), usual)
    guess = jnp.clip(guess, 1e-6, 1e3).astype(BF16)
    steps = [right - guess.astype(F32) * image for image, right in zip(images, rights)]
    for b, after in enumerate(steps):
        out_ref[0, b * probes : (b + 1) * probes, :] = after.astype(BF16)
    products = [[x * y for x, y in zip(*pair)] for pair in ((steps, steps), (steps, images), (images, images))]
    sums = [norm, curve] + [jnp.sum(sum(each), axis=1, keepdims=True) for each in products]
    lane = lax.broadcasted_iota(jnp.int32, (probes, 128), 1)
    flat = jnp.zeros((probes, 128), F32)
    for at, each in enumerate([*sums, guess.astype(F32)]):
        flat = jnp.where(lane == at, each, flat)
    high, middle, low = (part.astype(F32) for part in three_parts(turned(flat, 128)[:8]))
    rows = jnp.concatenate([jnp.concatenate([high, middle], axis=1), jnp.concatenate([low, jnp.zeros_like(low)], axis=1)])
    if slots > 256:
        rows = jnp.concatenate([rows, jnp.zeros((TAIL, slots - 256), F32)], axis=1)
    out_ref[0, len(images) * probes :, :] = rows.astype(BF16)


def apply_first(near, far, levels, right, products, feat, group, keep, last=False):
    copies, slots, probes = near.shape[0], near.shape[2], far[0].shape[1] - 2 * feat
    wide, steps, begin = group * slots, far[0].shape[0] // group, right is None
    product = pltpu.VMEM((probes, copies * slots), F32)
    outs = [product] * (len(far) if keep else 1 - last)
    if keep:
        outs = [pltpu.VMEM((steps, wide, copies * slots), BF16)] * len(far) + outs
    if last:
        outs = outs + [pltpu.VMEM((1, copies * probes + TAIL, slots), BF16), pltpu.VMEM((probes, slots), F32)]
    if begin:
        outs = outs + [pltpu.VMEM((feature_rows(feat), copies * slots), BF16)]
    before = products if last or not keep else products[-1:]
    arrays = [near, levels, *far, *([] if begin else [right]), *before]
    if keep:
        arrays = [stay(array) for array in arrays]
    done = pl.pallas_call(
        functools.partial(apply_kernel, feat, group, keep, begin, last, len(far), len(before)),
        out_shape=outs,
        in_specs=[VMEM] * len(arrays),
        out_specs=[VMEM] * len(outs),
        scratch_shapes=[pltpu.VMEM((probes, copies * slots), F32)],
        compiler_params=pltpu.CompilerParams(vmem_limit_bytes=(16 if keep else 40) * 2**20),
    )(*arrays)
    done = list(done)
    kept, done = (done[: len(far)], done[len(far) :]) if keep else ([None] * len(far), done)
    parts = len(far) if keep else 1 - last
    products = products + done[:parts] if keep else done[:parts]
    return kept, products, done[parts:] if last else done[parts] if begin else right


def step_sums(images, copies, probes):
    tails = []
    for w_ref in images:
        for g in range(w_ref.shape[0]):
            parts = w_ref[g, copies * probes :, :].astype(F32)
            tails.append(parts[:8, :128] + parts[:8, 128:256] + parts[8:, :128])
    norm_now, curve = (sum(tail[at : at + 1] for tail in tails) for at in range(2))
    step_size = norm_now / curve
    norm_next = jnp.zeros_like(norm_now)
    guesses = [tail[5:6] for tail in tails]
    for tail, guess in zip(tails, guesses):
        apart = guess - step_size
        norm_next = norm_next + (tail[2:3] + apart * (2.0 * tail[3:4] + apart * tail[4:5]))
    few = jnp.concatenate([step_size, norm_next / norm_now, norm_next, jnp.zeros((5, 128), F32)], axis=0)
    scales = []
    for start in range(0, len(guesses), 120):
        some = guesses[start : start + 120]
        columns = turned(jnp.concatenate([few] + [step_size / guess for guess in some], axis=0), 128)[:probes]
        scales += [columns[:, at + 8 : at + 9] for at in range(len(some))]
    return *(columns[:, at : at + 1] for at in range(3)), scales


def second_kernel(feat, group, keep, copies, levels_ref, own_ref, own_image_in_ref, *refs):
    points, images, refs = refs[:PIECES], refs[PIECES : 2 * PIECES], refs[2 * PIECES :]
    if keep:
        kept, refs = refs[:PIECES], refs[PIECES:]
    (partial_ref, solution_ref, residual_ref, own_dir_ref, own_image_ref, norm_ref, product_ref, scale_ref) = refs[:8]
    if not keep:
        right_ref = refs[8]
    slots, probes = images[0].shape[2], own_image_in_ref.shape[0]
    pairs = list(zip(points, images))
    groups = images[0].shape[0]

    def column(wide):
        return jnp.sum(wide, axis=1, keepdims=True)

    step_size, ratio, norm_next, scales = step_sums(images, copies, probes)
    for at, scale in enumerate(scales):
        scale_ref[at] = jnp.broadcast_to(scale, (probes, 128))

    def residual_of(piece, b):
        first = points[piece][b, 2 * feat :, :].astype(F32)
        sent = images[piece][b // copies, pl.ds(pl.multiple_of(b % copies * probes, probes), probes), :].astype(F32)
        return first + scale_ref[piece * groups + b // copies][:, :1] * (sent - first), first

    def direct(piece, b):
        residual, first = residual_of(piece, b)
        return (residual + ratio * first).astype(BF16)

    first = own_ref[0, 2 * feat : 2 * feat + probes, :].astype(F32)
    right = first + own_ref[0, 2 * feat + probes :, :].astype(F32)
    residual = right - step_size * own_image_in_ref[...]
    own_direction = (residual + ratio * first).astype(BF16)
    solution_ref[...] = step_size * first
    residual_ref[...] = residual
    own_dir_ref[...] = own_direction.astype(F32)
    if not keep:
        fill_right(points[0], levels_ref, right_ref, feat)

    def step(piece, g):
        directions = [direct(piece, g * group + b) for b in range(group)]
        if piece == 0:
            directions[0] = jnp.where(g == 0, own_direction, directions[0])
        if keep:
            block = kept[piece][g]
        else:
            blocks = [points[piece][g * group + b, : 2 * feat, :] for b in range(group)]
            left = jnp.concatenate([features(block, None, True) for block in blocks], axis=1)
            block = entries(left, right_ref[...])
        return jnp.dot(jnp.concatenate(directions, axis=1), block, preferred_element_type=F32)

    steps = points[0].shape[0] // group
    if steps == 1:
        product = sum(step(piece, 0) for piece in range(PIECES))
    else:
        product_ref[...] = jnp.zeros_like(product_ref)

        def add(piece, g, carry):
            product_ref[...] += step(piece, g)
            return carry

        for piece in range(PIECES):
            lax.fori_loop(0, steps, functools.partial(add, piece), 0)
        product = product_ref[...]

    curve = jnp.zeros((probes, slots), F32)
    for b in range(copies):
        direction = (direct(0, b) if b else own_direction).astype(F32)
        image = product[:, b * slots : (b + 1) * slots] + levels_ref[1:2, :] * direction
        curve = curve + direction * image
        if b == 0:
            own_image_ref[...] = image
    lane = lax.broadcasted_iota(jnp.int32, (probes, 128), 1)
    flat = jnp.where(lane == 0, column(curve), 0.0)
    partial_ref[...] = turned(flat, 128)[:8]
    norm_ref[...] = jnp.broadcast_to(norm_next, norm_ref.shape)


def sent_product(sent_ref, kept_ref, copies):
    probes = (sent_ref.shape[1] - TAIL) // copies
    sent = jnp.concatenate([sent_ref[0, b * probes : (b + 1) * probes, :] for b in range(copies)], axis=1)
    return jnp.dot(sent, kept_ref[0], preferred_element_type=F32)


def again_kernel(copies, count, *refs):
    for sent_ref, kept_ref, out_ref in zip(refs[:count], refs[count : 2 * count], refs[2 * count :]):
        out_ref[...] = sent_product(sent_ref, kept_ref, copies)


def apply_again(sent, kept, copies):
    outs = [pltpu.VMEM(((sent[0].shape[1] - TAIL) // copies, kept[0].shape[2]), F32)] * len(sent)
    done = pl.pallas_call(
        functools.partial(again_kernel, copies, len(sent)),
        out_shape=outs,
        in_specs=[VMEM] * (2 * len(sent)),
        out_specs=[VMEM] * len(sent),
        compiler_params=pltpu.CompilerParams(vmem_limit_bytes=16 * 2**20),
    )(*[stay(array) for array in (*sent, *kept)])
    return list(done)


def combine_kernel(feat, copies, levels_ref, own_ref, own_image_in_ref, near_ref, kept_near_ref, *refs):
    images, firsts, refs = refs[:PIECES], refs[PIECES : 2 * PIECES], refs[2 * PIECES :]
    late = LATE
    agains, kept, outs = refs[: PIECES - late], refs[PIECES - late : PIECES], refs[PIECES:]
    partial_ref, solution_ref, residual_ref, own_dir_ref, own_image_ref, norm_ref = outs
    slots, probes = images[0].shape[2], own_image_in_ref.shape[0]
    agains = [again_ref[...] for again_ref in agains]
    for image_ref, kept_ref in zip(images[PIECES - late :], kept):
        agains.append(sent_product(image_ref, kept_ref, copies))
    step_size, ratio, norm_next, scales = step_sums(images, copies, probes)
    product = jnp.zeros((probes, copies * slots), F32)
    for first_ref, again, scale in zip(firsts, agains, scales):
        product = product + ((1.0 - scale + ratio) * first_ref[...] + scale * again)

    first = own_ref[0, 2 * feat : 2 * feat + probes, :].astype(F32)
    right = first + own_ref[0, 2 * feat + probes :, :].astype(F32)
    residual = right - step_size * own_image_in_ref[...]
    directions = [(residual + ratio * first).astype(BF16).astype(F32)]
    solution_ref[...] = step_size * first
    residual_ref[...] = residual
    own_dir_ref[...] = directions[0]
    for b in range(copies):
        first = near_ref[b, 2 * feat :, :].astype(F32)
        sent = images[0][0, b * probes : (b + 1) * probes, :].astype(F32)
        directions.append((1.0 - scales[0] + ratio) * first + scales[0] * sent)
    exact, formed = directions[:2]
    product = product + jnp.dot((exact - formed).astype(BF16), kept_near_ref[0, :slots, :], preferred_element_type=F32)
    curve = jnp.zeros((probes, slots), F32)
    for b, direction in enumerate([exact] + directions[2:]):
        image = product[:, b * slots : (b + 1) * slots] + levels_ref[1:2, :] * direction
        curve = curve + direction * image
        if b == 0:
            own_image_ref[...] = image
    lane = lax.broadcasted_iota(jnp.int32, (probes, 128), 1)
    flat = jnp.where(lane == 0, jnp.sum(curve, axis=1, keepdims=True), 0.0)
    partial_ref[...] = turned(flat, 128)[:8]
    norm_ref[...] = jnp.broadcast_to(norm_next, norm_ref.shape)


def combine(levels, own, own_image, near, images, products, agains, kept, copies, feat):
    probes, slots = own_image.shape
    one, small = pltpu.VMEM((probes, slots), F32), pltpu.VMEM((probes, 128), F32)
    arrays = [levels, own, own_image, near, kept[0], *images, *products, *agains, *kept[len(agains) :]]
    return pl.pallas_call(
        functools.partial(combine_kernel, feat, copies),
        out_shape=[pltpu.VMEM((8, 128), F32), one, one, one, one, small],
        in_specs=[VMEM] * len(arrays),
        out_specs=[VMEM] * 6,
        compiler_params=pltpu.CompilerParams(vmem_limit_bytes=16 * 2**20),
    )(*[stay(array) for array in arrays])


def second(levels, own, own_image, points, images, kept, copies, feat, group):
    keep = kept is not None
    slots, probes = own_image.shape[1], own_image.shape[0]
    one, small = pltpu.VMEM((probes, slots), F32), pltpu.VMEM((probes, 128), F32)
    scratch = [
        pltpu.VMEM((probes, copies * slots), F32),
        pltpu.VMEM((PIECES * images[0].shape[0], probes, 128), F32),
    ]
    arrays = [levels, own, own_image, *points, *images, *(kept or ())]
    if keep:
        arrays = [stay(array) for array in arrays]
    else:
        scratch.append(pltpu.VMEM((feature_rows(feat), copies * slots), BF16))
    return pl.pallas_call(
        functools.partial(second_kernel, feat, group, keep, copies),
        out_shape=[pltpu.VMEM((8, 128), F32), one, one, one, one, small],
        in_specs=[VMEM] * len(arrays),
        out_specs=[VMEM] * 6,
        scratch_shapes=scratch,
        compiler_params=pltpu.CompilerParams(vmem_limit_bytes=(16 if keep else 48) * 2**20),
    )(*arrays)


def finish_kernel(curve_ref, norm_ref, solution_ref, residual_ref, direction_ref, image_ref, out_ref, left_ref):
    probes = norm_ref.shape[0]
    curve = turned(curve_ref[...], 128)[:probes, :1]
    step_size = norm_ref[:, :1] / curve
    out_ref[...] = solution_ref[...] + step_size * direction_ref[...]
    left_ref[...] = residual_ref[...] - step_size * image_ref[...]


def gather(held, bits, count):
    for at in range(0, len(bits), 2):
        pair = bits[at : at + 2]
        flips = pair if len(pair) == 1 else [pair[0], pair[1], sum(pair)]
        held = jnp.concatenate([held] + [swap(held, flip, count) for flip in reversed(flips)], axis=0)
    return held


def total(held, bits, count):
    for at in range(0, len(bits), 2):
        pair = bits[at : at + 2]
        flips = pair if len(pair) == 1 else [pair[0], pair[1], sum(pair)]
        held = sum([swap(held, flip, count) for flip in reversed(flips)], held)
    return held


def body(count, points, inv_lengths, signal_level, noise_level, right_sides, block_counts):
    slots, feat = points.shape
    probes = right_sides.shape[1]
    copies = COPIES
    while copies > 1 and (copies * PIECES > count or copies * count * slots * slots * 2 > KEEP_BYTES):
        copies //= 4
    group = math.gcd(count // PIECES, 8)
    keep = copies == group == count // PIECES and copies * count * slots * slots * 2 <= KEEP_BYTES
    bits = [1 << k for k in reversed(range(count.bit_length() - 1))]
    later = bits[copies.bit_length() - 1 :]
    one, two, core = bits[-3:]
    own = prepare(points, inv_lengths, right_sides, block_counts)
    own, signal_level, noise_level = lax.optimization_barrier((own, signal_level, noise_level))
    levels = jnp.stack([jnp.log(signal_level[0]) * LOG2E, noise_level[0]])
    levels = jnp.broadcast_to(levels[:, None], (2, slots))
    first = functools.partial(apply_first, feat=feat, group=group, keep=keep)

    held = gather(own, bits[:-3], count)
    held, levels = lax.optimization_barrier((held, levels))
    near = held[:copies]
    held = held[:, : 2 * feat + probes]
    beside = swap(held, core, count)
    up, over = swap_apart(held, one, two, core, count), swap_apart(held, two, one, core, count)
    kept_0, products, near_features = first(near, [held, beside], levels, None, [])
    up, products[-1] = lax.optimization_barrier((up, products[-1]))
    corner, up_beside = swap_apart(up, two, one, core, count), swap(up, core, count)
    kept_1, products, _ = first(near, [up], levels, near_features, products)
    over, products[-1] = lax.optimization_barrier((over, products[-1]))
    over_beside = swap(over, core, count)
    kept_2, products, _ = first(near, [up_beside, over], levels, near_features, products)
    corner, products[-1] = lax.optimization_barrier((corner, products[-1]))
    corner_beside = swap(corner, core, count)
    kept_3, products, _ = first(near, [over_beside, corner], levels, near_features, products)
    kept_4, products, (message, own_image) = first(near, [corner_beside], levels, near_features, products, last=True)
    pieces = [held, beside, up, up_beside, over, over_beside, corner, corner_beside]
    kept = [*kept_0, *kept_1, *kept_2, *kept_3, *kept_4]

    held = gather(message, later[:-3], count)
    beside, corner = swap(held, core, count), swap(held, one | two, count)
    up, over = swap_apart(held, one, two, core, count), swap_apart(held, two, one, core, count)
    if keep:
        corner_beside = swap(corner, core, count)
        again_0 = apply_again([held, beside], kept[:2], copies)
        over, up, again_0[0] = lax.optimization_barrier((over, up, again_0[0]))
    else:
        corner_beside = swap(corner, core, count)
    up_beside, over_beside = (swap(array, core, count) for array in (up, over))
    if keep:
        again_1 = apply_again([corner, corner_beside], kept[6:], copies)
        again_2 = apply_again([up, over], [kept[2], kept[4]], copies)
        images = [held, beside, corner, corner_beside, up, over, up_beside, over_beside]
        order = [0, 1, 6, 7, 2, 4, 3, 5]
        kept, products = ([each[at] for at in order] for each in (kept, products))
        agains = [*again_0, *again_1, *again_2]
        done = combine(levels, own, own_image, pieces[0], images, products, agains, kept, copies, feat)
    else:
        images = [held, beside, up, up_beside, over, over_beside, corner, corner_beside]
        done = second(levels, own, own_image, pieces, images, None, copies, feat, group)
    partial, solution, residual, direction, second_image, norm = done
    partial = partial + swap(partial, core, count)
    apart = swap_apart(partial, one, one | two, core, count)
    partial = partial + swap(partial, two, count) + (apart + swap(apart, core, count))
    partial = total(partial, later[:-3], count)
    done = jax.ShapeDtypeStruct((probes, slots), F32)
    solution, residual = pl.pallas_call(
        finish_kernel,
        out_shape=[done, done],
        in_specs=[VMEM] * 6,
        out_specs=[VMEM] * 2,
    )(*[stay(array) for array in (partial, norm, solution, residual, direction, second_image)])
    return solution.T, residual.T


def solution(mesh):
    count = math.prod(mesh.shape[axis] for axis in AXES)
    rows = P(AXES, None)
    return jax.shard_map(
        functools.partial(body, count),
        mesh=mesh,
        in_specs=(rows, P(), P(), P(), rows, P(AXES)),
        out_specs=(rows, rows),
        check_vma=False,
    )
```

```python
import functools
import math

import jax
import jax.numpy as jnp
from jax import lax
from jax.experimental import pallas as pl
from jax.experimental.pallas import tpu as pltpu
from jax.sharding import PartitionSpec as P

AXES = ("row", "col")
LOG2E = 1.0 / math.log(2.0)
FAR = 64.0
KEEP_BYTES = 20 * 2**20
COPIES = 4
PIECES = 8
TAIL = 16
LATE = 2
F32, BF16 = jnp.float32, jnp.bfloat16
VMEM = pl.BlockSpec(memory_space=pltpu.VMEM)


def stay(array):
    return pltpu.with_memory_space_constraint(array, pltpu.VMEM)


def swap(array, bit, count):
    return lax.ppermute(array, AXES, [(i, i ^ bit) for i in range(count)])


def two_parts(wide):
    high = wide.astype(BF16)
    return high, (wide - high.astype(F32)).astype(BF16)


def swap_apart(array, first, second, core, count):
    return lax.ppermute(array, AXES, [(i, i ^ (second if i & core else first)) for i in range(count)])


def three_parts(wide):
    high, _ = two_parts(wide)
    return high, *two_parts(wide - high.astype(F32))


def features(parts, level, left):
    feat = parts.shape[0] // 2
    high, low = parts[:feat], parts[feat:]
    scaled = high.astype(F32) + low.astype(F32)
    half = -0.5 * jnp.sum(scaled * scaled, axis=0, keepdims=True)
    if not left:
        half = half + level
    halves = [part.astype(F32) for part in three_parts(half)]
    ones = [jnp.ones_like(half)] * 3
    tail = (halves + ones if left else ones + halves) + [jnp.zeros((10, half.shape[1]), F32)]
    rows = [high, high, low, low] if left else [high, low, high, low]
    return jnp.concatenate(rows + [jnp.concatenate(tail, axis=0).astype(BF16)], axis=0)


def feature_rows(feat):
    return 4 * feat + 16


def prepare_kernel(points_ref, inv_ref, right_ref, count_ref, sent_ref):
    feat, slots = points_ref.shape
    probes = right_ref.shape[0]
    valid = lax.broadcasted_iota(jnp.int32, (1, slots), 1) < count_ref[0]
    row = lax.broadcasted_iota(jnp.int32, (feat, slots), 0)
    inverse = jnp.zeros((feat, slots), F32)
    for f in range(feat):
        inverse = jnp.where(row == f, inv_ref[f], inverse)
    scaled = points_ref[...] * inverse * math.sqrt(LOG2E)
    high, low = two_parts(jnp.where(valid, scaled, FAR))
    direction, rest = two_parts(jnp.where(valid, right_ref[...], 0.0))
    sent_ref[0, :feat, :] = high
    sent_ref[0, feat : 2 * feat, :] = low
    sent_ref[0, 2 * feat : 2 * feat + probes, :] = direction
    sent_ref[0, 2 * feat + probes :, :] = rest


def prepare(points, inv_lengths, right_sides, block_counts):
    smem = pl.BlockSpec(memory_space=pltpu.SMEM)
    return pl.pallas_call(
        prepare_kernel,
        out_shape=pltpu.VMEM((1, 2 * points.shape[1] + 2 * right_sides.shape[1], points.shape[0]), BF16),
        in_specs=[VMEM, smem, VMEM, smem],
        out_specs=VMEM,
    )(points.T, inv_lengths, right_sides.T, block_counts)


def fill_right(near_ref, levels_ref, right_ref, feat):
    blocks, slots = right_ref.shape[1] // near_ref.shape[2], near_ref.shape[2]
    for b in range(blocks):
        right_ref[:, b * slots : (b + 1) * slots] = features(near_ref[b, : 2 * feat, :], levels_ref[0:1, :], False)


def turned(rows, height):
    if rows.shape[0] < height:
        rows = jnp.concatenate([rows, jnp.zeros((height - rows.shape[0], rows.shape[1]), F32)], axis=0)
    return rows.T


def entries(left, right):
    powers = lax.dot_general(left, right, (((0,), (0,)), ((), ())), preferred_element_type=F32)
    return jnp.exp2(powers).astype(BF16)


def apply_kernel(feat, group, keep, begin, last, count, earlier, near_ref, levels_ref, *refs):
    far, refs = refs[:count], refs[count:]
    if begin:
        right_ref, refs = refs[-2], refs[:-2] + refs[-1:]
        fill_right(near_ref, levels_ref, right_ref, feat)
    else:
        right_ref, refs = refs[0], refs[1:]
    sum_ref, refs = refs[-1], refs[:-1]
    before, refs = refs[:earlier], refs[earlier:]
    kept, refs = (refs[:count], refs[count:]) if keep else ((), refs)
    products, refs = refs[: count if keep else 1 - last], refs[count if keep else 1 - last :]
    slots, probes = near_ref.shape[2], sum_ref.shape[0]

    def step(piece, g):
        blocks = [far[piece][g * group + b] for b in range(group)]
        left = jnp.concatenate([features(block[: 2 * feat], None, True) for block in blocks], axis=1)
        directions = jnp.concatenate([block[2 * feat :] for block in blocks], axis=1)
        block = entries(left, right_ref[...])
        if keep:
            kept[piece][g] = block
        return jnp.dot(directions, block, preferred_element_type=F32)

    steps = far[0].shape[0] // group
    if keep:
        done = [step(piece, 0) for piece in range(count)]
        for product_ref, product in zip(products, done):
            product_ref[...] = product
        if not last:
            return
        product = sum([before_ref[...] for before_ref in before], sum(done))
    else:
        sum_ref[...] = sum([before_ref[...] for before_ref in before], jnp.zeros(sum_ref.shape, F32))

        def add(piece, g, carry):
            sum_ref[...] += step(piece, g)
            return carry

        for piece in range(count):
            lax.fori_loop(0, steps, functools.partial(add, piece), 0)
        product = sum_ref[...]
        if not last:
            products[0][...] = product
            return
    out_ref, own_ref = refs
    images, rights = [], []
    norm = curve = jnp.zeros((probes, slots), F32)
    for b in range(near_ref.shape[0]):
        direction = near_ref[b, 2 * feat : 2 * feat + probes, :].astype(F32)
        right = direction + near_ref[b, 2 * feat + probes :, :].astype(F32)
        image = product[:, b * slots : (b + 1) * slots] + levels_ref[1:2, :] * direction
        norm = norm + right * right
        curve = curve + direction * image
        images.append(image)
        rights.append(right)
    own_ref[...] = images[0]
    norm, curve = (jnp.sum(each, axis=1, keepdims=True) for each in (norm, curve))
    usual = 1.0 / (jnp.exp2(levels_ref[0:1, :1]) + levels_ref[1:2, :1])
    likely = (norm > 0.0) & (curve > 1e-6 * norm)
    guess = jnp.where(likely, norm / jnp.where(likely, curve, 1.0), usual)
    guess = jnp.clip(guess, 1e-6, 1e3).astype(BF16)
    steps = [right - guess.astype(F32) * image for image, right in zip(images, rights)]
    for b, after in enumerate(steps):
        out_ref[0, b * probes : (b + 1) * probes, :] = after.astype(BF16)
    products = [[x * y for x, y in zip(*pair)] for pair in ((steps, steps), (steps, images), (images, images))]
    sums = [norm, curve] + [jnp.sum(sum(each), axis=1, keepdims=True) for each in products]
    lane = lax.broadcasted_iota(jnp.int32, (probes, 128), 1)
    flat = jnp.zeros((probes, 128), F32)
    for at, each in enumerate([*sums, guess.astype(F32)]):
        flat = jnp.where(lane == at, each, flat)
    high, middle, low = (part.astype(F32) for part in three_parts(turned(flat, 128)[:8]))
    rows = jnp.concatenate([jnp.concatenate([high, middle], axis=1), jnp.concatenate([low, jnp.zeros_like(low)], axis=1)])
    if slots > 256:
        rows = jnp.concatenate([rows, jnp.zeros((TAIL, slots - 256), F32)], axis=1)
    out_ref[0, len(images) * probes :, :] = rows.astype(BF16)


def apply_first(near, far, levels, right, products, feat, group, keep, last=False):
    copies, slots, probes = near.shape[0], near.shape[2], far[0].shape[1] - 2 * feat
    wide, steps, begin = group * slots, far[0].shape[0] // group, right is None
    product = pltpu.VMEM((probes, copies * slots), F32)
    outs = [product] * (len(far) if keep else 1 - last)
    if keep:
        outs = [pltpu.VMEM((steps, wide, copies * slots), BF16)] * len(far) + outs
    if last:
        outs = outs + [pltpu.VMEM((1, copies * probes + TAIL, slots), BF16), pltpu.VMEM((probes, slots), F32)]
    if begin:
        outs = outs + [pltpu.VMEM((feature_rows(feat), copies * slots), BF16)]
    before = products if last or not keep else products[-1:]
    arrays = [near, levels, *far, *([] if begin else [right]), *before]
    if keep:
        arrays = [stay(array) for array in arrays]
    done = pl.pallas_call(
        functools.partial(apply_kernel, feat, group, keep, begin, last, len(far), len(before)),
        out_shape=outs,
        in_specs=[VMEM] * len(arrays),
        out_specs=[VMEM] * len(outs),
        scratch_shapes=[pltpu.VMEM((probes, copies * slots), F32)],
        compiler_params=pltpu.CompilerParams(vmem_limit_bytes=(16 if keep else 40) * 2**20),
    )(*arrays)
    done = list(done)
    kept, done = (done[: len(far)], done[len(far) :]) if keep else ([None] * len(far), done)
    parts = len(far) if keep else 1 - last
    products = products + done[:parts] if keep else done[:parts]
    return kept, products, done[parts:] if last else done[parts] if begin else right


def step_sums(images, copies, probes):
    tails = []
    for w_ref in images:
        for g in range(w_ref.shape[0]):
            parts = w_ref[g, copies * probes :, :].astype(F32)
            tails.append(parts[:8, :128] + parts[:8, 128:256] + parts[8:, :128])
    norm_now, curve = (sum(tail[at : at + 1] for tail in tails) for at in range(2))
    step_size = norm_now / curve
    norm_next = jnp.zeros_like(norm_now)
    guesses = [tail[5:6] for tail in tails]
    for tail, guess in zip(tails, guesses):
        apart = guess - step_size
        norm_next = norm_next + (tail[2:3] + apart * (2.0 * tail[3:4] + apart * tail[4:5]))
    few = jnp.concatenate([step_size, norm_next / norm_now, norm_next, jnp.zeros((5, 128), F32)], axis=0)
    scales = []
    for start in range(0, len(guesses), 120):
        some = guesses[start : start + 120]
        columns = turned(jnp.concatenate([few] + [step_size / guess for guess in some], axis=0), 128)[:probes]
        scales += [columns[:, at + 8 : at + 9] for at in range(len(some))]
    return *(columns[:, at : at + 1] for at in range(3)), scales


def second_kernel(feat, group, keep, copies, levels_ref, own_ref, own_image_in_ref, *refs):
    points, images, refs = refs[:PIECES], refs[PIECES : 2 * PIECES], refs[2 * PIECES :]
    if keep:
        kept, refs = refs[:PIECES], refs[PIECES:]
    (partial_ref, solution_ref, residual_ref, own_dir_ref, own_image_ref, norm_ref, product_ref, scale_ref) = refs[:8]
    if not keep:
        right_ref = refs[8]
    slots, probes = images[0].shape[2], own_image_in_ref.shape[0]
    pairs = list(zip(points, images))
    groups = images[0].shape[0]

    def column(wide):
        return jnp.sum(wide, axis=1, keepdims=True)

    step_size, ratio, norm_next, scales = step_sums(images, copies, probes)
    for at, scale in enumerate(scales):
        scale_ref[at] = jnp.broadcast_to(scale, (probes, 128))

    def residual_of(piece, b):
        first = points[piece][b, 2 * feat :, :].astype(F32)
        sent = images[piece][b // copies, pl.ds(pl.multiple_of(b % copies * probes, probes), probes), :].astype(F32)
        return first + scale_ref[piece * groups + b // copies][:, :1] * (sent - first), first

    def direct(piece, b):
        residual, first = residual_of(piece, b)
        return (residual + ratio * first).astype(BF16)

    first = own_ref[0, 2 * feat : 2 * feat + probes, :].astype(F32)
    right = first + own_ref[0, 2 * feat + probes :, :].astype(F32)
    residual = right - step_size * own_image_in_ref[...]
    own_direction = (residual + ratio * first).astype(BF16)
    solution_ref[...] = step_size * first
    residual_ref[...] = residual
    own_dir_ref[...] = own_direction.astype(F32)
    if not keep:
        fill_right(points[0], levels_ref, right_ref, feat)

    def step(piece, g):
        directions = [direct(piece, g * group + b) for b in range(group)]
        if piece == 0:
            directions[0] = jnp.where(g == 0, own_direction, directions[0])
        if keep:
            block = kept[piece][g]
        else:
            blocks = [points[piece][g * group + b, : 2 * feat, :] for b in range(group)]
            left = jnp.concatenate([features(block, None, True) for block in blocks], axis=1)
            block = entries(left, right_ref[...])
        return jnp.dot(jnp.concatenate(directions, axis=1), block, preferred_element_type=F32)

    steps = points[0].shape[0] // group
    if steps == 1:
        product = sum(step(piece, 0) for piece in range(PIECES))
    else:
        product_ref[...] = jnp.zeros_like(product_ref)

        def add(piece, g, carry):
            product_ref[...] += step(piece, g)
            return carry

        for piece in range(PIECES):
            lax.fori_loop(0, steps, functools.partial(add, piece), 0)
        product = product_ref[...]

    curve = jnp.zeros((probes, slots), F32)
    for b in range(copies):
        direction = (direct(0, b) if b else own_direction).astype(F32)
        image = product[:, b * slots : (b + 1) * slots] + levels_ref[1:2, :] * direction
        curve = curve + direction * image
        if b == 0:
            own_image_ref[...] = image
    lane = lax.broadcasted_iota(jnp.int32, (probes, 128), 1)
    flat = jnp.where(lane == 0, column(curve), 0.0)
    partial_ref[...] = turned(flat, 128)[:8]
    norm_ref[...] = jnp.broadcast_to(norm_next, norm_ref.shape)


def sent_product(sent_ref, kept_ref, copies):
    probes = (sent_ref.shape[1] - TAIL) // copies
    sent = jnp.concatenate([sent_ref[0, b * probes : (b + 1) * probes, :] for b in range(copies)], axis=1)
    return jnp.dot(sent, kept_ref[0], preferred_element_type=F32)


def again_kernel(copies, count, *refs):
    for sent_ref, kept_ref, out_ref in zip(refs[:count], refs[count : 2 * count], refs[2 * count :]):
        out_ref[...] = sent_product(sent_ref, kept_ref, copies)


def apply_again(sent, kept, copies):
    outs = [pltpu.VMEM(((sent[0].shape[1] - TAIL) // copies, kept[0].shape[2]), F32)] * len(sent)
    done = pl.pallas_call(
        functools.partial(again_kernel, copies, len(sent)),
        out_shape=outs,
        in_specs=[VMEM] * (2 * len(sent)),
        out_specs=[VMEM] * len(sent),
        compiler_params=pltpu.CompilerParams(vmem_limit_bytes=16 * 2**20),
    )(*[stay(array) for array in (*sent, *kept)])
    return list(done)


def combine_kernel(feat, copies, levels_ref, own_ref, own_image_in_ref, near_ref, kept_near_ref, *refs):
    images, firsts, refs = refs[:PIECES], refs[PIECES : 2 * PIECES], refs[2 * PIECES :]
    late = LATE
    agains, kept, outs = refs[: PIECES - late], refs[PIECES - late : PIECES], refs[PIECES:]
    partial_ref, solution_ref, residual_ref, own_dir_ref, own_image_ref, norm_ref = outs
    slots, probes = images[0].shape[2], own_image_in_ref.shape[0]
    agains = [again_ref[...] for again_ref in agains]
    for image_ref, kept_ref in zip(images[PIECES - late :], kept):
        agains.append(sent_product(image_ref, kept_ref, copies))
    step_size, ratio, norm_next, scales = step_sums(images, copies, probes)
    product = jnp.zeros((probes, copies * slots), F32)
    for first_ref, again, scale in zip(firsts, agains, scales):
        product = product + ((1.0 - scale + ratio) * first_ref[...] + scale * again)

    first = own_ref[0, 2 * feat : 2 * feat + probes, :].astype(F32)
    right = first + own_ref[0, 2 * feat + probes :, :].astype(F32)
    residual = right - step_size * own_image_in_ref[...]
    directions = [(residual + ratio * first).astype(BF16).astype(F32)]
    solution_ref[...] = step_size * first
    residual_ref[...] = residual
    own_dir_ref[...] = directions[0]
    for b in range(copies):
        first = near_ref[b, 2 * feat :, :].astype(F32)
        sent = images[0][0, b * probes : (b + 1) * probes, :].astype(F32)
        directions.append((1.0 - scales[0] + ratio) * first + scales[0] * sent)
    exact, formed = directions[:2]
    product = product + jnp.dot((exact - formed).astype(BF16), kept_near_ref[0, :slots, :], preferred_element_type=F32)
    curve = jnp.zeros((probes, slots), F32)
    for b, direction in enumerate([exact] + directions[2:]):
        image = product[:, b * slots : (b + 1) * slots] + levels_ref[1:2, :] * direction
        curve = curve + direction * image
        if b == 0:
            own_image_ref[...] = image
    lane = lax.broadcasted_iota(jnp.int32, (probes, 128), 1)
    flat = jnp.where(lane == 0, jnp.sum(curve, axis=1, keepdims=True), 0.0)
    partial_ref[...] = turned(flat, 128)[:8]
    norm_ref[...] = jnp.broadcast_to(norm_next, norm_ref.shape)


def combine(levels, own, own_image, near, images, products, agains, kept, copies, feat):
    probes, slots = own_image.shape
    one, small = pltpu.VMEM((probes, slots), F32), pltpu.VMEM((probes, 128), F32)
    arrays = [levels, own, own_image, near, kept[0], *images, *products, *agains, *kept[len(agains) :]]
    return pl.pallas_call(
        functools.partial(combine_kernel, feat, copies),
        out_shape=[pltpu.VMEM((8, 128), F32), one, one, one, one, small],
        in_specs=[VMEM] * len(arrays),
        out_specs=[VMEM] * 6,
        compiler_params=pltpu.CompilerParams(vmem_limit_bytes=16 * 2**20),
    )(*[stay(array) for array in arrays])


def second(levels, own, own_image, points, images, kept, copies, feat, group):
    keep = kept is not None
    slots, probes = own_image.shape[1], own_image.shape[0]
    one, small = pltpu.VMEM((probes, slots), F32), pltpu.VMEM((probes, 128), F32)
    scratch = [
        pltpu.VMEM((probes, copies * slots), F32),
        pltpu.VMEM((PIECES * images[0].shape[0], probes, 128), F32),
    ]
    arrays = [levels, own, own_image, *points, *images, *(kept or ())]
    if keep:
        arrays = [stay(array) for array in arrays]
    else:
        scratch.append(pltpu.VMEM((feature_rows(feat), copies * slots), BF16))
    return pl.pallas_call(
        functools.partial(second_kernel, feat, group, keep, copies),
        out_shape=[pltpu.VMEM((8, 128), F32), one, one, one, one, small],
        in_specs=[VMEM] * len(arrays),
        out_specs=[VMEM] * 6,
        scratch_shapes=scratch,
        compiler_params=pltpu.CompilerParams(vmem_limit_bytes=(16 if keep else 48) * 2**20),
    )(*arrays)


def finish_kernel(curve_ref, norm_ref, solution_ref, residual_ref, direction_ref, image_ref, out_ref, left_ref):
    probes = norm_ref.shape[0]
    curve = turned(curve_ref[...], 128)[:probes, :1]
    step_size = norm_ref[:, :1] / curve
    out_ref[...] = solution_ref[...] + step_size * direction_ref[...]
    left_ref[...] = residual_ref[...] - step_size * image_ref[...]


def gather(held, bits, count):
    for at in range(0, len(bits), 2):
        pair = bits[at : at + 2]
        flips = pair if len(pair) == 1 else [pair[0], sum(pair), pair[1]]
        held = jnp.concatenate([held] + [swap(held, flip, count) for flip in flips], axis=0)
    return held


def total(held, bits, count):
    for at in range(0, len(bits), 2):
        pair = bits[at : at + 2]
        flips = pair if len(pair) == 1 else [pair[0], pair[1], sum(pair)]
        held = sum([swap(held, flip, count) for flip in reversed(flips)], held)
    return held


def body(count, points, inv_lengths, signal_level, noise_level, right_sides, block_counts):
    slots, feat = points.shape
    probes = right_sides.shape[1]
    copies = COPIES
    while copies > 1 and (copies * PIECES > count or copies * count * slots * slots * 2 > KEEP_BYTES):
        copies //= 4
    group = math.gcd(count // PIECES, 8)
    keep = copies == group == count // PIECES and copies * count * slots * slots * 2 <= KEEP_BYTES
    bits = [1 << k for k in reversed(range(count.bit_length() - 1))]
    later = bits[copies.bit_length() - 1 :]
    one, two, core = bits[-3:]
    own = prepare(points, inv_lengths, right_sides, block_counts)
    own, signal_level, noise_level = lax.optimization_barrier((own, signal_level, noise_level))
    levels = jnp.stack([jnp.log(signal_level[0]) * LOG2E, noise_level[0]])
    levels = jnp.broadcast_to(levels[:, None], (2, slots))
    first = functools.partial(apply_first, feat=feat, group=group, keep=keep)

    held = gather(own, bits[:-3], count)
    held, levels = lax.optimization_barrier((held, levels))
    near = held[:copies]
    held = held[:, : 2 * feat + probes]
    beside = swap(held, core, count)
    up = swap_apart(held, one, two, core, count)
    kept_h, products, near_features = first(near, [held], levels, None, [])
    held_again, products[-1] = lax.optimization_barrier((held, products[-1]))
    over = swap_apart(held_again, two, one, core, count)
    kept_0, products, _ = first(near, [beside], levels, near_features, products)
    kept_0 = [*kept_h, *kept_0]
    up, products[-1] = lax.optimization_barrier((up, products[-1]))
    corner, up_beside = swap_apart(up, two, one, core, count), swap(up, core, count)
    kept_1, products, _ = first(near, [up], levels, near_features, products)
    over, products[-1] = lax.optimization_barrier((over, products[-1]))
    over_beside = swap(over, core, count)
    kept_2, products, _ = first(near, [up_beside, over], levels, near_features, products)
    corner, products[-1] = lax.optimization_barrier((corner, products[-1]))
    corner_beside = swap(corner, core, count)
    kept_3, products, _ = first(near, [over_beside, corner], levels, near_features, products)
    kept_4, products, (message, own_image) = first(near, [corner_beside], levels, near_features, products, last=True)
    pieces = [held, beside, up, up_beside, over, over_beside, corner, corner_beside]
    kept = [*kept_0, *kept_1, *kept_2, *kept_3, *kept_4]

    held = gather(message, later[:-3], count)
    beside, corner = swap(held, core, count), swap(held, one | two, count)
    up, over = swap_apart(held, one, two, core, count), swap_apart(held, two, one, core, count)
    if keep:
        corner_beside = swap(corner, core, count)
        again_0 = apply_again([held, beside], kept[:2], copies)
        over, up, again_0[0] = lax.optimization_barrier((over, up, again_0[0]))
    else:
        corner_beside = swap(corner, core, count)
    up_beside, over_beside = (swap(array, core, count) for array in (up, over))
    if keep:
        again_1 = apply_again([corner, corner_beside], kept[6:], copies)
        again_2 = apply_again([up, over], [kept[2], kept[4]], copies)
        images = [held, beside, corner, corner_beside, up, over, up_beside, over_beside]
        order = [0, 1, 6, 7, 2, 4, 3, 5]
        kept, products = ([each[at] for at in order] for each in (kept, products))
        agains = [*again_0, *again_1, *again_2]
        done = combine(levels, own, own_image, pieces[0], images, products, agains, kept, copies, feat)
    else:
        images = [held, beside, up, up_beside, over, over_beside, corner, corner_beside]
        done = second(levels, own, own_image, pieces, images, None, copies, feat, group)
    partial, solution, residual, direction, second_image, norm = done
    partial = partial + swap(partial, core, count)
    apart = swap_apart(partial, one, one | two, core, count)
    partial = partial + swap(partial, two, count) + (apart + swap(apart, core, count))
    partial = total(partial, later[:-3], count)
    done = jax.ShapeDtypeStruct((probes, slots), F32)
    solution, residual = pl.pallas_call(
        finish_kernel,
        out_shape=[done, done],
        in_specs=[VMEM] * 6,
        out_specs=[VMEM] * 2,
    )(*[stay(array) for array in (partial, norm, solution, residual, direction, second_image)])
    return solution.T, residual.T


def solution(mesh):
    count = math.prod(mesh.shape[axis] for axis in AXES)
    rows = P(AXES, None)
    return jax.shard_map(
        functools.partial(body, count),
        mesh=mesh,
        in_specs=(rows, P(), P(), P(), rows, P(AXES)),
        out_specs=(rows, rows),
        check_vma=False,
    )
```

```python
import functools
import math

import jax
import jax.numpy as jnp
from jax import lax
from jax.experimental import pallas as pl
from jax.experimental.pallas import tpu as pltpu
from jax.sharding import PartitionSpec as P

AXES = ("row", "col")
LOG2E = 1.0 / math.log(2.0)
FAR = 64.0
KEEP_BYTES = 20 * 2**20
COPIES = 4
PIECES = 8
TAIL = 16
LATE = 2
F32, BF16 = jnp.float32, jnp.bfloat16
VMEM = pl.BlockSpec(memory_space=pltpu.VMEM)


def stay(array):
    return pltpu.with_memory_space_constraint(array, pltpu.VMEM)


def swap(array, bit, count):
    return lax.ppermute(array, AXES, [(i, i ^ bit) for i in range(count)])


def two_parts(wide):
    high = wide.astype(BF16)
    return high, (wide - high.astype(F32)).astype(BF16)


def swap_apart(array, first, second, core, count):
    return lax.ppermute(array, AXES, [(i, i ^ (second if i & core else first)) for i in range(count)])


def three_parts(wide):
    high, _ = two_parts(wide)
    return high, *two_parts(wide - high.astype(F32))


def features(parts, level, left):
    feat = parts.shape[0] // 2
    high, low = parts[:feat], parts[feat:]
    scaled = high.astype(F32) + low.astype(F32)
    half = -0.5 * jnp.sum(scaled * scaled, axis=0, keepdims=True)
    if not left:
        half = half + level
    halves = [part.astype(F32) for part in three_parts(half)]
    ones = [jnp.ones_like(half)] * 3
    tail = (halves + ones if left else ones + halves) + [jnp.zeros((10, half.shape[1]), F32)]
    rows = [high, high, low, low] if left else [high, low, high, low]
    return jnp.concatenate(rows + [jnp.concatenate(tail, axis=0).astype(BF16)], axis=0)


def feature_rows(feat):
    return 4 * feat + 16


def prepare_kernel(points_ref, inv_ref, right_ref, count_ref, sent_ref):
    feat, slots = points_ref.shape
    probes = right_ref.shape[0]
    valid = lax.broadcasted_iota(jnp.int32, (1, slots), 1) < count_ref[0]
    row = lax.broadcasted_iota(jnp.int32, (feat, slots), 0)
    inverse = jnp.zeros((feat, slots), F32)
    for f in range(feat):
        inverse = jnp.where(row == f, inv_ref[f], inverse)
    scaled = points_ref[...] * inverse * math.sqrt(LOG2E)
    high, low = two_parts(jnp.where(valid, scaled, FAR))
    direction, rest = two_parts(jnp.where(valid, right_ref[...], 0.0))
    sent_ref[0, :feat, :] = high
    sent_ref[0, feat : 2 * feat, :] = low
    sent_ref[0, 2 * feat : 2 * feat + probes, :] = direction
    sent_ref[0, 2 * feat + probes :, :] = rest


def prepare(points, inv_lengths, right_sides, block_counts):
    smem = pl.BlockSpec(memory_space=pltpu.SMEM)
    return pl.pallas_call(
        prepare_kernel,
        out_shape=pltpu.VMEM((1, 2 * points.shape[1] + 2 * right_sides.shape[1], points.shape[0]), BF16),
        in_specs=[VMEM, smem, VMEM, smem],
        out_specs=VMEM,
    )(points.T, inv_lengths, right_sides.T, block_counts)


def fill_right(near_ref, levels_ref, right_ref, feat):
    blocks, slots = right_ref.shape[1] // near_ref.shape[2], near_ref.shape[2]
    for b in range(blocks):
        right_ref[:, b * slots : (b + 1) * slots] = features(near_ref[b, : 2 * feat, :], levels_ref[0:1, :], False)


def turned(rows, height):
    if rows.shape[0] < height:
        rows = jnp.concatenate([rows, jnp.zeros((height - rows.shape[0], rows.shape[1]), F32)], axis=0)
    return rows.T


def entries(left, right):
    powers = lax.dot_general(left, right, (((0,), (0,)), ((), ())), preferred_element_type=F32)
    return jnp.exp2(powers).astype(BF16)


def apply_kernel(feat, group, keep, begin, last, count, earlier, near_ref, levels_ref, *refs):
    far, refs = refs[:count], refs[count:]
    if begin:
        right_ref, refs = refs[-2], refs[:-2] + refs[-1:]
        fill_right(near_ref, levels_ref, right_ref, feat)
    else:
        right_ref, refs = refs[0], refs[1:]
    sum_ref, refs = refs[-1], refs[:-1]
    before, refs = refs[:earlier], refs[earlier:]
    kept, refs = (refs[:count], refs[count:]) if keep else ((), refs)
    products, refs = refs[: count if keep else 1 - last], refs[count if keep else 1 - last :]
    slots, probes = near_ref.shape[2], sum_ref.shape[0]

    def step(piece, g):
        blocks = [far[piece][g * group + b] for b in range(group)]
        left = jnp.concatenate([features(block[: 2 * feat], None, True) for block in blocks], axis=1)
        directions = jnp.concatenate([block[2 * feat :] for block in blocks], axis=1)
        block = entries(left, right_ref[...])
        if keep:
            kept[piece][g] = block
        return jnp.dot(directions, block, preferred_element_type=F32)

    steps = far[0].shape[0] // group
    if keep:
        done = [step(piece, 0) for piece in range(count)]
        for product_ref, product in zip(products, done):
            product_ref[...] = product
        if not last:
            return
        product = sum([before_ref[...] for before_ref in before], sum(done))
    else:
        sum_ref[...] = sum([before_ref[...] for before_ref in before], jnp.zeros(sum_ref.shape, F32))

        def add(piece, g, carry):
            sum_ref[...] += step(piece, g)
            return carry

        for piece in range(count):
            lax.fori_loop(0, steps, functools.partial(add, piece), 0)
        product = sum_ref[...]
        if not last:
            products[0][...] = product
            return
    out_ref, own_ref = refs
    images, rights = [], []
    norm = curve = jnp.zeros((probes, slots), F32)
    for b in range(near_ref.shape[0]):
        direction = near_ref[b, 2 * feat : 2 * feat + probes, :].astype(F32)
        right = direction + near_ref[b, 2 * feat + probes :, :].astype(F32)
        image = product[:, b * slots : (b + 1) * slots] + levels_ref[1:2, :] * direction
        norm = norm + right * right
        curve = curve + direction * image
        images.append(image)
        rights.append(right)
    own_ref[...] = images[0]
    norm, curve = (jnp.sum(each, axis=1, keepdims=True) for each in (norm, curve))
    usual = 1.0 / (jnp.exp2(levels_ref[0:1, :1]) + levels_ref[1:2, :1])
    likely = (norm > 0.0) & (curve > 1e-6 * norm)
    guess = jnp.where(likely, norm / jnp.where(likely, curve, 1.0), usual)
    guess = jnp.clip(guess, 1e-6, 1e3).astype(BF16)
    steps = [right - guess.astype(F32) * image for image, right in zip(images, rights)]
    for b, after in enumerate(steps):
        out_ref[0, b * probes : (b + 1) * probes, :] = after.astype(BF16)
    products = [[x * y for x, y in zip(*pair)] for pair in ((steps, steps), (steps, images), (images, images))]
    sums = [norm, curve] + [jnp.sum(sum(each), axis=1, keepdims=True) for each in products]
    lane = lax.broadcasted_iota(jnp.int32, (probes, 128), 1)
    flat = jnp.zeros((probes, 128), F32)
    for at, each in enumerate([*sums, guess.astype(F32)]):
        flat = jnp.where(lane == at, each, flat)
    high, middle, low = (part.astype(F32) for part in three_parts(turned(flat, 128)[:8]))
    rows = jnp.concatenate([jnp.concatenate([high, middle], axis=1), jnp.concatenate([low, jnp.zeros_like(low)], axis=1)])
    if slots > 256:
        rows = jnp.concatenate([rows, jnp.zeros((TAIL, slots - 256), F32)], axis=1)
    out_ref[0, len(images) * probes :, :] = rows.astype(BF16)


def apply_first(near, far, levels, right, products, feat, group, keep, last=False):
    copies, slots, probes = near.shape[0], near.shape[2], far[0].shape[1] - 2 * feat
    wide, steps, begin = group * slots, far[0].shape[0] // group, right is None
    product = pltpu.VMEM((probes, copies * slots), F32)
    outs = [product] * (len(far) if keep else 1 - last)
    if keep:
        outs = [pltpu.VMEM((steps, wide, copies * slots), BF16)] * len(far) + outs
    if last:
        outs = outs + [pltpu.VMEM((1, copies * probes + TAIL, slots), BF16), pltpu.VMEM((probes, slots), F32)]
    if begin:
        outs = outs + [pltpu.VMEM((feature_rows(feat), copies * slots), BF16)]
    before = products if last or not keep else products[-1:]
    arrays = [near, levels, *far, *([] if begin else [right]), *before]
    if keep:
        arrays = [stay(array) for array in arrays]
    done = pl.pallas_call(
        functools.partial(apply_kernel, feat, group, keep, begin, last, len(far), len(before)),
        out_shape=outs,
        in_specs=[VMEM] * len(arrays),
        out_specs=[VMEM] * len(outs),
        scratch_shapes=[pltpu.VMEM((probes, copies * slots), F32)],
        compiler_params=pltpu.CompilerParams(vmem_limit_bytes=(16 if keep else 40) * 2**20),
    )(*arrays)
    done = list(done)
    kept, done = (done[: len(far)], done[len(far) :]) if keep else ([None] * len(far), done)
    parts = len(far) if keep else 1 - last
    products = products + done[:parts] if keep else done[:parts]
    return kept, products, done[parts:] if last else done[parts] if begin else right


def step_sums(images, copies, probes):
    tails = []
    for w_ref in images:
        for g in range(w_ref.shape[0]):
            parts = w_ref[g, copies * probes :, :].astype(F32)
            tails.append(parts[:8, :128] + parts[:8, 128:256] + parts[8:, :128])
    norm_now, curve = (sum(tail[at : at + 1] for tail in tails) for at in range(2))
    step_size = norm_now / curve
    norm_next = jnp.zeros_like(norm_now)
    guesses = [tail[5:6] for tail in tails]
    for tail, guess in zip(tails, guesses):
        apart = guess - step_size
        norm_next = norm_next + (tail[2:3] + apart * (2.0 * tail[3:4] + apart * tail[4:5]))
    few = jnp.concatenate([step_size, norm_next / norm_now, norm_next, jnp.zeros((5, 128), F32)], axis=0)
    scales = []
    for start in range(0, len(guesses), 120):
        some = guesses[start : start + 120]
        columns = turned(jnp.concatenate([few] + [step_size / guess for guess in some], axis=0), 128)[:probes]
        scales += [columns[:, at + 8 : at + 9] for at in range(len(some))]
    return *(columns[:, at : at + 1] for at in range(3)), scales


def second_kernel(feat, group, keep, copies, levels_ref, own_ref, own_image_in_ref, *refs):
    points, images, refs = refs[:PIECES], refs[PIECES : 2 * PIECES], refs[2 * PIECES :]
    if keep:
        kept, refs = refs[:PIECES], refs[PIECES:]
    (partial_ref, solution_ref, residual_ref, own_dir_ref, own_image_ref, norm_ref, product_ref, scale_ref) = refs[:8]
    if not keep:
        right_ref = refs[8]
    slots, probes = images[0].shape[2], own_image_in_ref.shape[0]
    pairs = list(zip(points, images))
    groups = images[0].shape[0]

    def column(wide):
        return jnp.sum(wide, axis=1, keepdims=True)

    step_size, ratio, norm_next, scales = step_sums(images, copies, probes)
    for at, scale in enumerate(scales):
        scale_ref[at] = jnp.broadcast_to(scale, (probes, 128))

    def residual_of(piece, b):
        first = points[piece][b, 2 * feat :, :].astype(F32)
        sent = images[piece][b // copies, pl.ds(pl.multiple_of(b % copies * probes, probes), probes), :].astype(F32)
        return first + scale_ref[piece * groups + b // copies][:, :1] * (sent - first), first

    def direct(piece, b):
        residual, first = residual_of(piece, b)
        return (residual + ratio * first).astype(BF16)

    first = own_ref[0, 2 * feat : 2 * feat + probes, :].astype(F32)
    right = first + own_ref[0, 2 * feat + probes :, :].astype(F32)
    residual = right - step_size * own_image_in_ref[...]
    own_direction = (residual + ratio * first).astype(BF16)
    solution_ref[...] = step_size * first
    residual_ref[...] = residual
    own_dir_ref[...] = own_direction.astype(F32)
    if not keep:
        fill_right(points[0], levels_ref, right_ref, feat)

    def step(piece, g):
        directions = [direct(piece, g * group + b) for b in range(group)]
        if piece == 0:
            directions[0] = jnp.where(g == 0, own_direction, directions[0])
        if keep:
            block = kept[piece][g]
        else:
            blocks = [points[piece][g * group + b, : 2 * feat, :] for b in range(group)]
            left = jnp.concatenate([features(block, None, True) for block in blocks], axis=1)
            block = entries(left, right_ref[...])
        return jnp.dot(jnp.concatenate(directions, axis=1), block, preferred_element_type=F32)

    steps = points[0].shape[0] // group
    if steps == 1:
        product = sum(step(piece, 0) for piece in range(PIECES))
    else:
        product_ref[...] = jnp.zeros_like(product_ref)

        def add(piece, g, carry):
            product_ref[...] += step(piece, g)
            return carry

        for piece in range(PIECES):
            lax.fori_loop(0, steps, functools.partial(add, piece), 0)
        product = product_ref[...]

    curve = jnp.zeros((probes, slots), F32)
    for b in range(copies):
        direction = (direct(0, b) if b else own_direction).astype(F32)
        image = product[:, b * slots : (b + 1) * slots] + levels_ref[1:2, :] * direction
        curve = curve + direction * image
        if b == 0:
            own_image_ref[...] = image
    lane = lax.broadcasted_iota(jnp.int32, (probes, 128), 1)
    flat = jnp.where(lane == 0, column(curve), 0.0)
    partial_ref[...] = turned(flat, 128)[:8]
    norm_ref[...] = jnp.broadcast_to(norm_next, norm_ref.shape)


def sent_product(sent_ref, kept_ref, copies):
    probes = (sent_ref.shape[1] - TAIL) // copies
    sent = jnp.concatenate([sent_ref[0, b * probes : (b + 1) * probes, :] for b in range(copies)], axis=1)
    return jnp.dot(sent, kept_ref[0], preferred_element_type=F32)


def again_kernel(copies, count, *refs):
    for sent_ref, kept_ref, out_ref in zip(refs[:count], refs[count : 2 * count], refs[2 * count :]):
        out_ref[...] = sent_product(sent_ref, kept_ref, copies)


def apply_again(sent, kept, copies):
    outs = [pltpu.VMEM(((sent[0].shape[1] - TAIL) // copies, kept[0].shape[2]), F32)] * len(sent)
    done = pl.pallas_call(
        functools.partial(again_kernel, copies, len(sent)),
        out_shape=outs,
        in_specs=[VMEM] * (2 * len(sent)),
        out_specs=[VMEM] * len(sent),
        compiler_params=pltpu.CompilerParams(vmem_limit_bytes=16 * 2**20),
    )(*[stay(array) for array in (*sent, *kept)])
    return list(done)


def combine_kernel(feat, copies, levels_ref, own_ref, own_image_in_ref, near_ref, kept_near_ref, *refs):
    images, firsts, refs = refs[:PIECES], refs[PIECES : 2 * PIECES], refs[2 * PIECES :]
    late = LATE
    agains, kept, outs = refs[: PIECES - late], refs[PIECES - late : PIECES], refs[PIECES:]
    partial_ref, solution_ref, residual_ref, own_dir_ref, own_image_ref, norm_ref = outs
    slots, probes = images[0].shape[2], own_image_in_ref.shape[0]
    agains = [again_ref[...] for again_ref in agains]
    for image_ref, kept_ref in zip(images[PIECES - late :], kept):
        agains.append(sent_product(image_ref, kept_ref, copies))
    step_size, ratio, norm_next, scales = step_sums(images, copies, probes)
    product = jnp.zeros((probes, copies * slots), F32)
    for first_ref, again, scale in zip(firsts, agains, scales):
        product = product + ((1.0 - scale + ratio) * first_ref[...] + scale * again)

    first = own_ref[0, 2 * feat : 2 * feat + probes, :].astype(F32)
    right = first + own_ref[0, 2 * feat + probes :, :].astype(F32)
    residual = right - step_size * own_image_in_ref[...]
    directions = [(residual + ratio * first).astype(BF16).astype(F32)]
    solution_ref[...] = step_size * first
    residual_ref[...] = residual
    own_dir_ref[...] = directions[0]
    for b in range(copies):
        first = near_ref[b, 2 * feat :, :].astype(F32)
        sent = images[0][0, b * probes : (b + 1) * probes, :].astype(F32)
        directions.append((1.0 - scales[0] + ratio) * first + scales[0] * sent)
    exact, formed = directions[:2]
    product = product + jnp.dot((exact - formed).astype(BF16), kept_near_ref[0, :slots, :], preferred_element_type=F32)
    curve = jnp.zeros((probes, slots), F32)
    for b, direction in enumerate([exact] + directions[2:]):
        image = product[:, b * slots : (b + 1) * slots] + levels_ref[1:2, :] * direction
        curve = curve + direction * image
        if b == 0:
            own_image_ref[...] = image
    lane = lax.broadcasted_iota(jnp.int32, (probes, 128), 1)
    flat = jnp.where(lane == 0, jnp.sum(curve, axis=1, keepdims=True), 0.0)
    partial_ref[...] = turned(flat, 128)[:8]
    norm_ref[...] = jnp.broadcast_to(norm_next, norm_ref.shape)


def combine(levels, own, own_image, near, images, products, agains, kept, copies, feat):
    probes, slots = own_image.shape
    one, small = pltpu.VMEM((probes, slots), F32), pltpu.VMEM((probes, 128), F32)
    arrays = [levels, own, own_image, near, kept[0], *images, *products, *agains, *kept[len(agains) :]]
    return pl.pallas_call(
        functools.partial(combine_kernel, feat, copies),
        out_shape=[pltpu.VMEM((8, 128), F32), one, one, one, one, small],
        in_specs=[VMEM] * len(arrays),
        out_specs=[VMEM] * 6,
        compiler_params=pltpu.CompilerParams(vmem_limit_bytes=16 * 2**20),
    )(*[stay(array) for array in arrays])


def second(levels, own, own_image, points, images, kept, copies, feat, group):
    keep = kept is not None
    slots, probes = own_image.shape[1], own_image.shape[0]
    one, small = pltpu.VMEM((probes, slots), F32), pltpu.VMEM((probes, 128), F32)
    scratch = [
        pltpu.VMEM((probes, copies * slots), F32),
        pltpu.VMEM((PIECES * images[0].shape[0], probes, 128), F32),
    ]
    arrays = [levels, own, own_image, *points, *images, *(kept or ())]
    if keep:
        arrays = [stay(array) for array in arrays]
    else:
        scratch.append(pltpu.VMEM((feature_rows(feat), copies * slots), BF16))
    return pl.pallas_call(
        functools.partial(second_kernel, feat, group, keep, copies),
        out_shape=[pltpu.VMEM((8, 128), F32), one, one, one, one, small],
        in_specs=[VMEM] * len(arrays),
        out_specs=[VMEM] * 6,
        scratch_shapes=scratch,
        compiler_params=pltpu.CompilerParams(vmem_limit_bytes=(16 if keep else 48) * 2**20),
    )(*arrays)


def finish_kernel(curve_ref, norm_ref, solution_ref, residual_ref, direction_ref, image_ref, out_ref, left_ref):
    probes = norm_ref.shape[0]
    curve = turned(curve_ref[...], 128)[:probes, :1]
    step_size = norm_ref[:, :1] / curve
    out_ref[...] = solution_ref[...] + step_size * direction_ref[...]
    left_ref[...] = residual_ref[...] - step_size * image_ref[...]


def gather(held, bits, count):
    for at in range(0, len(bits), 2):
        pair = bits[at : at + 2]
        flips = pair if len(pair) == 1 else [pair[0], sum(pair), pair[1]]
        held = jnp.concatenate([held] + [swap(held, flip, count) for flip in flips], axis=0)
    return held


def total(held, bits, count):
    for at in range(0, len(bits), 2):
        pair = bits[at : at + 2]
        flips = pair if len(pair) == 1 else [pair[0], pair[1], sum(pair)]
        held = sum([swap(held, flip, count) for flip in reversed(flips)], held)
    return held


def body(count, points, inv_lengths, signal_level, noise_level, right_sides, block_counts):
    slots, feat = points.shape
    probes = right_sides.shape[1]
    copies = COPIES
    while copies > 1 and (copies * PIECES > count or copies * count * slots * slots * 2 > KEEP_BYTES):
        copies //= 4
    group = math.gcd(count // PIECES, 8)
    keep = copies == group == count // PIECES and copies * count * slots * slots * 2 <= KEEP_BYTES
    bits = [1 << k for k in reversed(range(count.bit_length() - 1))]
    later = bits[copies.bit_length() - 1 :]
    one, two, core = bits[-3:]
    own = prepare(points, inv_lengths, right_sides, block_counts)
    own, signal_level, noise_level = lax.optimization_barrier((own, signal_level, noise_level))
    levels = jnp.stack([jnp.log(signal_level[0]) * LOG2E, noise_level[0]])
    levels = jnp.broadcast_to(levels[:, None], (2, slots))
    first = functools.partial(apply_first, feat=feat, group=group, keep=keep)

    held = gather(own, bits[:-3], count)
    held, levels = lax.optimization_barrier((held, levels))
    near = held[:copies]
    held = held[:, : 2 * feat + probes]
    beside = swap(held, core, count)
    up = swap_apart(held, one, two, core, count)
    kept_h, products, near_features = first(near, [held], levels, None, [])
    held_again, products[-1] = lax.optimization_barrier((held, products[-1]))
    over = swap_apart(held_again, two, one, core, count)
    kept_0, products, _ = first(near, [beside], levels, near_features, products)
    kept_0 = [*kept_h, *kept_0]
    up, products[-1] = lax.optimization_barrier((up, products[-1]))
    corner, up_beside = swap_apart(up, two, one, core, count), swap(up, core, count)
    kept_1, products, _ = first(near, [up], levels, near_features, products)
    over, products[-1] = lax.optimization_barrier((over, products[-1]))
    over_beside = swap(over, core, count)
    kept_2, products, _ = first(near, [up_beside, over], levels, near_features, products)
    corner, products[-1] = lax.optimization_barrier((corner, products[-1]))
    corner_beside = swap(corner, core, count)
    kept_3, products, _ = first(near, [over_beside, corner], levels, near_features, products)
    kept_4, products, (message, own_image) = first(near, [corner_beside], levels, near_features, products, last=True)
    pieces = [held, beside, up, up_beside, over, over_beside, corner, corner_beside]
    kept = [*kept_0, *kept_1, *kept_2, *kept_3, *kept_4]

    held = gather(message, later[:-3], count)
    beside, corner = swap(held, core, count), swap(held, one | two, count)
    up, over = swap_apart(held, one, two, core, count), swap_apart(held, two, one, core, count)
    if keep:
        again_0 = apply_again([held], kept[:1], copies)
        corner, again_0[0] = lax.optimization_barrier((corner, again_0[0]))
    corner_beside = swap(corner, core, count)
    if keep:
        again_1 = apply_again([beside, corner], [kept[1], kept[6]], copies)
        over, up, again_1[0] = lax.optimization_barrier((over, up, again_1[0]))
    up_beside, over_beside = (swap(array, core, count) for array in (up, over))
    if keep:
        again_2 = apply_again([corner_beside, up, over], [kept[7], kept[2], kept[4]], copies)
        images = [held, beside, corner, corner_beside, up, over, up_beside, over_beside]
        order = [0, 1, 6, 7, 2, 4, 3, 5]
        kept, products = ([each[at] for at in order] for each in (kept, products))
        agains = [*again_0, *again_1, *again_2]
        done = combine(levels, own, own_image, pieces[0], images, products, agains, kept, copies, feat)
    else:
        images = [held, beside, up, up_beside, over, over_beside, corner, corner_beside]
        done = second(levels, own, own_image, pieces, images, None, copies, feat, group)
    partial, solution, residual, direction, second_image, norm = done
    partial = partial + swap(partial, core, count)
    apart = swap_apart(partial, one, one | two, core, count)
    partial = partial + swap(partial, two, count) + (apart + swap(apart, core, count))
    partial = total(partial, later[:-3], count)
    done = jax.ShapeDtypeStruct((probes, slots), F32)
    solution, residual = pl.pallas_call(
        finish_kernel,
        out_shape=[done, done],
        in_specs=[VMEM] * 6,
        out_specs=[VMEM] * 2,
    )(*[stay(array) for array in (partial, norm, solution, residual, direction, second_image)])
    return solution.T, residual.T


def solution(mesh):
    count = math.prod(mesh.shape[axis] for axis in AXES)
    rows = P(AXES, None)
    return jax.shard_map(
        functools.partial(body, count),
        mesh=mesh,
        in_specs=(rows, P(), P(), P(), rows, P(AXES)),
        out_specs=(rows, rows),
        check_vma=False,
    )
```

```python
import functools
import math

import jax
import jax.numpy as jnp
from jax import lax
from jax.experimental import pallas as pl
from jax.experimental.pallas import tpu as pltpu
from jax.sharding import PartitionSpec as P

AXES = ("row", "col")
LOG2E = 1.0 / math.log(2.0)
FAR = 64.0
KEEP_BYTES = 20 * 2**20
COPIES = 4
PIECES = 8
TAIL = 16
LATE = 2
F32, BF16 = jnp.float32, jnp.bfloat16
VMEM = pl.BlockSpec(memory_space=pltpu.VMEM)


def stay(array):
    return pltpu.with_memory_space_constraint(array, pltpu.VMEM)


def swap(array, bit, count):
    return lax.ppermute(array, AXES, [(i, i ^ bit) for i in range(count)])


def two_parts(wide):
    high = wide.astype(BF16)
    return high, (wide - high.astype(F32)).astype(BF16)


def swap_apart(array, first, second, core, count):
    return lax.ppermute(array, AXES, [(i, i ^ (second if i & core else first)) for i in range(count)])


def three_parts(wide):
    high, _ = two_parts(wide)
    return high, *two_parts(wide - high.astype(F32))


def features(parts, level, left):
    feat = parts.shape[0] // 2
    high, low = parts[:feat], parts[feat:]
    scaled = high.astype(F32) + low.astype(F32)
    half = -0.5 * jnp.sum(scaled * scaled, axis=0, keepdims=True)
    if not left:
        half = half + level
    halves = [part.astype(F32) for part in three_parts(half)]
    ones = [jnp.ones_like(half)] * 3
    tail = (halves + ones if left else ones + halves) + [jnp.zeros((10, half.shape[1]), F32)]
    rows = [high, high, low, low] if left else [high, low, high, low]
    return jnp.concatenate(rows + [jnp.concatenate(tail, axis=0).astype(BF16)], axis=0)


def feature_rows(feat):
    return 4 * feat + 16


def prepare_kernel(points_ref, inv_ref, right_ref, count_ref, sent_ref):
    feat, slots = points_ref.shape
    probes = right_ref.shape[0]
    valid = lax.broadcasted_iota(jnp.int32, (1, slots), 1) < count_ref[0]
    row = lax.broadcasted_iota(jnp.int32, (feat, slots), 0)
    inverse = jnp.zeros((feat, slots), F32)
    for f in range(feat):
        inverse = jnp.where(row == f, inv_ref[f], inverse)
    scaled = points_ref[...] * inverse * math.sqrt(LOG2E)
    high, low = two_parts(jnp.where(valid, scaled, FAR))
    direction, rest = two_parts(jnp.where(valid, right_ref[...], 0.0))
    sent_ref[0, :feat, :] = high
    sent_ref[0, feat : 2 * feat, :] = low
    sent_ref[0, 2 * feat : 2 * feat + probes, :] = direction
    sent_ref[0, 2 * feat + probes :, :] = rest


def prepare(points, inv_lengths, right_sides, block_counts):
    smem = pl.BlockSpec(memory_space=pltpu.SMEM)
    return pl.pallas_call(
        prepare_kernel,
        out_shape=pltpu.VMEM((1, 2 * points.shape[1] + 2 * right_sides.shape[1], points.shape[0]), BF16),
        in_specs=[VMEM, smem, VMEM, smem],
        out_specs=VMEM,
    )(points.T, inv_lengths, right_sides.T, block_counts)


def fill_right(near_ref, levels_ref, right_ref, feat):
    blocks, slots = right_ref.shape[1] // near_ref.shape[2], near_ref.shape[2]
    for b in range(blocks):
        right_ref[:, b * slots : (b + 1) * slots] = features(near_ref[b, : 2 * feat, :], levels_ref[0:1, :], False)


def turned(rows, height):
    if rows.shape[0] < height:
        rows = jnp.concatenate([rows, jnp.zeros((height - rows.shape[0], rows.shape[1]), F32)], axis=0)
    return rows.T


def entries(left, right):
    powers = lax.dot_general(left, right, (((0,), (0,)), ((), ())), preferred_element_type=F32)
    return jnp.exp2(powers).astype(BF16)


def apply_kernel(feat, group, keep, begin, last, count, earlier, near_ref, levels_ref, *refs):
    far, refs = refs[:count], refs[count:]
    if begin:
        right_ref, refs = refs[-2], refs[:-2] + refs[-1:]
        fill_right(near_ref, levels_ref, right_ref, feat)
    else:
        right_ref, refs = refs[0], refs[1:]
    sum_ref, refs = refs[-1], refs[:-1]
    before, refs = refs[:earlier], refs[earlier:]
    kept, refs = (refs[:count], refs[count:]) if keep else ((), refs)
    products, refs = refs[: count if keep else 1 - last], refs[count if keep else 1 - last :]
    slots, probes = near_ref.shape[2], sum_ref.shape[0]

    def step(piece, g):
        blocks = [far[piece][g * group + b] for b in range(group)]
        left = jnp.concatenate([features(block[: 2 * feat], None, True) for block in blocks], axis=1)
        directions = jnp.concatenate([block[2 * feat :] for block in blocks], axis=1)
        block = entries(left, right_ref[...])
        if keep:
            kept[piece][g] = block
        return jnp.dot(directions, block, preferred_element_type=F32)

    if last:
        rough = sum([before_ref[...] for before_ref in before])
        firsts, rights = [], []
        norm = curve = jnp.zeros((probes, slots), F32)
        for b in range(near_ref.shape[0]):
            direction = near_ref[b, 2 * feat : 2 * feat + probes, :].astype(F32)
            right = direction + near_ref[b, 2 * feat + probes :, :].astype(F32)
            norm = norm + right * right
            curve = curve + direction * (rough[:, b * slots : (b + 1) * slots] + levels_ref[1:2, :] * direction)
            firsts.append(direction)
            rights.append(right)
        norm, curve = (jnp.sum(each, axis=1, keepdims=True) for each in (norm, curve))
        usual = 1.0 / (jnp.exp2(levels_ref[0:1, :1]) + levels_ref[1:2, :1])
        likely = (norm > 0.0) & (curve > 1e-6 * norm)
        guess = jnp.where(likely, norm / jnp.where(likely, curve, 1.0), usual)
        guess = jnp.clip(guess, 1e-6, 1e3).astype(BF16)
    steps = far[0].shape[0] // group
    if keep:
        done = [step(piece, 0) for piece in range(count)]
        for product_ref, product in zip(products, done):
            product_ref[...] = product
        if not last:
            return
        product = sum([before_ref[...] for before_ref in before], sum(done))
    else:
        sum_ref[...] = sum([before_ref[...] for before_ref in before], jnp.zeros(sum_ref.shape, F32))

        def add(piece, g, carry):
            sum_ref[...] += step(piece, g)
            return carry

        for piece in range(count):
            lax.fori_loop(0, steps, functools.partial(add, piece), 0)
        product = sum_ref[...]
        if not last:
            products[0][...] = product
            return
    out_ref, own_ref = refs
    images = [product[:, b * slots : (b + 1) * slots] + levels_ref[1:2, :] * first for b, first in enumerate(firsts)]
    own_ref[...] = images[0]
    steps = [right - guess.astype(F32) * image for image, right in zip(images, rights)]
    for b, after in enumerate(steps):
        out_ref[0, b * probes : (b + 1) * probes, :] = after.astype(BF16)
    products = [[x * y for x, y in zip(*pair)] for pair in ((steps, steps), (steps, images), (images, images))]
    products.append([first * image for first, image in zip(firsts, images)])
    after_after, after_image, image_image, curve = (jnp.sum(sum(each), axis=1, keepdims=True) for each in products)
    sums = [norm, curve, after_after, after_image, image_image]
    lane = lax.broadcasted_iota(jnp.int32, (probes, 128), 1)
    flat = jnp.zeros((probes, 128), F32)
    for at, each in enumerate([*sums, guess.astype(F32)]):
        flat = jnp.where(lane == at, each, flat)
    high, middle, low = (part.astype(F32) for part in three_parts(turned(flat, 128)[:8]))
    rows = jnp.concatenate([jnp.concatenate([high, middle], axis=1), jnp.concatenate([low, jnp.zeros_like(low)], axis=1)])
    if slots > 256:
        rows = jnp.concatenate([rows, jnp.zeros((TAIL, slots - 256), F32)], axis=1)
    out_ref[0, len(images) * probes :, :] = rows.astype(BF16)


def apply_first(near, far, levels, right, products, feat, group, keep, last=False):
    copies, slots, probes = near.shape[0], near.shape[2], far[0].shape[1] - 2 * feat
    wide, steps, begin = group * slots, far[0].shape[0] // group, right is None
    product = pltpu.VMEM((probes, copies * slots), F32)
    outs = [product] * (len(far) if keep else 1 - last)
    if keep:
        outs = [pltpu.VMEM((steps, wide, copies * slots), BF16)] * len(far) + outs
    if last:
        outs = outs + [pltpu.VMEM((1, copies * probes + TAIL, slots), BF16), pltpu.VMEM((probes, slots), F32)]
    if begin:
        outs = outs + [pltpu.VMEM((feature_rows(feat), copies * slots), BF16)]
    before = products if last or not keep else products[-1:]
    arrays = [near, levels, *far, *([] if begin else [right]), *before]
    if keep:
        arrays = [stay(array) for array in arrays]
    done = pl.pallas_call(
        functools.partial(apply_kernel, feat, group, keep, begin, last, len(far), len(before)),
        out_shape=outs,
        in_specs=[VMEM] * len(arrays),
        out_specs=[VMEM] * len(outs),
        scratch_shapes=[pltpu.VMEM((probes, copies * slots), F32)],
        compiler_params=pltpu.CompilerParams(vmem_limit_bytes=(16 if keep else 40) * 2**20),
    )(*arrays)
    done = list(done)
    kept, done = (done[: len(far)], done[len(far) :]) if keep else ([None] * len(far), done)
    parts = len(far) if keep else 1 - last
    products = products + done[:parts] if keep else done[:parts]
    return kept, products, done[parts:] if last else done[parts] if begin else right


def step_sums(images, copies, probes):
    tails = []
    for w_ref in images:
        for g in range(w_ref.shape[0]):
            parts = w_ref[g, copies * probes :, :].astype(F32)
            tails.append(parts[:8, :128] + parts[:8, 128:256] + parts[8:, :128])
    norm_now, curve = (sum(tail[at : at + 1] for tail in tails) for at in range(2))
    step_size = norm_now / curve
    norm_next = jnp.zeros_like(norm_now)
    guesses = [tail[5:6] for tail in tails]
    for tail, guess in zip(tails, guesses):
        apart = guess - step_size
        norm_next = norm_next + (tail[2:3] + apart * (2.0 * tail[3:4] + apart * tail[4:5]))
    few = jnp.concatenate([step_size, norm_next / norm_now, norm_next, jnp.zeros((5, 128), F32)], axis=0)
    scales = []
    for start in range(0, len(guesses), 120):
        some = guesses[start : start + 120]
        columns = turned(jnp.concatenate([few] + [step_size / guess for guess in some], axis=0), 128)[:probes]
        scales += [columns[:, at + 8 : at + 9] for at in range(len(some))]
    return *(columns[:, at : at + 1] for at in range(3)), scales


def second_kernel(feat, group, keep, copies, levels_ref, own_ref, own_image_in_ref, *refs):
    points, images, refs = refs[:PIECES], refs[PIECES : 2 * PIECES], refs[2 * PIECES :]
    if keep:
        kept, refs = refs[:PIECES], refs[PIECES:]
    (partial_ref, solution_ref, residual_ref, own_dir_ref, own_image_ref, norm_ref, product_ref, scale_ref) = refs[:8]
    if not keep:
        right_ref = refs[8]
    slots, probes = images[0].shape[2], own_image_in_ref.shape[0]
    pairs = list(zip(points, images))
    groups = images[0].shape[0]

    def column(wide):
        return jnp.sum(wide, axis=1, keepdims=True)

    step_size, ratio, norm_next, scales = step_sums(images, copies, probes)
    for at, scale in enumerate(scales):
        scale_ref[at] = jnp.broadcast_to(scale, (probes, 128))

    def residual_of(piece, b):
        first = points[piece][b, 2 * feat :, :].astype(F32)
        sent = images[piece][b // copies, pl.ds(pl.multiple_of(b % copies * probes, probes), probes), :].astype(F32)
        return first + scale_ref[piece * groups + b // copies][:, :1] * (sent - first), first

    def direct(piece, b):
        residual, first = residual_of(piece, b)
        return (residual + ratio * first).astype(BF16)

    first = own_ref[0, 2 * feat : 2 * feat + probes, :].astype(F32)
    right = first + own_ref[0, 2 * feat + probes :, :].astype(F32)
    residual = right - step_size * own_image_in_ref[...]
    own_direction = (residual + ratio * first).astype(BF16)
    solution_ref[...] = step_size * first
    residual_ref[...] = residual
    own_dir_ref[...] = own_direction.astype(F32)
    if not keep:
        fill_right(points[0], levels_ref, right_ref, feat)

    def step(piece, g):
        directions = [direct(piece, g * group + b) for b in range(group)]
        if piece == 0:
            directions[0] = jnp.where(g == 0, own_direction, directions[0])
        if keep:
            block = kept[piece][g]
        else:
            blocks = [points[piece][g * group + b, : 2 * feat, :] for b in range(group)]
            left = jnp.concatenate([features(block, None, True) for block in blocks], axis=1)
            block = entries(left, right_ref[...])
        return jnp.dot(jnp.concatenate(directions, axis=1), block, preferred_element_type=F32)

    steps = points[0].shape[0] // group
    if steps == 1:
        product = sum(step(piece, 0) for piece in range(PIECES))
    else:
        product_ref[...] = jnp.zeros_like(product_ref)

        def add(piece, g, carry):
            product_ref[...] += step(piece, g)
            return carry

        for piece in range(PIECES):
            lax.fori_loop(0, steps, functools.partial(add, piece), 0)
        product = product_ref[...]

    curve = jnp.zeros((probes, slots), F32)
    for b in range(copies):
        direction = (direct(0, b) if b else own_direction).astype(F32)
        image = product[:, b * slots : (b + 1) * slots] + levels_ref[1:2, :] * direction
        curve = curve + direction * image
        if b == 0:
            own_image_ref[...] = image
    lane = lax.broadcasted_iota(jnp.int32, (probes, 128), 1)
    flat = jnp.where(lane == 0, column(curve), 0.0)
    partial_ref[...] = turned(flat, 128)[:8]
    norm_ref[...] = jnp.broadcast_to(norm_next, norm_ref.shape)


def sent_product(sent_ref, kept_ref, copies):
    probes = (sent_ref.shape[1] - TAIL) // copies
    sent = jnp.concatenate([sent_ref[0, b * probes : (b + 1) * probes, :] for b in range(copies)], axis=1)
    return jnp.dot(sent, kept_ref[0], preferred_element_type=F32)


def again_kernel(copies, count, *refs):
    for sent_ref, kept_ref, out_ref in zip(refs[:count], refs[count : 2 * count], refs[2 * count :]):
        out_ref[...] = sent_product(sent_ref, kept_ref, copies)


def apply_again(sent, kept, copies):
    outs = [pltpu.VMEM(((sent[0].shape[1] - TAIL) // copies, kept[0].shape[2]), F32)] * len(sent)
    done = pl.pallas_call(
        functools.partial(again_kernel, copies, len(sent)),
        out_shape=outs,
        in_specs=[VMEM] * (2 * len(sent)),
        out_specs=[VMEM] * len(sent),
        compiler_params=pltpu.CompilerParams(vmem_limit_bytes=16 * 2**20),
    )(*[stay(array) for array in (*sent, *kept)])
    return list(done)


def combine_kernel(feat, copies, levels_ref, own_ref, own_image_in_ref, near_ref, kept_near_ref, *refs):
    images, firsts, refs = refs[:PIECES], refs[PIECES : 2 * PIECES], refs[2 * PIECES :]
    late = LATE
    agains, kept, outs = refs[: PIECES - late], refs[PIECES - late : PIECES], refs[PIECES:]
    partial_ref, solution_ref, residual_ref, own_dir_ref, own_image_ref, norm_ref = outs
    slots, probes = images[0].shape[2], own_image_in_ref.shape[0]
    agains = [again_ref[...] for again_ref in agains]
    for image_ref, kept_ref in zip(images[PIECES - late :], kept):
        agains.append(sent_product(image_ref, kept_ref, copies))
    step_size, ratio, norm_next, scales = step_sums(images, copies, probes)
    product = jnp.zeros((probes, copies * slots), F32)
    for first_ref, again, scale in zip(firsts, agains, scales):
        product = product + ((1.0 - scale + ratio) * first_ref[...] + scale * again)

    first = own_ref[0, 2 * feat : 2 * feat + probes, :].astype(F32)
    right = first + own_ref[0, 2 * feat + probes :, :].astype(F32)
    residual = right - step_size * own_image_in_ref[...]
    directions = [(residual + ratio * first).astype(BF16).astype(F32)]
    solution_ref[...] = step_size * first
    residual_ref[...] = residual
    own_dir_ref[...] = directions[0]
    for b in range(copies):
        first = near_ref[b, 2 * feat :, :].astype(F32)
        sent = images[0][0, b * probes : (b + 1) * probes, :].astype(F32)
        directions.append((1.0 - scales[0] + ratio) * first + scales[0] * sent)
    exact, formed = directions[:2]
    product = product + jnp.dot((exact - formed).astype(BF16), kept_near_ref[0, :slots, :], preferred_element_type=F32)
    curve = jnp.zeros((probes, slots), F32)
    for b, direction in enumerate([exact] + directions[2:]):
        image = product[:, b * slots : (b + 1) * slots] + levels_ref[1:2, :] * direction
        curve = curve + direction * image
        if b == 0:
            own_image_ref[...] = image
    lane = lax.broadcasted_iota(jnp.int32, (probes, 128), 1)
    flat = jnp.where(lane == 0, jnp.sum(curve, axis=1, keepdims=True), 0.0)
    partial_ref[...] = turned(flat, 128)[:8]
    norm_ref[...] = jnp.broadcast_to(norm_next, norm_ref.shape)


def combine(levels, own, own_image, near, images, products, agains, kept, copies, feat):
    probes, slots = own_image.shape
    one, small = pltpu.VMEM((probes, slots), F32), pltpu.VMEM((probes, 128), F32)
    arrays = [levels, own, own_image, near, kept[0], *images, *products, *agains, *kept[len(agains) :]]
    return pl.pallas_call(
        functools.partial(combine_kernel, feat, copies),
        out_shape=[pltpu.VMEM((8, 128), F32), one, one, one, one, small],
        in_specs=[VMEM] * len(arrays),
        out_specs=[VMEM] * 6,
        compiler_params=pltpu.CompilerParams(vmem_limit_bytes=16 * 2**20),
    )(*[stay(array) for array in arrays])


def second(levels, own, own_image, points, images, kept, copies, feat, group):
    keep = kept is not None
    slots, probes = own_image.shape[1], own_image.shape[0]
    one, small = pltpu.VMEM((probes, slots), F32), pltpu.VMEM((probes, 128), F32)
    scratch = [
        pltpu.VMEM((probes, copies * slots), F32),
        pltpu.VMEM((PIECES * images[0].shape[0], probes, 128), F32),
    ]
    arrays = [levels, own, own_image, *points, *images, *(kept or ())]
    if keep:
        arrays = [stay(array) for array in arrays]
    else:
        scratch.append(pltpu.VMEM((feature_rows(feat), copies * slots), BF16))
    return pl.pallas_call(
        functools.partial(second_kernel, feat, group, keep, copies),
        out_shape=[pltpu.VMEM((8, 128), F32), one, one, one, one, small],
        in_specs=[VMEM] * len(arrays),
        out_specs=[VMEM] * 6,
        scratch_shapes=scratch,
        compiler_params=pltpu.CompilerParams(vmem_limit_bytes=(16 if keep else 48) * 2**20),
    )(*arrays)


def finish_kernel(curve_ref, norm_ref, solution_ref, residual_ref, direction_ref, image_ref, out_ref, left_ref):
    probes = norm_ref.shape[0]
    curve = turned(curve_ref[...], 128)[:probes, :1]
    step_size = norm_ref[:, :1] / curve
    out_ref[...] = solution_ref[...] + step_size * direction_ref[...]
    left_ref[...] = residual_ref[...] - step_size * image_ref[...]


def gather(held, bits, count):
    for at in range(0, len(bits), 2):
        pair = bits[at : at + 2]
        flips = pair if len(pair) == 1 else [pair[0], sum(pair), pair[1]]
        held = jnp.concatenate([held] + [swap(held, flip, count) for flip in flips], axis=0)
    return held


def total(held, bits, count):
    for at in range(0, len(bits), 2):
        pair = bits[at : at + 2]
        flips = pair if len(pair) == 1 else [pair[0], pair[1], sum(pair)]
        held = sum([swap(held, flip, count) for flip in reversed(flips)], held)
    return held


def body(count, points, inv_lengths, signal_level, noise_level, right_sides, block_counts):
    slots, feat = points.shape
    probes = right_sides.shape[1]
    copies = COPIES
    while copies > 1 and (copies * PIECES > count or copies * count * slots * slots * 2 > KEEP_BYTES):
        copies //= 4
    group = math.gcd(count // PIECES, 8)
    keep = copies == group == count // PIECES and copies * count * slots * slots * 2 <= KEEP_BYTES
    bits = [1 << k for k in reversed(range(count.bit_length() - 1))]
    later = bits[copies.bit_length() - 1 :]
    one, two, core = bits[-3:]
    own = prepare(points, inv_lengths, right_sides, block_counts)
    own, signal_level, noise_level = lax.optimization_barrier((own, signal_level, noise_level))
    levels = jnp.stack([jnp.log(signal_level[0]) * LOG2E, noise_level[0]])
    levels = jnp.broadcast_to(levels[:, None], (2, slots))
    first = functools.partial(apply_first, feat=feat, group=group, keep=keep)

    held = gather(own, bits[:-3], count)
    held, levels = lax.optimization_barrier((held, levels))
    near = held[:copies]
    held = held[:, : 2 * feat + probes]
    beside = swap(held, core, count)
    up = swap_apart(held, one, two, core, count)
    kept_h, products, near_features = first(near, [held], levels, None, [])
    held_again, products[-1] = lax.optimization_barrier((held, products[-1]))
    over = swap_apart(held_again, two, one, core, count)
    kept_0, products, _ = first(near, [beside], levels, near_features, products)
    kept_0 = [*kept_h, *kept_0]
    up, products[-1] = lax.optimization_barrier((up, products[-1]))
    corner, up_beside = swap_apart(up, two, one, core, count), swap(up, core, count)
    kept_1, products, _ = first(near, [up], levels, near_features, products)
    over, products[-1] = lax.optimization_barrier((over, products[-1]))
    over_beside = swap(over, core, count)
    kept_2, products, _ = first(near, [up_beside, over], levels, near_features, products)
    corner, products[-1] = lax.optimization_barrier((corner, products[-1]))
    corner_beside = swap(corner, core, count)
    kept_3, products, _ = first(near, [over_beside, corner], levels, near_features, products)
    kept_4, products, (message, own_image) = first(near, [corner_beside], levels, near_features, products, last=True)
    pieces = [held, beside, up, up_beside, over, over_beside, corner, corner_beside]
    kept = [*kept_0, *kept_1, *kept_2, *kept_3, *kept_4]

    held = gather(message, later[:-3], count)
    beside, corner = swap(held, core, count), swap(held, one | two, count)
    up, over = swap_apart(held, one, two, core, count), swap_apart(held, two, one, core, count)
    if keep:
        again_0 = apply_again([held], kept[:1], copies)
        corner, again_0[0] = lax.optimization_barrier((corner, again_0[0]))
    corner_beside = swap(corner, core, count)
    if keep:
        again_1 = apply_again([beside, corner], [kept[1], kept[6]], copies)
        over, up, again_1[0] = lax.optimization_barrier((over, up, again_1[0]))
    up_beside, over_beside = (swap(array, core, count) for array in (up, over))
    if keep:
        again_2 = apply_again([corner_beside, up, over], [kept[7], kept[2], kept[4]], copies)
        images = [held, beside, corner, corner_beside, up, over, up_beside, over_beside]
        order = [0, 1, 6, 7, 2, 4, 3, 5]
        kept, products = ([each[at] for at in order] for each in (kept, products))
        agains = [*again_0, *again_1, *again_2]
        done = combine(levels, own, own_image, pieces[0], images, products, agains, kept, copies, feat)
    else:
        images = [held, beside, up, up_beside, over, over_beside, corner, corner_beside]
        done = second(levels, own, own_image, pieces, images, None, copies, feat, group)
    partial, solution, residual, direction, second_image, norm = done
    partial = partial + swap(partial, core, count)
    apart = swap_apart(partial, one, one | two, core, count)
    partial = partial + swap(partial, two, count) + (apart + swap(apart, core, count))
    partial = total(partial, later[:-3], count)
    done = jax.ShapeDtypeStruct((probes, slots), F32)
    solution, residual = pl.pallas_call(
        finish_kernel,
        out_shape=[done, done],
        in_specs=[VMEM] * 6,
        out_specs=[VMEM] * 2,
    )(*[stay(array) for array in (partial, norm, solution, residual, direction, second_image)])
    return solution.T, residual.T


def solution(mesh):
    count = math.prod(mesh.shape[axis] for axis in AXES)
    rows = P(AXES, None)
    return jax.shard_map(
        functools.partial(body, count),
        mesh=mesh,
        in_specs=(rows, P(), P(), P(), rows, P(AXES)),
        out_specs=(rows, rows),
        check_vma=False,
    )
```

```python
import functools
import math

import jax
import jax.numpy as jnp
from jax import lax
from jax.experimental import pallas as pl
from jax.experimental.pallas import tpu as pltpu
from jax.sharding import PartitionSpec as P

AXES = ("row", "col")
LOG2E = 1.0 / math.log(2.0)
FAR = 64.0
KEEP_BYTES = 20 * 2**20
COPIES = 4
PIECES = 8
TAIL = 16
LATE = 2
F32, BF16 = jnp.float32, jnp.bfloat16
VMEM = pl.BlockSpec(memory_space=pltpu.VMEM)


def stay(array):
    return pltpu.with_memory_space_constraint(array, pltpu.VMEM)


def swap(array, bit, count):
    return lax.ppermute(array, AXES, [(i, i ^ bit) for i in range(count)])


def two_parts(wide):
    high = wide.astype(BF16)
    return high, (wide - high.astype(F32)).astype(BF16)


def swap_apart(array, first, second, core, count):
    return lax.ppermute(array, AXES, [(i, i ^ (second if i & core else first)) for i in range(count)])


def three_parts(wide):
    high, _ = two_parts(wide)
    return high, *two_parts(wide - high.astype(F32))


def features(parts, level, left):
    feat = parts.shape[0] // 2
    high, low = parts[:feat], parts[feat:]
    scaled = high.astype(F32) + low.astype(F32)
    half = -0.5 * jnp.sum(scaled * scaled, axis=0, keepdims=True)
    if not left:
        half = half + level
    halves = [part.astype(F32) for part in three_parts(half)]
    ones = [jnp.ones_like(half)] * 3
    tail = (halves + ones if left else ones + halves) + [jnp.zeros((10, half.shape[1]), F32)]
    rows = [high, high, low, low] if left else [high, low, high, low]
    return jnp.concatenate(rows + [jnp.concatenate(tail, axis=0).astype(BF16)], axis=0)


def feature_rows(feat):
    return 4 * feat + 16


def prepare_kernel(points_ref, inv_ref, right_ref, count_ref, sent_ref):
    feat, slots = points_ref.shape
    probes = right_ref.shape[0]
    valid = lax.broadcasted_iota(jnp.int32, (1, slots), 1) < count_ref[0]
    row = lax.broadcasted_iota(jnp.int32, (feat, slots), 0)
    inverse = jnp.zeros((feat, slots), F32)
    for f in range(feat):
        inverse = jnp.where(row == f, inv_ref[f], inverse)
    scaled = points_ref[...] * inverse * math.sqrt(LOG2E)
    high, low = two_parts(jnp.where(valid, scaled, FAR))
    direction, rest = two_parts(jnp.where(valid, right_ref[...], 0.0))
    sent_ref[0, :feat, :] = high
    sent_ref[0, feat : 2 * feat, :] = low
    sent_ref[0, 2 * feat : 2 * feat + probes, :] = direction
    sent_ref[0, 2 * feat + probes :, :] = rest


def prepare(points, inv_lengths, right_sides, block_counts):
    smem = pl.BlockSpec(memory_space=pltpu.SMEM)
    return pl.pallas_call(
        prepare_kernel,
        out_shape=pltpu.VMEM((1, 2 * points.shape[1] + 2 * right_sides.shape[1], points.shape[0]), BF16),
        in_specs=[VMEM, smem, VMEM, smem],
        out_specs=VMEM,
    )(points.T, inv_lengths, right_sides.T, block_counts)


def fill_right(near_ref, levels_ref, right_ref, feat):
    blocks, slots = right_ref.shape[1] // near_ref.shape[2], near_ref.shape[2]
    for b in range(blocks):
        right_ref[:, b * slots : (b + 1) * slots] = features(near_ref[b, : 2 * feat, :], levels_ref[0:1, :], False)


def turned(rows, height):
    if rows.shape[0] < height:
        rows = jnp.concatenate([rows, jnp.zeros((height - rows.shape[0], rows.shape[1]), F32)], axis=0)
    return rows.T


def entries(left, right):
    powers = lax.dot_general(left, right, (((0,), (0,)), ((), ())), preferred_element_type=F32)
    return jnp.exp2(powers).astype(BF16)


def apply_kernel(feat, group, keep, begin, last, count, earlier, near_ref, levels_ref, *refs):
    far, refs = refs[:count], refs[count:]
    if begin:
        right_ref, refs = refs[-2], refs[:-2] + refs[-1:]
        fill_right(near_ref, levels_ref, right_ref, feat)
    else:
        right_ref, refs = refs[0], refs[1:]
    sum_ref, refs = refs[-1], refs[:-1]
    before, refs = refs[:earlier], refs[earlier:]
    kept, refs = (refs[:count], refs[count:]) if keep else ((), refs)
    products, refs = refs[: count if keep else 1 - last], refs[count if keep else 1 - last :]
    slots, probes = near_ref.shape[2], sum_ref.shape[0]

    def step(piece, g):
        blocks = [far[piece][g * group + b] for b in range(group)]
        left = jnp.concatenate([features(block[: 2 * feat], None, True) for block in blocks], axis=1)
        directions = jnp.concatenate([block[2 * feat :] for block in blocks], axis=1)
        block = entries(left, right_ref[...])
        if keep:
            kept[piece][g] = block
        return jnp.dot(directions, block, preferred_element_type=F32)

    steps = far[0].shape[0] // group
    if keep:
        done = [step(piece, 0) for piece in range(count)]
        for product_ref, product in zip(products, done):
            product_ref[...] = product
        if not last:
            return
        product = sum([before_ref[...] for before_ref in before], sum(done))
    else:
        sum_ref[...] = sum([before_ref[...] for before_ref in before], jnp.zeros(sum_ref.shape, F32))

        def add(piece, g, carry):
            sum_ref[...] += step(piece, g)
            return carry

        for piece in range(count):
            lax.fori_loop(0, steps, functools.partial(add, piece), 0)
        product = sum_ref[...]
        if not last:
            products[0][...] = product
            return
    out_ref, own_ref = refs
    images, rights = [], []
    norm = curve = jnp.zeros((probes, slots), F32)
    for b in range(near_ref.shape[0]):
        direction = near_ref[b, 2 * feat : 2 * feat + probes, :].astype(F32)
        right = direction + near_ref[b, 2 * feat + probes :, :].astype(F32)
        image = product[:, b * slots : (b + 1) * slots] + levels_ref[1:2, :] * direction
        norm = norm + right * right
        curve = curve + direction * image
        images.append(image)
        rights.append(right)
    own_ref[...] = images[0]
    norm, curve = (jnp.sum(each, axis=1, keepdims=True) for each in (norm, curve))
    usual = 1.0 / (jnp.exp2(levels_ref[0:1, :1]) + levels_ref[1:2, :1])
    likely = (norm > 0.0) & (curve > 1e-6 * norm)
    guess = jnp.where(likely, norm / jnp.where(likely, curve, 1.0), usual)
    guess = jnp.clip(guess, 1e-6, 1e3).astype(BF16)
    steps = [right - guess.astype(F32) * image for image, right in zip(images, rights)]
    for b, after in enumerate(steps):
        out_ref[0, b * probes : (b + 1) * probes, :] = after.astype(BF16)
    products = [[x * y for x, y in zip(*pair)] for pair in ((steps, steps), (steps, images), (images, images))]
    sums = [norm, curve] + [jnp.sum(sum(each), axis=1, keepdims=True) for each in products]
    lane = lax.broadcasted_iota(jnp.int32, (probes, 128), 1)
    flat = jnp.zeros((probes, 128), F32)
    for at, each in enumerate([*sums, guess.astype(F32)]):
        flat = jnp.where(lane == at, each, flat)
    high, middle, low = (part.astype(F32) for part in three_parts(turned(flat, 128)[:8]))
    rows = jnp.concatenate([jnp.concatenate([high, middle], axis=1), jnp.concatenate([low, jnp.zeros_like(low)], axis=1)])
    if slots > 256:
        rows = jnp.concatenate([rows, jnp.zeros((TAIL, slots - 256), F32)], axis=1)
    out_ref[0, len(images) * probes :, :] = rows.astype(BF16)


def apply_first(near, far, levels, right, products, feat, group, keep, last=False):
    copies, slots, probes = near.shape[0], near.shape[2], far[0].shape[1] - 2 * feat
    wide, steps, begin = group * slots, far[0].shape[0] // group, right is None
    product = pltpu.VMEM((probes, copies * slots), F32)
    outs = [product] * (len(far) if keep else 1 - last)
    if keep:
        outs = [pltpu.VMEM((steps, wide, copies * slots), BF16)] * len(far) + outs
    if last:
        outs = outs + [pltpu.VMEM((1, copies * probes + TAIL, slots), BF16), pltpu.VMEM((probes, slots), F32)]
    if begin:
        outs = outs + [pltpu.VMEM((feature_rows(feat), copies * slots), BF16)]
    before = products if last or not keep else products[-1:]
    arrays = [near, levels, *far, *([] if begin else [right]), *before]
    if keep:
        arrays = [stay(array) for array in arrays]
    done = pl.pallas_call(
        functools.partial(apply_kernel, feat, group, keep, begin, last, len(far), len(before)),
        out_shape=outs,
        in_specs=[VMEM] * len(arrays),
        out_specs=[VMEM] * len(outs),
        scratch_shapes=[pltpu.VMEM((probes, copies * slots), F32)],
        compiler_params=pltpu.CompilerParams(vmem_limit_bytes=(16 if keep else 40) * 2**20),
    )(*arrays)
    done = list(done)
    kept, done = (done[: len(far)], done[len(far) :]) if keep else ([None] * len(far), done)
    parts = len(far) if keep else 1 - last
    products = products + done[:parts] if keep else done[:parts]
    return kept, products, done[parts:] if last else done[parts] if begin else right


def step_sums(images, copies, probes):
    tails = []
    for w_ref in images:
        for g in range(w_ref.shape[0]):
            parts = w_ref[g, copies * probes :, :].astype(F32)
            tails.append(parts[:8, :128] + parts[:8, 128:256] + parts[8:, :128])
    norm_now, curve = (sum(tail[at : at + 1] for tail in tails) for at in range(2))
    step_size = norm_now / curve
    norm_next = jnp.zeros_like(norm_now)
    guesses = [tail[5:6] for tail in tails]
    for tail, guess in zip(tails, guesses):
        apart = guess - step_size
        norm_next = norm_next + (tail[2:3] + apart * (2.0 * tail[3:4] + apart * tail[4:5]))
    few = jnp.concatenate([step_size, norm_next / norm_now, norm_next, jnp.zeros((5, 128), F32)], axis=0)
    scales = []
    for start in range(0, len(guesses), 120):
        some = guesses[start : start + 120]
        columns = turned(jnp.concatenate([few] + [step_size / guess for guess in some], axis=0), 128)[:probes]
        scales += [columns[:, at + 8 : at + 9] for at in range(len(some))]
    return *(columns[:, at : at + 1] for at in range(3)), scales


def second_kernel(feat, group, keep, copies, levels_ref, own_ref, own_image_in_ref, *refs):
    points, images, refs = refs[:PIECES], refs[PIECES : 2 * PIECES], refs[2 * PIECES :]
    if keep:
        kept, refs = refs[:PIECES], refs[PIECES:]
    (partial_ref, solution_ref, residual_ref, own_dir_ref, own_image_ref, norm_ref, product_ref, scale_ref) = refs[:8]
    if not keep:
        right_ref = refs[8]
    slots, probes = images[0].shape[2], own_image_in_ref.shape[0]
    pairs = list(zip(points, images))
    groups = images[0].shape[0]

    def column(wide):
        return jnp.sum(wide, axis=1, keepdims=True)

    step_size, ratio, norm_next, scales = step_sums(images, copies, probes)
    for at, scale in enumerate(scales):
        scale_ref[at] = jnp.broadcast_to(scale, (probes, 128))

    def residual_of(piece, b):
        first = points[piece][b, 2 * feat :, :].astype(F32)
        sent = images[piece][b // copies, pl.ds(pl.multiple_of(b % copies * probes, probes), probes), :].astype(F32)
        return first + scale_ref[piece * groups + b // copies][:, :1] * (sent - first), first

    def direct(piece, b):
        residual, first = residual_of(piece, b)
        return (residual + ratio * first).astype(BF16)

    first = own_ref[0, 2 * feat : 2 * feat + probes, :].astype(F32)
    right = first + own_ref[0, 2 * feat + probes :, :].astype(F32)
    residual = right - step_size * own_image_in_ref[...]
    own_direction = (residual + ratio * first).astype(BF16)
    solution_ref[...] = step_size * first
    residual_ref[...] = residual
    own_dir_ref[...] = own_direction.astype(F32)
    if not keep:
        fill_right(points[0], levels_ref, right_ref, feat)

    def step(piece, g):
        directions = [direct(piece, g * group + b) for b in range(group)]
        if piece == 0:
            directions[0] = jnp.where(g == 0, own_direction, directions[0])
        if keep:
            block = kept[piece][g]
        else:
            blocks = [points[piece][g * group + b, : 2 * feat, :] for b in range(group)]
            left = jnp.concatenate([features(block, None, True) for block in blocks], axis=1)
            block = entries(left, right_ref[...])
        return jnp.dot(jnp.concatenate(directions, axis=1), block, preferred_element_type=F32)

    steps = points[0].shape[0] // group
    if steps == 1:
        product = sum(step(piece, 0) for piece in range(PIECES))
    else:
        product_ref[...] = jnp.zeros_like(product_ref)

        def add(piece, g, carry):
            product_ref[...] += step(piece, g)
            return carry

        for piece in range(PIECES):
            lax.fori_loop(0, steps, functools.partial(add, piece), 0)
        product = product_ref[...]

    curve = jnp.zeros((probes, slots), F32)
    for b in range(copies):
        direction = (direct(0, b) if b else own_direction).astype(F32)
        image = product[:, b * slots : (b + 1) * slots] + levels_ref[1:2, :] * direction
        curve = curve + direction * image
        if b == 0:
            own_image_ref[...] = image
    lane = lax.broadcasted_iota(jnp.int32, (probes, 128), 1)
    flat = jnp.where(lane == 0, column(curve), 0.0)
    partial_ref[...] = turned(flat, 128)[:8]
    norm_ref[...] = jnp.broadcast_to(norm_next, norm_ref.shape)


def sent_product(sent_ref, kept_ref, copies):
    probes = (sent_ref.shape[1] - TAIL) // copies
    sent = jnp.concatenate([sent_ref[0, b * probes : (b + 1) * probes, :] for b in range(copies)], axis=1)
    return jnp.dot(sent, kept_ref[0], preferred_element_type=F32)


def again_kernel(copies, count, *refs):
    for sent_ref, kept_ref, out_ref in zip(refs[:count], refs[count : 2 * count], refs[2 * count :]):
        out_ref[...] = sent_product(sent_ref, kept_ref, copies)


def apply_again(sent, kept, copies):
    outs = [pltpu.VMEM(((sent[0].shape[1] - TAIL) // copies, kept[0].shape[2]), F32)] * len(sent)
    done = pl.pallas_call(
        functools.partial(again_kernel, copies, len(sent)),
        out_shape=outs,
        in_specs=[VMEM] * (2 * len(sent)),
        out_specs=[VMEM] * len(sent),
        compiler_params=pltpu.CompilerParams(vmem_limit_bytes=16 * 2**20),
    )(*[stay(array) for array in (*sent, *kept)])
    return list(done)


def combine_kernel(feat, copies, levels_ref, own_ref, own_image_in_ref, near_ref, kept_near_ref, *refs):
    images, firsts, refs = refs[:PIECES], refs[PIECES : 2 * PIECES], refs[2 * PIECES :]
    late = LATE
    agains, kept, outs = refs[: PIECES - late], refs[PIECES - late : PIECES], refs[PIECES:]
    partial_ref, solution_ref, residual_ref, own_dir_ref, own_image_ref, norm_ref = outs
    slots, probes = images[0].shape[2], own_image_in_ref.shape[0]
    agains = [again_ref[...] for again_ref in agains]
    for image_ref, kept_ref in zip(images[PIECES - late :], kept):
        agains.append(sent_product(image_ref, kept_ref, copies))
    step_size, ratio, norm_next, scales = step_sums(images, copies, probes)
    product = jnp.zeros((probes, copies * slots), F32)
    for first_ref, again, scale in zip(firsts, agains, scales):
        product = product + ((1.0 - scale + ratio) * first_ref[...] + scale * again)

    first = own_ref[0, 2 * feat : 2 * feat + probes, :].astype(F32)
    right = first + own_ref[0, 2 * feat + probes :, :].astype(F32)
    residual = right - step_size * own_image_in_ref[...]
    directions = [(residual + ratio * first).astype(BF16).astype(F32)]
    solution_ref[...] = step_size * first
    residual_ref[...] = residual
    own_dir_ref[...] = directions[0]
    for b in range(copies):
        first = near_ref[b, 2 * feat :, :].astype(F32)
        sent = images[0][0, b * probes : (b + 1) * probes, :].astype(F32)
        directions.append((1.0 - scales[0] + ratio) * first + scales[0] * sent)
    exact, formed = directions[:2]
    own = jnp.dot((exact - formed).astype(BF16), kept_near_ref[0, :slots, :slots], preferred_element_type=F32)
    curve = jnp.zeros((probes, slots), F32)
    for b, direction in enumerate([exact] + directions[2:]):
        image = product[:, b * slots : (b + 1) * slots] + levels_ref[1:2, :] * direction
        if b == 0:
            image = image + own
            own_image_ref[...] = image
        curve = curve + direction * image
    lane = lax.broadcasted_iota(jnp.int32, (probes, 128), 1)
    flat = jnp.where(lane == 0, jnp.sum(curve, axis=1, keepdims=True), 0.0)
    partial_ref[...] = turned(flat, 128)[:8]
    norm_ref[...] = jnp.broadcast_to(norm_next, norm_ref.shape)


def combine(levels, own, own_image, near, images, products, agains, kept, copies, feat):
    probes, slots = own_image.shape
    one, small = pltpu.VMEM((probes, slots), F32), pltpu.VMEM((probes, 128), F32)
    arrays = [levels, own, own_image, near, kept[0], *images, *products, *agains, *kept[len(agains) :]]
    return pl.pallas_call(
        functools.partial(combine_kernel, feat, copies),
        out_shape=[pltpu.VMEM((8, 128), F32), one, one, one, one, small],
        in_specs=[VMEM] * len(arrays),
        out_specs=[VMEM] * 6,
        compiler_params=pltpu.CompilerParams(vmem_limit_bytes=16 * 2**20),
    )(*[stay(array) for array in arrays])


def second(levels, own, own_image, points, images, kept, copies, feat, group):
    keep = kept is not None
    slots, probes = own_image.shape[1], own_image.shape[0]
    one, small = pltpu.VMEM((probes, slots), F32), pltpu.VMEM((probes, 128), F32)
    scratch = [
        pltpu.VMEM((probes, copies * slots), F32),
        pltpu.VMEM((PIECES * images[0].shape[0], probes, 128), F32),
    ]
    arrays = [levels, own, own_image, *points, *images, *(kept or ())]
    if keep:
        arrays = [stay(array) for array in arrays]
    else:
        scratch.append(pltpu.VMEM((feature_rows(feat), copies * slots), BF16))
    return pl.pallas_call(
        functools.partial(second_kernel, feat, group, keep, copies),
        out_shape=[pltpu.VMEM((8, 128), F32), one, one, one, one, small],
        in_specs=[VMEM] * len(arrays),
        out_specs=[VMEM] * 6,
        scratch_shapes=scratch,
        compiler_params=pltpu.CompilerParams(vmem_limit_bytes=(16 if keep else 48) * 2**20),
    )(*arrays)


def finish_kernel(curve_ref, norm_ref, solution_ref, residual_ref, direction_ref, image_ref, out_ref, left_ref):
    probes = norm_ref.shape[0]
    curve = turned(curve_ref[...], 128)[:probes, :1]
    step_size = norm_ref[:, :1] / curve
    out_ref[...] = solution_ref[...] + step_size * direction_ref[...]
    left_ref[...] = residual_ref[...] - step_size * image_ref[...]


def gather(held, bits, count):
    for at in range(0, len(bits), 2):
        pair = bits[at : at + 2]
        flips = pair if len(pair) == 1 else [pair[0], sum(pair), pair[1]]
        held = jnp.concatenate([held] + [swap(held, flip, count) for flip in flips], axis=0)
    return held


def total(held, bits, count):
    for at in range(0, len(bits), 2):
        pair = bits[at : at + 2]
        flips = pair if len(pair) == 1 else [pair[0], pair[1], sum(pair)]
        held = sum([swap(held, flip, count) for flip in reversed(flips)], held)
    return held


def body(count, points, inv_lengths, signal_level, noise_level, right_sides, block_counts):
    slots, feat = points.shape
    probes = right_sides.shape[1]
    copies = COPIES
    while copies > 1 and (copies * PIECES > count or copies * count * slots * slots * 2 > KEEP_BYTES):
        copies //= 4
    group = math.gcd(count // PIECES, 8)
    keep = copies == group == count // PIECES and copies * count * slots * slots * 2 <= KEEP_BYTES
    bits = [1 << k for k in reversed(range(count.bit_length() - 1))]
    later = bits[copies.bit_length() - 1 :]
    one, two, core = bits[-3:]
    own = prepare(points, inv_lengths, right_sides, block_counts)
    own, signal_level, noise_level = lax.optimization_barrier((own, signal_level, noise_level))
    levels = jnp.stack([jnp.log(signal_level[0]) * LOG2E, noise_level[0]])
    levels = jnp.broadcast_to(levels[:, None], (2, slots))
    first = functools.partial(apply_first, feat=feat, group=group, keep=keep)

    held = gather(own, bits[:-3], count)
    held, levels = lax.optimization_barrier((held, levels))
    near = held[:copies]
    held = held[:, : 2 * feat + probes]
    beside = swap(held, core, count)
    up = swap_apart(held, one, two, core, count)
    kept_h, products, near_features = first(near, [held], levels, None, [])
    held_again, products[-1] = lax.optimization_barrier((held, products[-1]))
    over = swap_apart(held_again, two, one, core, count)
    kept_0, products, _ = first(near, [beside], levels, near_features, products)
    kept_0 = [*kept_h, *kept_0]
    up, products[-1] = lax.optimization_barrier((up, products[-1]))
    corner, up_beside = swap_apart(up, two, one, core, count), swap(up, core, count)
    kept_1, products, _ = first(near, [up], levels, near_features, products)
    over, products[-1] = lax.optimization_barrier((over, products[-1]))
    over_beside = swap(over, core, count)
    kept_2, products, _ = first(near, [up_beside, over], levels, near_features, products)
    corner, products[-1] = lax.optimization_barrier((corner, products[-1]))
    corner_beside = swap(corner, core, count)
    kept_3, products, _ = first(near, [over_beside, corner], levels, near_features, products)
    kept_4, products, (message, own_image) = first(near, [corner_beside], levels, near_features, products, last=True)
    pieces = [held, beside, up, up_beside, over, over_beside, corner, corner_beside]
    kept = [*kept_0, *kept_1, *kept_2, *kept_3, *kept_4]

    held = gather(message, later[:-3], count)
    beside, corner = swap(held, core, count), swap(held, one | two, count)
    up, over = swap_apart(held, one, two, core, count), swap_apart(held, two, one, core, count)
    if keep:
        again_0 = apply_again([held], kept[:1], copies)
        corner, again_0[0] = lax.optimization_barrier((corner, again_0[0]))
    corner_beside = swap(corner, core, count)
    if keep:
        again_1 = apply_again([beside, corner], [kept[1], kept[6]], copies)
        over, up, again_1[0] = lax.optimization_barrier((over, up, again_1[0]))
    up_beside, over_beside = (swap(array, core, count) for array in (up, over))
    if keep:
        again_2 = apply_again([corner_beside, up, over], [kept[7], kept[2], kept[4]], copies)
        images = [held, beside, corner, corner_beside, up, over, up_beside, over_beside]
        order = [0, 1, 6, 7, 2, 4, 3, 5]
        kept, products = ([each[at] for at in order] for each in (kept, products))
        agains = [*again_0, *again_1, *again_2]
        done = combine(levels, own, own_image, pieces[0], images, products, agains, kept, copies, feat)
    else:
        images = [held, beside, up, up_beside, over, over_beside, corner, corner_beside]
        done = second(levels, own, own_image, pieces, images, None, copies, feat, group)
    partial, solution, residual, direction, second_image, norm = done
    partial = partial + swap(partial, core, count)
    apart = swap_apart(partial, one, one | two, core, count)
    partial = partial + swap(partial, two, count) + (apart + swap(apart, core, count))
    partial = total(partial, later[:-3], count)
    done = jax.ShapeDtypeStruct((probes, slots), F32)
    solution, residual = pl.pallas_call(
        finish_kernel,
        out_shape=[done, done],
        in_specs=[VMEM] * 6,
        out_specs=[VMEM] * 2,
    )(*[stay(array) for array in (partial, norm, solution, residual, direction, second_image)])
    return solution.T, residual.T


def solution(mesh):
    count = math.prod(mesh.shape[axis] for axis in AXES)
    rows = P(AXES, None)
    return jax.shard_map(
        functools.partial(body, count),
        mesh=mesh,
        in_specs=(rows, P(), P(), P(), rows, P(AXES)),
        out_specs=(rows, rows),
        check_vma=False,
    )
```
